32 devices in a mesh: dp: 8 (over y, x, core), mp: 4 (over z).
Axes of the slice: x: 2, y: 2, z: 4, core: 2. Of those that a mesh axis runs over, the one named last changes fastest.
Arguments:
- text_embeds: bfloat16 [4, 16, 40, 768], P(None, 'dp'), may hold values from -6 to 6
- text_lengths: int32 [4, 16], P(None, 'dp'), may hold values from 10 to 40
- image_embeds: bfloat16 [4, 16, 145, 768], P(None, 'dp'), may hold values from -6 to 6
- image_mask: int32 [4, 16, 145], P(None, 'dp'), may hold values from 0 to 1, as said below
- image_ids: int32 [4, 16], replicated, may hold values from 0 to 7
- out_cot: bfloat16 [4, 16, 40, 768], P(None, 'dp', 'mp'), may hold values from -6 to 6
- text_qkv: bfloat16 [3, 768, 768], P(None, 'dp', 'mp'), may hold values from -0.21875 to 0.21875
- text_out: bfloat16 [768, 768], P('mp', 'dp'), may hold values from -0.5 to 0.5
- text_up: bfloat16 [768, 3072], P('dp', 'mp'), may hold values from -0.21875 to 0.21875
- text_down: bfloat16 [3072, 768], P('mp', 'dp'), may hold values from -0.109375 to 0.109375
- merge_qkv: bfloat16 [6, 768, 768], P(None, 'dp', 'mp'), may hold values from -0.21875 to 0.21875
- merge_out: bfloat16 [2, 768, 768], P(None, 'mp', 'dp'), may hold values from -0.625 to 0.625
- merge_up: bfloat16 [768, 3072], P('dp', 'mp'), may hold values from -0.21875 to 0.21875
- merge_down: bfloat16 [3072, 768], P('mp', 'dp'), may hold values from -0.109375 to 0.109375
- projections: bfloat16 [2, 768, 256], P(None, 'dp'), may hold values from -0.21875 to 0.21875
- norm_gains: float32 [5, 768], replicated, may hold values from 0.5 to 1.5
- offsets: float32 [10, 768], replicated, may hold values from -1.2 to 1.2
- head_biases: float32 [6, 768], P(None, 'mp'), may hold values from -1.2 to 1.2
- up_biases: float32 [2, 3072], P(None, 'mp'), may hold values from -1.2 to 1.2
Outputs:
- merged: float32 [4, 16, 40, 768], P(None, 'dp', 'mp')
- pair_loss: float32 [4, 16], P(None, 'dp')
- text_grad: float32 [4, 16, 40, 768], P(None, 'dp', 'mp')
- image_grad: float32 [4, 16, 145, 768], P(None, 'dp', None, 'mp')
- text_qkv_grad: float32 [3, 768, 768], P(None, 'dp', 'mp')
- text_out_grad: float32 [768, 768], P('mp', 'dp')
- text_up_grad: float32 [768, 3072], P('dp', 'mp')
- text_down_grad: float32 [3072, 768], P('mp', 'dp')
- merge_qkv_grad: float32 [6, 768, 768], P(None, 'dp', 'mp')
- merge_out_grad: float32 [2, 768, 768], P(None, 'mp', 'dp')
- merge_up_grad: float32 [768, 3072], P('dp', 'mp')
- merge_down_grad: float32 [3072, 768], P('mp', 'dp')
- projections_grad: float32 [2, 768, 256], P(None, 'dp')
- norm_gains_grad: float32 [5, 768], replicated
- offsets_grad: float32 [10, 768], replicated
- head_biases_grad: float32 [6, 768], P(None, 'mp')
- up_biases_grad: float32 [2, 3072], P(None, 'mp')
The draws below stay inside these ranges and needn't reach their ends.
Inputs may be any that keep to these rules, and one draw needn't show every extreme that they name: `image_mask`: in each image the first 50 tokens are live and the rest are either all live or all padding; in each micro-batch exactly 8 images are fully live.
All inputs are finite; a program needn't handle non-finite values.
Results may differ from the reference program's by a relative error of at most 0.028.
Values may be sent and summed in bfloat16 or wider, within the bound.
A program may use at most 192 MiB of HBM per device.

```python
import math
import jax
import jax.numpy as jnp
from jax import lax

D = 768
HEADS = 12
FF = 3072
E = 256
HEAD_DIM = 64
TXT = 40
IMG = 145
IMG_SHORT = 50
MICRO = 4
PAIRS = 16


def draw_image_mask(key, part):

    def one_batch(batch_key):
        order = jax.random.permutation(batch_key, PAIRS)
        longer = order < PAIRS // 2
        places = lax.broadcasted_iota(jnp.int32, (PAIRS, IMG), 1)
        return jnp.where((places < IMG_SHORT) | longer[:, None], 1, 0).astype(jnp.int32)
    return jax.vmap(one_batch)(jax.random.split(key, MICRO))


def place_ends(drawn, own_key, least, top_value):
    index_at = [jax.random.randint(jax.random.fold_in(own_key, axis), (), 0, length) for axis, length in enumerate(drawn.shape)]
    main_axis = drawn.shape.index(max(drawn.shape))
    neighbour = index_at[:main_axis] + [(index_at[main_axis] + 1) % drawn.shape[main_axis]] + index_at[main_axis + 1:]
    return drawn.at[tuple(index_at)].set(least).at[tuple(neighbour)].set(top_value)


def shard_levels(key, shape, pieces, low, high):
    def one(position, shards_of):
        draws = jax.random.uniform(jax.random.fold_in(jax.random.fold_in(key, 6), position), (shards_of,), jnp.float32, low / len(pieces), high / len(pieces))
        return jnp.repeat(jnp.exp(draws), shape[position] // shards_of).reshape((-1,) + (1,) * (len(shape) - position - 1))

    level = one(*pieces[0])
    for cut in pieces[1:]:
        level = level * one(*cut)
    return level


def scatter_about(own_key, shape, width, reach, cuts=(), kind=jnp.bfloat16):
    factor_of = shard_levels(own_key, shape, cuts, -0.22, 0.18) if cuts else 1.0
    array = jax.random.normal(own_key, shape, jnp.float32) * width * factor_of
    return jnp.minimum(jnp.maximum(array, -reach), reach).astype(kind)


def setup_inputs(seed: int = 0) -> dict:
    seeds = jax.random.split(jax.random.key(seed), 20)
    text_embeds = scatter_about(seeds[0], (MICRO, PAIRS, TXT, D), 1.0, 6.0, ((1, 8),))
    text_lengths = place_ends(jax.random.randint(seeds[1], (MICRO, PAIRS), TXT // 4, TXT + 1), jax.random.fold_in(seeds[1], 1), TXT // 4, TXT).astype(jnp.int32)
    image_embeds = scatter_about(seeds[2], (MICRO, PAIRS, IMG, D), 1.0, 6.0, ((1, 8),))
    image_mask = draw_image_mask(jax.random.fold_in(seeds[19], 71), 0)
    image_ids = place_ends(jax.random.randint(seeds[4], (MICRO, PAIRS), 0, PAIRS // 2), jax.random.fold_in(seeds[4], 1), 0, (PAIRS // 2) - 1).astype(jnp.int32)
    out_cot = scatter_about(seeds[5], (MICRO, PAIRS, TXT, D), 1.0, 6.0, ((1, 8), (2, 4)))
    text_qkv = scatter_about(seeds[6], (3, D, D), D ** -0.5, 0.21875, ((1, 8), (2, 4)))
    text_out = scatter_about(seeds[7], (D, D), (D // 5) ** -0.5, 0.5, ((0, 4), (1, 8)))
    text_up = scatter_about(seeds[8], (D, FF), D ** -0.5, 0.21875, ((0, 8), (1, 4)))
    text_down = scatter_about(seeds[9], (FF, D), FF ** -0.5, 0.109375, ((0, 4), (1, 8)))
    merge_qkv = scatter_about(seeds[10], (6, D, D), D ** -0.5, 0.21875, ((1, 8), (2, 4)))
    merge_out = scatter_about(seeds[11], (2, D, D), (D // 8) ** -0.5, 0.625, ((1, 4), (2, 8)))
    merge_up = scatter_about(seeds[12], (D, FF), D ** -0.5, 0.21875, ((0, 8), (1, 4)))
    merge_down = scatter_about(seeds[13], (FF, D), FF ** -0.5, 0.109375, ((0, 4), (1, 8)))
    projections = scatter_about(seeds[14], (2, D, E), D ** -0.5, 0.21875, ((1, 8),))
    norm_gains = jnp.clip(1.0 + 0.1 * jax.random.normal(seeds[15], (5, D), jnp.float32), 0.5, 1.5)
    offsets = scatter_about(seeds[16], (10, D), 0.2, 1.2, (), jnp.float32)
    head_biases = scatter_about(seeds[17], (6, D), 0.2, 1.2, ((1, 4),), jnp.float32)
    up_biases = scatter_about(seeds[18], (2, FF), 0.2, 1.2, ((1, 4),), jnp.float32)
    return {"text_embeds": text_embeds, "text_lengths": text_lengths, "image_embeds": image_embeds, "image_mask": image_mask, "image_ids": image_ids, "out_cot": out_cot, "text_qkv": text_qkv, "text_out": text_out, "text_up": text_up, "text_down": text_down, "merge_qkv": merge_qkv, "merge_out": merge_out, "merge_up": merge_up, "merge_down": merge_down, "projections": projections, "norm_gains": norm_gains, "offsets": offsets, "head_biases": head_biases, "up_biases": up_biases}


EPS = 1e-06
SCORE_SCALE = 0.05
EXACT_DOT_MODE = lax.Precision.HIGHEST
NEGATIVE = -1e+30

@jax.custom_vjp
def low(v):
    return lax.optimization_barrier(v.astype(jnp.bfloat16)).astype(jnp.float32)

@jax.custom_vjp
def low_back(v):
    return v

def low_keep(v):
    return (low(v), None)

def low_pass(kept, grad):
    return (grad,)

def back_keep(v):
    return (v, None)

def back_low(kept, grad):
    return (low(grad),)
low.defvjp(low_keep, low_pass)
low_back.defvjp(back_keep, back_low)

def layer_norm(before, gain, shift):
    centre = before - lax.optimization_barrier(jnp.mean(before, -1, keepdims=True))
    second = lax.optimization_barrier(jnp.mean(centre * centre, -1, keepdims=True))
    return centre * lax.rsqrt(second + EPS) * gain + shift

def unit_rows(raw):
    return raw * lax.rsqrt(lax.optimization_barrier(jnp.sum(raw * raw, -1, keepdims=True)) + EPS)

def project(source, weight):
    return jnp.einsum('pld,de->ple', source, weight, precision=EXACT_DOT_MODE)

def attend(query_in, key_in, weight_query, bias_query, weight_key, weight_value, bias_value, weight_out, bias_out, valid):
    pairs, query_len, _ = query_in.shape
    key_len = key_in.shape[1]
    queries = low(low_back(project(query_in, weight_query) + bias_query)).reshape(pairs, query_len, HEADS, HEAD_DIM)
    keys = low(low_back(project(key_in, weight_key))).reshape(pairs, key_len, HEADS, HEAD_DIM)
    values = low(low_back(project(key_in, weight_value) + bias_value)).reshape(pairs, key_len, HEADS, HEAD_DIM)
    scores = low_back(jnp.einsum('pqhd,pkhd->phqk', queries, keys, precision=EXACT_DOT_MODE) * (1.0 / math.sqrt(HEAD_DIM)))
    scores = jnp.where(valid[:, None, None, :], scores, NEGATIVE)
    probs = low(jax.nn.softmax(scores, axis=-1))
    mixed = jnp.einsum('phqk,pkhd->pqhd', probs, values, precision=EXACT_DOT_MODE).reshape(pairs, query_len, HEADS * HEAD_DIM)
    mixed = low(low_back(mixed))
    return low_back(project(mixed, weight_out) + bias_out)

def feed(source, weight_up, bias_up, weight_down, bias_down):
    pre = low_back(project(source, weight_up) + bias_up)
    active = low(jax.nn.gelu(pre, approximate=False))
    return low_back(project(active, weight_down) + bias_down)

def forward(params, text_in, image_in, text_valid, image_valid, ids):
    text_qkv, text_out, text_up, text_down, merge_qkv, merge_out, merge_up, merge_down, projections, gains, offsets, head_biases, up_biases = params
    branch = attend(text_in, text_in, text_qkv[0], head_biases[0], text_qkv[1], text_qkv[2], head_biases[1], text_out, offsets[0], text_valid)
    hidden1 = low(layer_norm(text_in + branch, gains[0], offsets[5]))
    branch = feed(hidden1, text_up, up_biases[0], text_down, offsets[1])
    hidden2 = low(layer_norm(hidden1 + branch, gains[1], offsets[6]))
    branch = attend(hidden2, hidden2, merge_qkv[0], head_biases[2], merge_qkv[1], merge_qkv[2], head_biases[3], merge_out[0], offsets[2], text_valid)
    hidden3 = low(layer_norm(hidden2 + branch, gains[2], offsets[7]))
    branch = attend(hidden3, image_in, merge_qkv[3], head_biases[4], merge_qkv[4], merge_qkv[5], head_biases[5], merge_out[1], offsets[3], image_valid)
    hidden4 = low(layer_norm(hidden3 + branch, gains[3], offsets[8]))
    branch = feed(hidden4, merge_up, up_biases[1], merge_down, offsets[4])
    merged = layer_norm(hidden4 + branch, gains[4], offsets[9])
    caption_normed_embedding = unit_rows(jnp.matmul(hidden2[:, 0], projections[0], precision=EXACT_DOT_MODE))
    picture_normed_embedding = unit_rows(jnp.matmul(image_in[:, 0], projections[1], precision=EXACT_DOT_MODE))
    cosine_score_matrix = jnp.matmul(caption_normed_embedding, picture_normed_embedding.T, precision=EXACT_DOT_MODE) / SCORE_SCALE
    same = (ids[:, None] == ids[None, :]).astype(cosine_score_matrix.dtype)
    paired_target_index = same / lax.optimization_barrier(jnp.sum(same, 1, keepdims=True))
    text_side = lax.optimization_barrier(jnp.sum(paired_target_index * jax.nn.log_softmax(cosine_score_matrix, axis=1), 1))
    image_side = lax.optimization_barrier(jnp.sum(paired_target_index * jax.nn.log_softmax(cosine_score_matrix.T, axis=1), 1))
    return (merged, -0.5 * (text_side + image_side))

def reference(text_embeds, text_lengths, image_embeds, image_mask, image_ids, out_cot, text_qkv, text_out, text_up, text_down, merge_qkv, merge_out, merge_up, merge_down, projections, norm_gains, offsets, head_biases, up_biases):
    params = tuple((weight.astype(jnp.float32) for weight in (text_qkv, text_out, text_up, text_down, merge_qkv, merge_out, merge_up, merge_down, projections, norm_gains, offsets, head_biases, up_biases)))

    def one_batch(totals, batch):
        embeds, lengths, images, mask, ids, cotangent = batch
        text_valid = lax.broadcasted_iota(jnp.int32, (PAIRS, TXT), 1) < lengths[:, None]
        image_valid = mask > 0

        def run(weights, text_in, image_in):
            return forward(weights, text_in, image_in, text_valid, image_valid, ids)
        (merged, loss), pull = jax.vjp(run, params, embeds, images)
        weight_grads, text_grad, image_grad = pull((cotangent, jnp.ones_like(loss)))
        totals = jax.tree.map(lambda left, right: left + right, totals, weight_grads)
        return (totals, (merged, loss, text_grad, image_grad))
    start = jax.tree.map(jnp.zeros_like, params)
    totals, (merged, loss, text_grad, image_grad) = lax.scan(one_batch, start, (text_embeds.astype(jnp.float32), text_lengths, image_embeds.astype(jnp.float32), image_mask, image_ids, out_cot.astype(jnp.float32)))
    return (merged, loss, text_grad, image_grad, totals[0], totals[1], totals[2], totals[3], totals[4], totals[5], totals[6], totals[7], totals[8], totals[9], totals[10], totals[11], totals[12])
```

```python
import math

import jax
import jax.numpy as jnp
from jax import lax
from jax.experimental import pallas as pl
from jax.experimental.pallas import tpu as pltpu
from jax.sharding import PartitionSpec as P

HEAD_DIM = 64


EPS = 1e-06
SCORE_SCALE = 0.05
EXACT_DOT_MODE = lax.Precision.HIGHEST
NEGATIVE = -1e30


def layer_norm(before, gain, shift):
    centre = before - jnp.mean(before, -1, keepdims=True)
    second = jnp.mean(centre * centre, -1, keepdims=True)
    return centre * lax.rsqrt(second + EPS) * gain + shift


def unit_rows(raw):
    return raw * lax.rsqrt(jnp.sum(raw * raw, -1, keepdims=True) + EPS)


def gelu_exact(pre):
    return jax.nn.gelu(pre, approximate=False)


def product(left, right):
    return jnp.dot(left, right, preferred_element_type=jnp.float32)


def row_contract(left, right):
    return lax.dot_general(
        left, right, (((0,), (0,)), ((), ())), preferred_element_type=jnp.float32
    )


def column_contract(left, right):
    return lax.dot_general(
        left, right, (((1,), (1,)), ((), ())), preferred_element_type=jnp.float32
    )


def rows_from(source, start, count):
    return lax.dynamic_slice_in_dim(source, start, count, 0)


def out_term(mixed, weight):

    def term(start, count):
        return product(rows_from(mixed, start, count), weight)

    return term


def back_term(grads, weight):

    def term(start, count):
        return column_contract(rows_from(grads, start, count), weight)

    return term


def joined_split(joined_grad, count):
    rows, columns = joined_grad.shape
    return jnp.transpose(joined_grad.reshape(rows, count, columns // count), (1, 0, 2))


def settle(hidden, term, bias, gain, shift):
    share_rows = hidden.shape[0] // lax.axis_size("mp")
    start = lax.axis_index("mp") * share_rows
    summed = lax.psum_scatter(
        term(jnp.int32(0), share_rows * lax.axis_size("mp")), "mp", scatter_dimension=0, tiled=True
    )
    before = rows_from(hidden, start, share_rows).astype(jnp.float32) + summed + bias
    return (before, layer_norm(before, gain, shift))


def spread(share):
    return lax.all_gather(share.astype(jnp.bfloat16), "mp", axis=0, tiled=True)


def unsettle(grad_share, before, gain, shift):
    _, pull = jax.vjp(layer_norm, before, gain, shift)
    grad_before, grad_gain, grad_shift = pull(grad_share)
    rounded = grad_before.astype(jnp.bfloat16)
    grad_bias = jnp.sum(rounded.astype(jnp.float32), 0)
    grad_full = lax.all_gather(rounded, "mp", axis=0, tiled=True)
    return (grad_before, grad_full, grad_gain, grad_shift, grad_bias)


def gather_back(grad_before, term):
    return grad_before + lax.psum_scatter(
        term(jnp.int32(0), grad_before.shape[0] * lax.axis_size("mp")),
        "mp",
        scatter_dimension=0,
        tiled=True,
    )


def attention_forward(queries, keys, values, valid, scale):
    scores = (
        jnp.einsum("qphd,pkhd->phqk", queries, keys, preferred_element_type=jnp.float32) * scale
    )
    scores = jnp.where(valid[:, None, None, :], scores, NEGATIVE)
    highest = jnp.max(scores, -1, keepdims=True)
    raised = jnp.exp(scores - highest)
    totals = jnp.sum(raised, -1, keepdims=True)
    probs = (raised / totals).astype(jnp.bfloat16)
    mixed = jnp.einsum("phqk,pkhd->qphd", probs, values, preferred_element_type=jnp.float32)
    return (mixed.astype(jnp.bfloat16), highest + jnp.log(totals))


def attention_backward(queries, keys, values, valid, log_total, grad_mixed, scale):
    scores = (
        jnp.einsum("qphd,pkhd->phqk", queries, keys, preferred_element_type=jnp.float32) * scale
    )
    scores = jnp.where(valid[:, None, None, :], scores, NEGATIVE)
    probs = jnp.exp(scores - log_total)
    grad_values = jnp.einsum(
        "phqk,qphd->pkhd",
        probs.astype(jnp.bfloat16),
        grad_mixed,
        preferred_element_type=jnp.float32,
    )
    grad_probs = jnp.einsum(
        "qphd,pkhd->phqk", grad_mixed, values, preferred_element_type=jnp.float32
    )
    grad_scores = probs * (grad_probs - jnp.sum(grad_probs * probs, -1, keepdims=True))
    rounded = grad_scores.astype(jnp.bfloat16)
    grad_queries = (
        jnp.einsum("phqk,pkhd->qphd", rounded, keys, preferred_element_type=jnp.float32) * scale
    )
    grad_keys = (
        jnp.einsum("phqk,qphd->pkhd", rounded, queries, preferred_element_type=jnp.float32) * scale
    )
    return (
        grad_queries.astype(jnp.bfloat16),
        grad_keys.astype(jnp.bfloat16),
        grad_values.astype(jnp.bfloat16),
    )


def self_forward(hidden, joined, bias_query, bias_value, valid, pairs, scale):
    local = joined.shape[1] // 3
    heads = local // HEAD_DIM
    made = product(hidden, joined)
    queries = (
        (made[:, :local] + bias_query).astype(jnp.bfloat16).reshape(-1, pairs, heads, HEAD_DIM)
    )
    keys = jnp.swapaxes(
        made[:, local : 2 * local].astype(jnp.bfloat16).reshape(-1, pairs, heads, HEAD_DIM), 0, 1
    )
    values = jnp.swapaxes(
        (made[:, 2 * local :] + bias_value)
        .astype(jnp.bfloat16)
        .reshape(-1, pairs, heads, HEAD_DIM),
        0,
        1,
    )
    mixed, log_total = attention_forward(queries, keys, values, valid, scale)
    return ((queries, keys, values, log_total), mixed.reshape(-1, local))


def self_backward(kept, hidden, mixed, grad_full, joined, weight_out, valid, scale):
    queries, keys, values, log_total = kept
    rows = hidden.shape[0]
    local = mixed.shape[1]
    grad_mixed = column_contract(grad_full, weight_out).astype(jnp.bfloat16).reshape(queries.shape)
    grad_queries, grad_keys, grad_values = attention_backward(
        queries, keys, values, valid, log_total, grad_mixed, scale
    )
    grads = jnp.concatenate(
        [
            grad_queries.reshape(rows, local),
            jnp.swapaxes(grad_keys, 0, 1).reshape(rows, local),
            jnp.swapaxes(grad_values, 0, 1).reshape(rows, local),
        ],
        1,
    )
    joined_grad = row_contract(hidden, grads)
    out_grad = row_contract(mixed, grad_full)
    bias_query = jnp.sum(grads[:, :local].astype(jnp.float32), 0)
    bias_value = jnp.sum(grads[:, 2 * local :].astype(jnp.float32), 0)
    return (back_term(grads, joined), joined_grad, out_grad, bias_query, bias_value)


def cross_forward(
    hidden, image_rows, weight_query, joined, bias_query, bias_value, valid, pairs, scale
):
    local = weight_query.shape[1]
    heads = local // HEAD_DIM
    queries = (
        (product(hidden, weight_query) + bias_query)
        .astype(jnp.bfloat16)
        .reshape(-1, pairs, heads, HEAD_DIM)
    )
    made = product(image_rows, joined)
    keys = made[:, :local].astype(jnp.bfloat16).reshape(pairs, -1, heads, HEAD_DIM)
    values = (made[:, local:] + bias_value).astype(jnp.bfloat16).reshape(pairs, -1, heads, HEAD_DIM)
    mixed, log_total = attention_forward(queries, keys, values, valid, scale)
    return ((queries, keys, values, log_total), mixed.reshape(-1, local))


def cross_backward(
    kept, hidden, image_rows, mixed, grad_full, weight_query, joined, weight_out, valid, scale
):
    queries, keys, values, log_total = kept
    rows = hidden.shape[0]
    local = mixed.shape[1]
    grad_mixed = column_contract(grad_full, weight_out).astype(jnp.bfloat16).reshape(queries.shape)
    grad_queries, grad_keys, grad_values = attention_backward(
        queries, keys, values, valid, log_total, grad_mixed, scale
    )
    query_grads = grad_queries.reshape(rows, local)
    image_grads = jnp.concatenate([grad_keys.reshape(-1, local), grad_values.reshape(-1, local)], 1)
    query_weight_grad = row_contract(hidden, query_grads)
    joined_grad = row_contract(image_rows, image_grads)
    out_grad = row_contract(mixed, grad_full)
    image_part = column_contract(image_grads, joined)
    bias_query = jnp.sum(query_grads.astype(jnp.float32), 0)
    bias_value = jnp.sum(image_grads[:, local:].astype(jnp.float32), 0)
    return (
        back_term(query_grads, weight_query),
        image_part,
        query_weight_grad,
        joined_grad,
        out_grad,
        bias_query,
        bias_value,
    )


def ffn_forward(hidden, weight_up, bias_up):
    pre = product(hidden, weight_up) + bias_up
    return (pre, gelu_exact(pre).astype(jnp.bfloat16))


def ffn_backward(hidden, pre, active, grad_full, weight_up, weight_down):
    grad_active = column_contract(grad_full, weight_down)
    _, pull = jax.vjp(gelu_exact, pre)
    grad_pre = pull(grad_active)[0].astype(jnp.bfloat16)
    down_grad = row_contract(active, grad_full)
    up_grad = row_contract(hidden, grad_pre)
    bias_grad = jnp.sum(grad_pre.astype(jnp.float32), 0)
    return (back_term(grad_pre, weight_up), up_grad, down_grad, bias_grad)


def contrast(text_cls, image_cls, text_proj, image_proj, own_ids, all_ids):
    caption_normed_embedding, text_pull = jax.vjp(unit_rows, product(text_cls, text_proj))
    picture_normed_embedding, image_pull = jax.vjp(unit_rows, product(image_cls, image_proj))
    gathered_text_features, gathered_image_features = (
        lax.all_gather(caption_normed_embedding, "dp", axis=0, tiled=True),
        lax.all_gather(picture_normed_embedding, "dp", axis=0, tiled=True),
    )
    same = (own_ids[:, None] == all_ids[None, :]).astype(jnp.float32)
    paired_target_index = same / jnp.sum(same, 1, keepdims=True)
    caption_row_logsoftmax = jax.nn.log_softmax(
        jnp.dot(caption_normed_embedding, gathered_image_features.T, precision=EXACT_DOT_MODE)
        / SCORE_SCALE,
        axis=1,
    )
    picture_row_logsoftmax = jax.nn.log_softmax(
        jnp.dot(picture_normed_embedding, gathered_text_features.T, precision=EXACT_DOT_MODE)
        / SCORE_SCALE,
        axis=1,
    )
    loss = -0.5 * (
        jnp.sum(paired_target_index * caption_row_logsoftmax, 1)
        + jnp.sum(paired_target_index * picture_row_logsoftmax, 1)
    )
    caption_score_excess = (
        0.5 * (jnp.exp(caption_row_logsoftmax) - paired_target_index) / SCORE_SCALE
    )
    picture_score_excess = (
        0.5 * (jnp.exp(picture_row_logsoftmax) - paired_target_index) / SCORE_SCALE
    )
    grad_text_own = jnp.dot(caption_score_excess, gathered_image_features, precision=EXACT_DOT_MODE)
    grad_image_own = jnp.dot(picture_score_excess, gathered_text_features, precision=EXACT_DOT_MODE)
    grad_all_image = jnp.dot(
        caption_score_excess.T, caption_normed_embedding, precision=EXACT_DOT_MODE
    )
    grad_all_text = jnp.dot(
        picture_score_excess.T, picture_normed_embedding, precision=EXACT_DOT_MODE
    )
    back_text, back_image = (
        lax.psum_scatter(grad_all_text, "dp", scatter_dimension=0, tiled=True),
        lax.psum_scatter(grad_all_image, "dp", scatter_dimension=0, tiled=True),
    )
    text_feature = grad_text_own + back_text
    image_feature = grad_image_own + back_image
    text_raw_grad = text_pull(text_feature)[0]
    image_raw_grad = image_pull(image_feature)[0]
    text_proj_grad = jnp.dot(
        text_cls.astype(jnp.float32).T, text_raw_grad, precision=EXACT_DOT_MODE
    )
    image_proj_grad = jnp.dot(
        image_cls.astype(jnp.float32).T, image_raw_grad, precision=EXACT_DOT_MODE
    )
    text_cls_grad = jnp.dot(
        text_raw_grad, text_proj.astype(jnp.float32).T, precision=EXACT_DOT_MODE
    )
    image_cls_grad = jnp.dot(
        image_raw_grad, image_proj.astype(jnp.float32).T, precision=EXACT_DOT_MODE
    )
    return (loss, text_cls_grad, image_cls_grad, text_proj_grad, image_proj_grad)


def shards(
    text_embeds,
    text_lengths,
    image_embeds,
    image_mask,
    image_ids,
    out_cot,
    text_qkv,
    text_out,
    text_up,
    text_down,
    merge_qkv,
    merge_out,
    merge_up,
    merge_down,
    projections,
    norm_gains,
    offsets,
    head_biases,
    up_biases,
):
    (
        text_qkv_all,
        text_out_all,
        text_up_all,
        text_down_all,
        merge_qkv_all,
        merge_out_all,
        merge_up_all,
        merge_down_all,
        projections_all,
    ) = (
        lax.all_gather(text_qkv, "dp", axis=1, tiled=True),
        lax.all_gather(text_out, "dp", axis=1, tiled=True),
        lax.all_gather(text_up, "dp", axis=0, tiled=True),
        lax.all_gather(text_down, "dp", axis=1, tiled=True),
        lax.all_gather(merge_qkv, "dp", axis=1, tiled=True),
        lax.all_gather(merge_out, "dp", axis=2, tiled=True),
        lax.all_gather(merge_up, "dp", axis=0, tiled=True),
        lax.all_gather(merge_down, "dp", axis=1, tiled=True),
        lax.all_gather(projections, "dp", axis=1, tiled=True),
    )
    text_joined = jnp.concatenate([text_qkv_all[0], text_qkv_all[1], text_qkv_all[2]], 1)
    self_joined = jnp.concatenate([merge_qkv_all[0], merge_qkv_all[1], merge_qkv_all[2]], 1)
    cross_joined = jnp.concatenate([merge_qkv_all[4], merge_qkv_all[5]], 1)
    micro, pairs, tokens, width = text_embeds.shape
    images = image_embeds.shape[2]
    local = text_qkv_all.shape[2]
    hidden_local = text_up_all.shape[1]
    model_parts = lax.axis_size("mp")
    model_index = lax.axis_index("mp")
    data_index = lax.axis_index("dp")
    scale = 1.0 / math.sqrt(HEAD_DIM)
    first_share = (model_index == 0).astype(jnp.float32)
    text_joined_grad = jnp.zeros((width, 3 * local), jnp.float32)
    text_out_grad = jnp.zeros((local, width), jnp.float32)
    text_up_grad = jnp.zeros((width, hidden_local), jnp.float32)
    text_down_grad = jnp.zeros((hidden_local, width), jnp.float32)
    self_joined_grad = jnp.zeros((width, 3 * local), jnp.float32)
    cross_query_grad = jnp.zeros((width, local), jnp.float32)
    cross_joined_grad = jnp.zeros((width, 2 * local), jnp.float32)
    self_out_grad = jnp.zeros((local, width), jnp.float32)
    cross_out_grad = jnp.zeros((local, width), jnp.float32)
    merge_up_grad = jnp.zeros((width, hidden_local), jnp.float32)
    merge_down_grad = jnp.zeros((hidden_local, width), jnp.float32)
    text_proj_total = jnp.zeros(projections_all.shape[1:], jnp.float32)
    image_proj_total = jnp.zeros(projections_all.shape[1:], jnp.float32)
    gain_list = [jnp.zeros((width,), jnp.float32) for place in range(5)]
    offset_list = [jnp.zeros((width,), jnp.float32) for place in range(10)]
    head_list = [jnp.zeros((local,), jnp.float32) for place in range(6)]
    up_list = [jnp.zeros((hidden_local,), jnp.float32) for place in range(2)]
    merged_list, loss_list, text_list, image_list = ([], [], [], [])
    for step in range(micro):
        hidden0 = jnp.swapaxes(text_embeds[step], 0, 1).reshape(tokens * pairs, width)
        image_rows = image_embeds[step].reshape(pairs * images, width)
        text_valid = (
            lax.broadcasted_iota(jnp.int32, (pairs, tokens), 1) < text_lengths[step][:, None]
        )
        image_valid = image_mask[step] > 0
        kept0, mixed0 = self_forward(
            hidden0, text_joined, head_biases[0], head_biases[1], text_valid, pairs, scale
        )
        before0, share1 = settle(
            hidden0, out_term(mixed0, text_out_all), offsets[0], norm_gains[0], offsets[5]
        )
        hidden1 = spread(share1)
        pre1, active1 = ffn_forward(hidden1, text_up_all, up_biases[0])
        before1, share2 = settle(
            hidden1, out_term(active1, text_down_all), offsets[1], norm_gains[1], offsets[6]
        )
        hidden2 = spread(share2)
        all_ids = image_ids[step]
        own_start = data_index * pairs
        own_ids = lax.dynamic_slice_in_dim(all_ids, own_start, pairs, 0)
        loss, text_cls_grad, image_cls_grad, text_proj_grad, image_proj_grad = contrast(
            hidden2[:pairs],
            image_embeds[step][:, 0],
            projections_all[0],
            projections_all[1],
            own_ids,
            all_ids,
        )
        loss_list.append(loss)
        text_proj_total = text_proj_total + text_proj_grad
        image_proj_total = image_proj_total + image_proj_grad
        kept2, mixed2 = self_forward(
            hidden2, self_joined, head_biases[2], head_biases[3], text_valid, pairs, scale
        )
        before2, share3 = settle(
            hidden2, out_term(mixed2, merge_out_all[0]), offsets[2], norm_gains[2], offsets[7]
        )
        hidden3 = spread(share3)
        kept3, mixed3 = cross_forward(
            hidden3,
            image_rows,
            merge_qkv_all[3],
            cross_joined,
            head_biases[4],
            head_biases[5],
            image_valid,
            pairs,
            scale,
        )
        before3, share4 = settle(
            hidden3, out_term(mixed3, merge_out_all[1]), offsets[3], norm_gains[3], offsets[8]
        )
        hidden4 = spread(share4)
        pre4, active4 = ffn_forward(hidden4, merge_up_all, up_biases[1])
        before4, out_share = settle(
            hidden4, out_term(active4, merge_down_all), offsets[4], norm_gains[4], offsets[9]
        )
        share_tokens = out_share.shape[0] // pairs
        merged_list.append(jnp.swapaxes(out_share.reshape(share_tokens, pairs, width), 0, 1))
        cot_rows = jnp.swapaxes(out_cot[step], 0, 1).reshape(-1, width).astype(jnp.float32)
        grad_before, grad_full, grad_gain, grad_shift, grad_bias = unsettle(
            cot_rows, before4, norm_gains[4], offsets[9]
        )
        gain_list[4] = gain_list[4] + grad_gain
        offset_list[9] = offset_list[9] + grad_shift
        offset_list[4] = offset_list[4] + grad_bias
        term, up_grad, down_grad, bias_up = ffn_backward(
            hidden4, pre4, active4, grad_full, merge_up_all, merge_down_all
        )
        merge_up_grad = merge_up_grad + up_grad
        merge_down_grad = merge_down_grad + down_grad
        up_list[1] = up_list[1] + bias_up
        grad_hidden4 = gather_back(grad_before, term)
        grad_before, grad_full, grad_gain, grad_shift, grad_bias = unsettle(
            grad_hidden4, before3, norm_gains[3], offsets[8]
        )
        gain_list[3] = gain_list[3] + grad_gain
        offset_list[8] = offset_list[8] + grad_shift
        offset_list[3] = offset_list[3] + grad_bias
        term, image_part, query_grad, joined_grad, out_grad, bias_query, bias_value = (
            cross_backward(
                kept3,
                hidden3,
                image_rows,
                mixed3,
                grad_full,
                merge_qkv_all[3],
                cross_joined,
                merge_out_all[1],
                image_valid,
                scale,
            )
        )
        cross_query_grad = cross_query_grad + query_grad
        cross_joined_grad = cross_joined_grad + joined_grad
        cross_out_grad = cross_out_grad + out_grad
        head_list[4] = head_list[4] + bias_query
        head_list[5] = head_list[5] + bias_value
        image_share = lax.psum_scatter(image_part, "mp", scatter_dimension=1, tiled=True).reshape(
            pairs, images, local
        )
        cls_part = lax.dynamic_slice_in_dim(image_cls_grad, model_index * local, local, 1)
        image_list.append(
            jnp.concatenate([image_share[:, :1] + cls_part[:, None], image_share[:, 1:]], 1)
        )
        grad_hidden3 = gather_back(grad_before, term)
        grad_before, grad_full, grad_gain, grad_shift, grad_bias = unsettle(
            grad_hidden3, before2, norm_gains[2], offsets[7]
        )
        gain_list[2] = gain_list[2] + grad_gain
        offset_list[7] = offset_list[7] + grad_shift
        offset_list[2] = offset_list[2] + grad_bias
        term, joined_grad, out_grad, bias_query, bias_value = self_backward(
            kept2, hidden2, mixed2, grad_full, self_joined, merge_out_all[0], text_valid, scale
        )
        self_joined_grad = self_joined_grad + joined_grad
        self_out_grad = self_out_grad + out_grad
        head_list[2] = head_list[2] + bias_query
        head_list[3] = head_list[3] + bias_value
        grad_hidden2 = gather_back(grad_before, term)
        extra = jnp.concatenate(
            [text_cls_grad, jnp.zeros((grad_hidden2.shape[0] - pairs, width), jnp.float32)], 0
        )
        grad_hidden2 = grad_hidden2 + extra * first_share
        grad_before, grad_full, grad_gain, grad_shift, grad_bias = unsettle(
            grad_hidden2, before1, norm_gains[1], offsets[6]
        )
        gain_list[1] = gain_list[1] + grad_gain
        offset_list[6] = offset_list[6] + grad_shift
        offset_list[1] = offset_list[1] + grad_bias
        term, up_grad, down_grad, bias_up = ffn_backward(
            hidden1, pre1, active1, grad_full, text_up_all, text_down_all
        )
        text_up_grad = text_up_grad + up_grad
        text_down_grad = text_down_grad + down_grad
        up_list[0] = up_list[0] + bias_up
        grad_hidden1 = gather_back(grad_before, term)
        grad_before, grad_full, grad_gain, grad_shift, grad_bias = unsettle(
            grad_hidden1, before0, norm_gains[0], offsets[5]
        )
        gain_list[0] = gain_list[0] + grad_gain
        offset_list[5] = offset_list[5] + grad_shift
        offset_list[0] = offset_list[0] + grad_bias
        term, joined_grad, out_grad, bias_query, bias_value = self_backward(
            kept0, hidden0, mixed0, grad_full, text_joined, text_out_all, text_valid, scale
        )
        text_joined_grad = text_joined_grad + joined_grad
        text_out_grad = text_out_grad + out_grad
        head_list[0] = head_list[0] + bias_query
        head_list[1] = head_list[1] + bias_value
        grad_hidden0 = gather_back(grad_before, term)
        text_list.append(jnp.swapaxes(grad_hidden0.reshape(share_tokens, pairs, width), 0, 1))
    head_full = lax.dynamic_update_slice_in_dim(
        jnp.zeros((6, width), jnp.float32), jnp.stack(head_list), model_index * local, 1
    )
    up_full = lax.dynamic_update_slice_in_dim(
        jnp.zeros((2, hidden_local * model_parts), jnp.float32),
        jnp.stack(up_list),
        model_index * hidden_local,
        1,
    )
    gains_sum, offsets_sum, heads_sum, ups_sum = lax.psum(
        (jnp.stack(gain_list), jnp.stack(offset_list), head_full, up_full), ("dp", "mp")
    )
    head_out = lax.dynamic_slice_in_dim(heads_sum, model_index * local, local, 1)
    up_out = lax.dynamic_slice_in_dim(ups_sum, model_index * hidden_local, hidden_local, 1)
    text_qkv_grad = joined_split(text_joined_grad, 3)
    projections_grad = jnp.stack([text_proj_total, image_proj_total])
    merging_qkv_grad = jnp.concatenate(
        [
            joined_split(self_joined_grad, 3),
            cross_query_grad[None],
            joined_split(cross_joined_grad, 2),
        ],
        0,
    )
    merging_out_grad = jnp.stack([self_out_grad, cross_out_grad])
    (
        text_qkv_done,
        text_out_done,
        text_up_done,
        text_down_done,
        projections_done,
        merge_qkv_done,
        merge_out_done,
        merge_up_done,
        merge_down_done,
    ) = (
        lax.psum_scatter(text_qkv_grad, "dp", scatter_dimension=1, tiled=True),
        lax.psum_scatter(text_out_grad, "dp", scatter_dimension=1, tiled=True),
        lax.psum_scatter(text_up_grad, "dp", scatter_dimension=0, tiled=True),
        lax.psum_scatter(text_down_grad, "dp", scatter_dimension=1, tiled=True),
        lax.psum_scatter(projections_grad, "dp", scatter_dimension=1, tiled=True),
        lax.psum_scatter(merging_qkv_grad, "dp", scatter_dimension=1, tiled=True),
        lax.psum_scatter(merging_out_grad, "dp", scatter_dimension=2, tiled=True),
        lax.psum_scatter(merge_up_grad, "dp", scatter_dimension=0, tiled=True),
        lax.psum_scatter(merge_down_grad, "dp", scatter_dimension=1, tiled=True),
    )
    return (
        jnp.stack(merged_list),
        jnp.stack(loss_list),
        jnp.stack(text_list),
        jnp.stack(image_list),
        text_qkv_done,
        text_out_done,
        text_up_done,
        text_down_done,
        merge_qkv_done,
        merge_out_done,
        merge_up_done,
        merge_down_done,
        projections_done,
        gains_sum,
        offsets_sum,
        head_out,
        up_out,
    )


MESH = pl.DeviceIdType.MESH
BF = jnp.bfloat16
F32 = jnp.float32
T_ATT, T_UP, T_DOWN, M_SELF, M_CROSS, M_UP, M_DOWN = range(7)
BLOCKS = 7
BACK_ORDER = (M_DOWN, M_UP, M_CROSS, M_SELF, T_DOWN, T_UP, T_ATT)
SLOTS = 4
IMAGE_PAD = 160
NORMS = 5


def mm(left, right):
    return lax.dot_general(left, right, (((1,), (0,)), ((), ())), preferred_element_type=F32)


def mm_nt(left, right):
    return lax.dot_general(left, right, (((1,), (1,)), ((), ())), preferred_element_type=F32)


def mm_tn(left, right):
    return lax.dot_general(left, right, (((0,), (0,)), ((), ())), preferred_element_type=F32)


def mm_exact(left, right, dims):
    return lax.dot_general(
        left, right, (dims, ((), ())), precision=EXACT_DOT_MODE, preferred_element_type=F32
    )


NN, NT, TN = ((1,), (0,)), ((1,), (1,)), ((0,), (0,))


def remote(src, dst, send, recv, where):
    return pltpu.make_async_remote_copy(
        src_ref=src, dst_ref=dst, send_sem=send, recv_sem=recv, device_id=where, device_id_type=MESH
    )


def gelu_parts(pre):
    cdf = 0.5 * (1.0 + lax.erf(pre * (1.0 / math.sqrt(2.0))))
    return cdf


def layers(
    wsh, psh, bias, hid0, img, cot, tmask, cmask, id_row, id_col, gains, offs,
    wout, mout, tgout, imout, pjout, lossout, vout,
    G, PJ, H, XH, RSD, SQ, SK, SV, CQ, CK, CV, OA, PS, PC, PRE, ACT, XS, XR, ACC, DZ, DPRE, DQKV, DKV,
    RC, R2, R1, RZ, BG, CT, MS, TG, IMO, IMS, IMR, IML, CG, CLS, DU, DUW, DPJ, PXS, PXR, V, VR, LS,
    own_s, z_s, z_r, s1_s, s1_r, s2_s, s2_r, sc_s, sc_r,
    b2_s, b2_r, b1_s, b1_r, bc_s, bc_r, bz_s, bz_r,
    x_s, x_r, m_s, m_r, cg_s, cg_r, v_s, v_r,
):
    width = hid0.shape[1]
    rows = hid0.shape[0]
    local = width // 4
    heads = local // HEAD_DIM
    quarter = rows // 4
    scale = 1.0 / math.sqrt(HEAD_DIM)
    dp = lax.axis_index("dp")
    z = lax.axis_index("mp")
    y = lax.div(dp, 4)
    x = lax.rem(lax.div(dp, 2), 2)
    c = lax.rem(dp, 2)
    group = lax.div(z, 2)
    rank = lax.rem(z, 2)
    z1 = z + 1 - 2 * rank
    z2 = z + 2 - 4 * group
    z3 = z1 + 2 - 4 * group
    to_x = (dp + 2 - 4 * x, z)
    to_y = (dp + 4 - 8 * y, z)
    to_c = (dp + 1 - 2 * c, z)
    to_z1, to_z2, to_z3 = (dp, z1), (dp, z2), (dp, z3)

    barrier = pltpu.get_barrier_semaphore()
    others = [(lax.rem(dp + step, 8), z) for step in range(1, 8)]
    for where in others + [to_z1, to_z2, to_z3]:
        pl.semaphore_signal(barrier, inc=1, device_id=where, device_id_type=MESH)
    pl.semaphore_wait(barrier, 10)

    def own(k):
        return pltpu.make_async_copy(wsh.at[k], G.at[k, 0, y, x, c], own_s.at[k])

    def hop_z(k):
        return remote(wsh.at[k], G.at[k, 1, y, x, c], z_s.at[k], z_r.at[k], to_z2)

    def hop_1(k, q):
        if q == 0:
            return remote(wsh.at[k], G.at[k, 0, y, x, c], s1_s.at[k, 0], s1_r.at[k, 0], to_x)
        part = G.at[k, 1, y, x, c]
        return remote(part, part, s1_s.at[k, 1], s1_r.at[k, 1], to_y)

    def hop_2(k, q):
        part = G.at[k, 0, y, :, c] if q == 0 else G.at[k, 1, :, x, c]
        return remote(part, part, s2_s.at[k, q], s2_r.at[k, q], to_y if q == 0 else to_x)

    def hop_c(k, q):
        part = G.at[k, q, :, :, c]
        return remote(part, part, sc_s.at[k, q], sc_r.at[k, q], to_c)

    p_own = pltpu.make_async_copy(psh, PJ.at[y, x, c], own_s.at[BLOCKS])
    p_1 = remote(psh, PJ.at[y, x, c], s1_s.at[BLOCKS, 0], s1_r.at[BLOCKS, 0], to_x)
    p_2 = remote(PJ.at[y, :, c], PJ.at[y, :, c], s2_s.at[BLOCKS, 0], s2_r.at[BLOCKS, 0], to_y)
    p_c = remote(PJ.at[:, :, c], PJ.at[:, :, c], sc_s.at[BLOCKS, 0], sc_r.at[BLOCKS, 0], to_c)

    def tick(j):
        k = j
        if k < BLOCKS:
            own(k).start()
            hop_z(k).start()
            hop_1(k, 0).start()
        elif k == BLOCKS:
            p_own.start()
            p_1.start()
        k = j - 1
        if 0 <= k < BLOCKS:
            hop_z(k).wait_recv()
            hop_1(k, 1).start()
        k = j - 2
        if 0 <= k < BLOCKS:
            own(k).wait()
            for q in range(2):
                hop_1(k, q).wait_recv()
                hop_2(k, q).start()
        elif k == BLOCKS:
            p_own.wait()
            p_1.wait_recv()
            p_2.start()
        k = j - 3
        if 0 <= k < BLOCKS:
            for q in range(2):
                hop_2(k, q).wait_recv()
                hop_c(k, q).start()
        elif k == BLOCKS:
            p_2.wait_recv()
            p_c.start()
        k = j - 4
        if 0 <= k < BLOCKS:
            for q in range(2):
                hop_c(k, q).wait_recv()
        elif k == BLOCKS:
            p_c.wait_recv()

    def sent_all():
        for k in range(BLOCKS):
            hop_z(k).wait_send()
            for q in range(2):
                hop_1(k, q).wait_send()
                hop_2(k, q).wait_send()
                hop_c(k, q).wait_send()
        p_1.wait_send()
        p_2.wait_send()
        p_c.wait_send()

    def swap(e):
        return remote(XS.at[e % 2], XR.at[e], x_s.at[e % 2], x_r.at[e], to_z1)

    def swap_start(e):
        if e >= 2:
            swap(e - 2).wait_send()
        XS[e % 2] = ACC[...].astype(BF)
        swap(e).start()

    def swap_sum(e):
        swap(e).wait_recv()
        return XS[e % 2].astype(F32) + XR[e].astype(F32)

    bias_copy = remote(bias, BG.at[1], m_s.at[0], m_r.at[0], to_z2)
    bias_copy.start()
    BG[0] = bias[...]
    cot_copies = [
        remote(cot.at[group], CT.at[z], m_s.at[1], m_r.at[1], to_z1),
        remote(cot.at[1 - group], CT.at[z], m_s.at[2], m_r.at[2], to_z2),
        remote(cot.at[1 - group], CT.at[z], m_s.at[3], m_r.at[3], to_z3),
    ]

    for j in range(4):
        tick(j)
    bias_copy.wait()
    for copy in cot_copies:
        copy.start()
    CT[z] = cot[group]

    def weight(k, q, lo, hi):
        return G[k, q, :, :, :, :, lo:hi].reshape(width, hi - lo)

    def norm_forward(e, before):
        centre = before - jnp.mean(before, -1, keepdims=True)
        inverse = lax.rsqrt(jnp.mean(centre * centre, -1, keepdims=True) + EPS)
        xhat = centre * inverse
        XH[e] = xhat
        RSD[e] = inverse
        return xhat * gains[e : e + 1, :] + offs[NORMS + e : NORMS + e + 1, :]

    def settle_forward(e):
        before = H[e].astype(F32) + offs[e : e + 1, :] + swap_sum(e)
        out = norm_forward(e, before)
        if e + 1 < NORMS:
            H[e + 1] = out.astype(BF)
        return out

    def softmax(scores, mask):
        scores = jnp.where(mask > 0, scores * scale, NEGATIVE)
        raised = jnp.exp(scores - jnp.max(scores, -1, keepdims=True))
        return raised / jnp.sum(raised, -1, keepdims=True)

    def self_attention(k, e, layer):
        ACC[...] = jnp.zeros_like(ACC)

        def part(q, carry):
            made = mm(H[e], weight(k, q, 0, 3 * local))
            queries = (made[:, :local] + BG[q, 2 * layer : 2 * layer + 1, :local]).astype(BF)
            keys = made[:, local : 2 * local].astype(BF)
            values = (
                made[:, 2 * local :] + BG[q, 2 * layer + 1 : 2 * layer + 2, :local]
            ).astype(BF)
            SQ[layer, q], SK[layer, q], SV[layer, q] = queries, keys, values
            mixed = []
            for n in range(heads):
                cut = slice(n * HEAD_DIM, (n + 1) * HEAD_DIM)
                probs = softmax(mm_nt(queries[:, cut], keys[:, cut]), tmask[...]).astype(BF)
                PS[layer, q, n] = probs
                mixed.append(mm(probs, values[:, cut]).astype(BF))
            mixed = jnp.concatenate(mixed, 1)
            OA[layer, q] = mixed
            ACC[...] += mm_nt(mixed, weight(k, q, 3 * local, 4 * local))
            return carry

        lax.fori_loop(0, 2, part, 0)

    def image_keys():
        def part(q, carry):
            made = mm(img[...], weight(M_CROSS, q, local, 3 * local))
            CK[q] = made[:, :local].astype(BF)
            CV[q] = (made[:, local:] + BG[q, 5:6, :local]).astype(BF)
            return carry

        lax.fori_loop(0, 2, part, 0)

    def cross_attention():
        ACC[...] = jnp.zeros_like(ACC)

        def part(q, carry):
            queries = (mm(H[3], weight(M_CROSS, q, 0, local)) + BG[q, 4:5, :local]).astype(BF)
            CQ[q] = queries
            mixed = []
            for n in range(heads):
                cut = slice(n * HEAD_DIM, (n + 1) * HEAD_DIM)
                probs = softmax(mm_nt(queries[:, cut], CK[q, :, cut]), cmask[...]).astype(BF)
                PC[q, n] = probs
                mixed.append(mm(probs, CV[q, :, cut]).astype(BF))
            mixed = jnp.concatenate(mixed, 1)
            OA[2, q] = mixed
            ACC[...] += mm_nt(mixed, weight(M_CROSS, q, 3 * local, 4 * local))
            return carry

        lax.fori_loop(0, 2, part, 0)

    def feed_up(k, e, layer):
        def part(q, carry):
            pre = mm(H[e], weight(k, q, 0, width)) + BG[q, 6 + layer : 7 + layer, :]
            PRE[layer, q] = pre
            ACT[layer, q] = (pre * gelu_parts(pre)).astype(BF)
            return carry

        lax.fori_loop(0, 2, part, 0)

    def feed_down(k, layer):
        ACC[...] = jnp.zeros_like(ACC)

        def part(q, carry):
            ACC[...] += mm_nt(ACT[layer, q], weight(k, q, 0, width))
            return carry

        lax.fori_loop(0, 2, part, 0)

    H[0] = hid0[...]
    tick(4)
    self_attention(T_ATT, 0, 0)
    swap_start(0)
    tick(5)
    settle_forward(0)
    feed_up(T_UP, 1, 0)
    tick(6)
    feed_down(T_DOWN, 0)
    swap_start(1)
    tick(7)
    settle_forward(1)

    def summary_rows():
        spot = lax.broadcasted_iota(jnp.int32, (8, rows), 0)
        place = lax.broadcasted_iota(jnp.int32, (8, rows), 1)
        pick = jnp.where((place == spot * (quarter // 4)) & (spot < 4), 1.0, 0.0).astype(BF)
        text_rows = mm(pick, H[2])
        spot = lax.broadcasted_iota(jnp.int32, (8, img.shape[0]), 0)
        place = lax.broadcasted_iota(jnp.int32, (8, img.shape[0]), 1)
        pick = jnp.where((place == spot * IMAGE_PAD) & (spot < 4), 1.0, 0.0).astype(BF)
        image_rows = mm(pick, img[...])
        CLS[...] = jnp.concatenate([text_rows, image_rows], 0).astype(BF)
        CG[dp] = CLS[...]

    summary_rows()
    summary = [
        remote(CLS, CG.at[dp], cg_s.at[i], cg_r.at[i], where) for i, where in enumerate(others)
    ]
    self_attention(M_SELF, 2, 1)
    swap_start(2)
    for copy in summary:
        copy.start()
    tick(8)
    image_keys()
    settle_forward(2)
    cross_attention()
    swap_start(3)
    tick(9)
    settle_forward(3)
    feed_up(M_UP, 4, 1)
    tick(10)
    feed_down(M_DOWN, 1)
    swap_start(4)
    tick(11)
    merged = settle_forward(4)
    MS[...] = merged.reshape(4, quarter, width)
    mout[group] = MS[z]
    merged_copy = remote(MS.at[z2], mout.at[group], m_s.at[4], m_r.at[4], to_z2)
    merged_copy.start()
    sent_all()

    def back_c(k, q):
        slot = BACK_ORDER.index(k) % SLOTS
        return remote(
            G.at[k, q, :, :, 1 - c], RC.at[slot, q], bc_s.at[k, q], bc_r.at[k, q], to_c
        )

    def back_2(k, q):
        part = G.at[k, 0, 1 - y, :, c] if q == 0 else G.at[k, 1, :, 1 - x, c]
        return remote(part, R2.at[k, q], b2_s.at[k, q], b2_r.at[k, q], to_y if q == 0 else to_x)

    def back_1(k, q):
        part = G.at[k, 0, y, 1 - x, c] if q == 0 else G.at[k, 1, 1 - y, x, c]
        return remote(part, R1.at[k, q], b1_s.at[k, q], b1_r.at[k, q], to_x if q == 0 else to_y)

    def back_z(k):
        return remote(G.at[k, 1, y, x, c], RZ.at[k], bz_s.at[k], bz_r.at[k], to_z2)

    def both(a, b):
        return (a.astype(F32) + b.astype(F32)).astype(BF)

    def back_tick(j):
        n = j
        if n < BLOCKS:
            for q in range(2):
                back_c(BACK_ORDER[n], q).start()
        n = j - 1
        if 0 <= n < BLOCKS:
            k = BACK_ORDER[n]
            for q in range(2):
                back_c(k, q).wait()
                for a in range(2):
                    for b in range(2):
                        G[k, q, a, b, c] = both(G[k, q, a, b, c], RC[n % SLOTS, q, a, b])
                back_2(k, q).start()
        n = j - 2
        if 0 <= n < BLOCKS:
            k = BACK_ORDER[n]
            for q in range(2):
                back_2(k, q).wait()
                for a in range(2):
                    if q == 0:
                        G[k, 0, y, a, c] = both(G[k, 0, y, a, c], R2[k, 0, a])
                    else:
                        G[k, 1, a, x, c] = both(G[k, 1, a, x, c], R2[k, 1, a])
                back_1(k, q).start()
        n = j - 3
        if 0 <= n < BLOCKS:
            k = BACK_ORDER[n]
            back_1(k, 1).wait()
            G[k, 1, y, x, c] = both(G[k, 1, y, x, c], R1[k, 1])
            back_z(k).start()
            back_1(k, 0).wait()
            wout[k] = G[k, 0, y, x, c].astype(F32) + R1[k, 0].astype(F32)
        n = j - 4
        if 0 <= n < BLOCKS:
            k = BACK_ORDER[n]
            back_z(k).wait()
            wout[k] = wout[k] + RZ[k].astype(F32)

    V[...] = jnp.zeros_like(V)

    def norm_backward(e, grad):
        xhat = XH[e]
        V[e : e + 1, :] = jnp.sum(grad * xhat, 0, keepdims=True)
        V[2 * NORMS + e : 2 * NORMS + e + 1, :] = jnp.sum(grad, 0, keepdims=True)
        scaled = grad * gains[e : e + 1, :]
        first = jnp.mean(scaled, -1, keepdims=True)
        second = jnp.mean(scaled * xhat, -1, keepdims=True)
        grad = RSD[e] * (scaled - first - xhat * second)
        DZ[...] = grad
        rounded = grad.astype(BF)
        V[NORMS + e : NORMS + e + 1, :] = jnp.sum(rounded.astype(F32), 0, keepdims=True)
        return rounded

    def keep_grad(k, q, lo, value):
        value = value.astype(BF)
        G[k, q, :, :, :, :, lo : lo + value.shape[1]] = value.reshape(
            2, 2, 2, width // 8, value.shape[1]
        )

    def feed_backward(up, down, e, layer, rounded):
        ACC[...] = jnp.zeros_like(ACC)

        def part(q, carry):
            grad = mm(rounded, weight(down, q, 0, width))
            pre = PRE[layer, q]
            slope = gelu_parts(pre) + pre * (
                jnp.exp(-0.5 * pre * pre) * (1.0 / math.sqrt(2.0 * math.pi))
            )
            grad = (grad * slope).astype(BF)
            DPRE[q] = grad
            V[pl.ds(15 + 2 * q + layer, 1), :] = jnp.sum(grad.astype(F32), 0, keepdims=True)
            ACC[...] += mm_nt(grad, weight(up, q, 0, width))
            return carry

        lax.fori_loop(0, 2, part, 0)

    def feed_down_grad(down, layer, rounded):
        turned = rounded.T

        def part(q, carry):
            keep_grad(down, q, 0, mm(turned, ACT[layer, q]))
            return carry

        lax.fori_loop(0, 2, part, 0)

    def feed_up_grad(up, e):
        turned = H[e].T

        def part(q, carry):
            keep_grad(up, q, 0, mm(turned, DPRE[q]))
            return carry

        lax.fori_loop(0, 2, part, 0)

    def head_backward(probs, queries, keys, values, grad):
        wide = probs.astype(F32)
        grad_values = mm_tn(probs, grad)
        grad_probs = mm_nt(grad, values)
        grad_scores = wide * (grad_probs - jnp.sum(grad_probs * wide, -1, keepdims=True))
        grad_scores = grad_scores.astype(BF)
        grad_queries = mm(grad_scores, keys) * scale
        grad_keys = mm_tn(grad_scores, queries) * scale
        return grad_queries.astype(BF), grad_keys.astype(BF), grad_values.astype(BF)

    def bias_sums(q, layer, grad_queries, grad_values):
        V[pl.ds(19 + 6 * q + 2 * layer, 1), 0:local] = jnp.sum(
            grad_queries.astype(F32), 0, keepdims=True
        )
        V[pl.ds(20 + 6 * q + 2 * layer, 1), 0:local] = jnp.sum(
            grad_values.astype(F32), 0, keepdims=True
        )

    def self_backward(k, layer, rounded):
        ACC[...] = jnp.zeros_like(ACC)

        def part(q, carry):
            grad_mixed = mm(rounded, weight(k, q, 3 * local, 4 * local)).astype(BF)
            parts = []
            for n in range(heads):
                cut = slice(n * HEAD_DIM, (n + 1) * HEAD_DIM)
                parts.append(
                    head_backward(
                        PS[layer, q, n],
                        SQ[layer, q, :, cut],
                        SK[layer, q, :, cut],
                        SV[layer, q, :, cut],
                        grad_mixed[:, cut],
                    )
                )
            made = [jnp.concatenate([part[i] for part in parts], 1) for i in range(3)]
            bias_sums(q, layer, made[0], made[2])
            grads = jnp.concatenate(made, 1)
            DQKV[q] = grads
            ACC[...] += mm_nt(grads, weight(k, q, 0, 3 * local))
            return carry

        lax.fori_loop(0, 2, part, 0)

    def self_grad(k, e, layer, rounded):
        turned = H[e].T
        turned_out = rounded.T

        def part(q, carry):
            keep_grad(
                k,
                q,
                0,
                jnp.concatenate(
                    [mm(turned, DQKV[q]), mm(turned_out, OA[layer, q])], 1
                ),
            )
            return carry

        lax.fori_loop(0, 2, part, 0)

    def cross_backward(rounded):
        ACC[...] = jnp.zeros_like(ACC)

        def part(q, carry):
            grad_mixed = mm(rounded, weight(M_CROSS, q, 3 * local, 4 * local)).astype(BF)
            parts = []
            for n in range(heads):
                cut = slice(n * HEAD_DIM, (n + 1) * HEAD_DIM)
                parts.append(
                    head_backward(
                        PC[q, n],
                        CQ[q, :, cut],
                        CK[q, :, cut],
                        CV[q, :, cut],
                        grad_mixed[:, cut],
                    )
                )
            made = [jnp.concatenate([part[i] for part in parts], 1) for i in range(3)]
            bias_sums(q, 2, made[0], made[2])
            DQKV[q, :, 0:local] = made[0]
            DKV[q] = jnp.concatenate(made[1:], 1)
            ACC[...] += mm_nt(made[0], weight(M_CROSS, q, 0, local))
            return carry

        lax.fori_loop(0, 2, part, 0)

    def image_columns(first, second):
        def rows_of(q, place):
            part = G[M_CROSS, q, lax.div(place, 2), lax.rem(place, 2), :, :, local : 3 * local]
            return part.reshape(local, 2 * local)

        total = None
        for q in range(2):
            turned = jnp.concatenate([rows_of(q, first), rows_of(q, second)], 0)
            term = mm_nt(DKV[q], turned)
            total = term if total is None else total + term
        return total

    def cross_grad(rounded):
        turned = H[3].T
        turned_out = rounded.T
        turned_image = img[...].T

        def part(q, carry):
            keep_grad(
                M_CROSS,
                q,
                0,
                jnp.concatenate(
                    [
                        mm(turned, DQKV[q, :, 0:local]),
                        mm(turned_image, DKV[q]),
                        mm(turned_out, OA[2, q]),
                    ],
                    1,
                ),
            )
            return carry

        lax.fori_loop(0, 2, part, 0)

    def contrast():
        spots = CG.shape[0] * 8
        proj = PJ[...].reshape(width, PJ.shape[-1])
        half = proj.shape[1] // 2
        text_rows = CG[:, 0:8, :].reshape(spots, width)
        image_rows = CG[:, 8:16, :].reshape(spots, width)
        raw_t = mm(text_rows, proj[:, :half])
        raw_w = mm(image_rows, proj[:, half:])
        inv_t = lax.rsqrt(jnp.sum(raw_t * raw_t, -1, keepdims=True) + EPS)
        inv_w = lax.rsqrt(jnp.sum(raw_w * raw_w, -1, keepdims=True) + EPS)
        t, w = raw_t * inv_t, raw_w * inv_w
        row_key, col_key = id_row[:, 0:1], id_col[0:1, 0:spots]
        row_batch, col_batch = id_row[:, 1:2], id_col[1:2, 0:spots]
        live = row_batch == col_batch
        same = jnp.where(live & (row_key == col_key), 1.0, 0.0)
        target = same / jnp.sum(same, 1, keepdims=True)

        def log_rows(scores):
            scores = jnp.where(live, scores / SCORE_SCALE, NEGATIVE)
            shifted = scores - jnp.max(scores, -1, keepdims=True)
            return shifted - jnp.log(jnp.sum(jnp.exp(shifted), -1, keepdims=True))

        log_t = log_rows(mm_exact(t, w, NT))
        log_w = log_rows(mm_exact(w, t, NT))
        loss = -0.5 * (
            jnp.sum(target * jnp.where(live, log_t, 0.0), 1, keepdims=True)
            + jnp.sum(target * jnp.where(live, log_w, 0.0), 1, keepdims=True)
        )
        over_t = (0.5 / SCORE_SCALE) * (jnp.exp(log_t) - target)
        over_w = (0.5 / SCORE_SCALE) * (jnp.exp(log_w) - target)
        grad_t = mm_exact(over_t, w, NN) + mm_exact(over_w, w, TN)
        grad_w = mm_exact(over_t, t, TN) + mm_exact(over_w, t, NN)
        grad_t = (grad_t - t * jnp.sum(t * grad_t, -1, keepdims=True)) * inv_t
        grad_w = (grad_w - w * jnp.sum(w * grad_w, -1, keepdims=True)) * inv_w
        valid = id_row[:, 2:3]
        grad_t, grad_w = grad_t * valid, grad_w * valid
        DU[...] = grad_t.reshape(8, 8, half)
        DUW[...] = grad_w.reshape(8, 8, half)
        LS[...] = jnp.broadcast_to(loss, (spots, 128)).reshape(8, 8, 128)
        DPJ[:, :, 0:half] = mm_exact(text_rows.astype(F32), grad_t, TN).reshape(
            8, width // 8, half
        )
        DPJ[:, :, half:] = mm_exact(image_rows.astype(F32), grad_w, TN).reshape(
            8, width // 8, half
        )
        PXS[0 : width // 8, :] = DPJ[dp]
        PXS[width // 8 :, :] = jnp.concatenate([LS[dp]] * (PXS.shape[1] // 128), 1)

    pair_copy = remote(PXS, PXR, m_s.at[5], m_r.at[5], to_z2)

    for copy in cot_copies:
        copy.wait()
    grad = jnp.concatenate([CT[i].astype(F32)[:quarter] for i in range(4)], 0)
    rounded = norm_backward(4, grad)
    feed_backward(M_UP, M_DOWN, 4, 1, rounded)
    swap_start(5)
    feed_down_grad(M_DOWN, 1, rounded)
    back_tick(0)
    feed_up_grad(M_UP, 4)
    back_tick(1)
    rounded = norm_backward(3, DZ[...] + swap_sum(5))
    cross_backward(rounded)
    swap_start(6)
    IMS[...] = image_columns(z1, z3).astype(BF)
    image_copy = remote(IMS, IMR, m_s.at[6], m_r.at[6], to_z1)
    image_copy.start()
    IMO[...] = image_columns(z, z2)
    cross_grad(rounded)
    back_tick(2)
    rounded = norm_backward(2, DZ[...] + swap_sum(6))
    self_backward(M_SELF, 1, rounded)
    swap_start(7)
    self_grad(M_SELF, 2, 1, rounded)
    back_tick(3)
    for copy in summary:
        copy.wait()
    contrast()
    pair_copy.start()

    proj_text = PJ[:, :, :, :, 0 : PJ.shape[-1] // 2].reshape(width, PJ.shape[-1] // 2)
    extra = mm_exact(DU[dp], proj_text.astype(F32), NT)
    place = lax.broadcasted_iota(jnp.int32, (rows, width), 0)
    grad = DZ[...] + swap_sum(7)
    for n in range(4):
        grad = grad + jnp.where(place == n * (quarter // 4), extra[n : n + 1, :], 0.0)
    rounded = norm_backward(1, grad)
    feed_backward(T_UP, T_DOWN, 1, 0, rounded)
    swap_start(8)
    feed_down_grad(T_DOWN, 0, rounded)
    back_tick(4)
    feed_up_grad(T_UP, 1)
    back_tick(5)
    rounded = norm_backward(0, DZ[...] + swap_sum(8))
    self_backward(T_ATT, 0, rounded)
    swap_start(9)
    self_grad(T_ATT, 0, 0, rounded)
    back_tick(6)

    stat_to = (to_c, to_x, to_y, to_z2)

    def stat_copy(i):
        return remote(V, VR.at[i], v_s.at[i], v_r.at[i], stat_to[i])

    stat_copy(0).start()

    def image_extra(place):
        part = PJ[lax.div(place, 2), lax.rem(place, 2), :, :, PJ.shape[-1] // 2 :]
        return mm_exact(DUW[dp], part.reshape(local, PJ.shape[-1] // 2).astype(F32), NT)

    image_copy.wait()
    IMO[...] += IMR[...].astype(F32)
    extra = jnp.concatenate([image_extra(z), image_extra(z2)], 1)
    first_row = lax.broadcasted_iota(jnp.int32, (8, 2 * local), 0) == 0
    for n in range(4):
        span = slice(n * IMAGE_PAD, n * IMAGE_PAD + 8)
        IMO[span, :] = IMO[span, :] + jnp.where(first_row, extra[n : n + 1, :], 0.0)
    imout[group] = IMO[:, :local].astype(BF)
    IML[...] = IMO[:, local:].astype(BF)
    image_last = remote(IML, imout.at[group], m_s.at[7], m_r.at[7], to_z2)
    image_last.start()

    grad = DZ[...] + swap_sum(9)
    TG[...] = grad.reshape(4, quarter, width)
    tgout[group] = TG[z]
    text_copy = remote(TG.at[z2], tgout.at[group], m_s.at[8], m_r.at[8], to_z2)
    text_copy.start()
    for i in range(4):
        back_tick(7 + i)
        stat_copy(i).wait()
        if i < 3:
            V[...] = V[...] + VR[i]
            stat_copy(i + 1).start()
    vout[0:15, :] = V[0:15, :] + VR[3, 0:15, :]
    vout[16:18, :] = V[15:17, :] + VR[3, 17:19, :]
    vout[24:30, :] = V[19:25, :] + VR[3, 25:31, :]
    pair_copy.wait()
    pjout[...] = PXS[0 : width // 8, :] + PXR[0 : width // 8, :]
    lossout[group] = PXS[width // 8 :, 0:128]
    lossout[1 - group] = PXR[width // 8 :, 0:128]
    image_last.wait()
    text_copy.wait()
    merged_copy.wait()
    swap(8).wait_send()
    swap(9).wait_send()


def fast_shards(
    text_embeds,
    text_lengths,
    image_embeds,
    image_mask,
    image_ids,
    out_cot,
    text_qkv,
    text_out,
    text_up,
    text_down,
    merge_qkv,
    merge_out,
    merge_up,
    merge_down,
    projections,
    norm_gains,
    offsets,
    head_biases,
    up_biases,
):
    micro, pairs, tokens, width = text_embeds.shape
    images = image_embeds.shape[2]
    data_parts = lax.axis_size("dp")
    model_parts = lax.axis_size("mp")
    z = lax.axis_index("mp")
    group = z // 2
    local = width // model_parts
    shard = width // data_parts
    half_micro = micro // 2
    groups = 2
    count = half_micro * pairs
    share = tokens // model_parts
    rows = count * tokens
    quarter = rows // model_parts

    def mine(array):
        return lax.dynamic_slice_in_dim(array, group * half_micro, half_micro, 0)

    def attention_block(qkv, out):
        return jnp.concatenate([qkv[0], qkv[1], qkv[2], out.T], 1)

    wsh = jnp.stack(
        [
            attention_block(text_qkv, text_out),
            text_up,
            text_down.T,
            attention_block(merge_qkv[:3], merge_out[0]),
            attention_block(merge_qkv[3:], merge_out[1]),
            merge_up,
            merge_down.T,
        ]
    )
    psh = jnp.concatenate([projections[0], projections[1]], 1)
    bias = jnp.concatenate(
        [jnp.pad(head_biases, ((0, 0), (0, width - local))), up_biases], 0
    )
    hid0 = (
        mine(text_embeds)
        .reshape(half_micro, pairs, model_parts, share, width)
        .transpose(2, 0, 1, 3, 4)
        .reshape(rows, width)
    )
    img = jnp.pad(
        mine(image_embeds), ((0, 0), (0, 0), (0, IMAGE_PAD - images), (0, 0))
    ).reshape(count * IMAGE_PAD, width)
    cot = jnp.pad(
        out_cot.reshape(groups, quarter, width), ((0, 0), (0, 48 - quarter), (0, 0))
    )
    lengths = mine(text_lengths).reshape(count)
    place = jnp.arange(rows)
    pair_of = (place // share) % count
    token_of = (place // quarter) * share + place % share
    text_live = token_of < lengths[pair_of]
    tmask = ((pair_of[:, None] == pair_of[None, :]) & text_live[None, :]).astype(jnp.float32)
    image_live = jnp.pad(
        mine(image_mask), ((0, 0), (0, 0), (0, IMAGE_PAD - images))
    ).reshape(count * IMAGE_PAD)
    image_of = jnp.arange(count * IMAGE_PAD) // IMAGE_PAD
    cmask = ((pair_of[:, None] == image_of[None, :]) & (image_live > 0)[None, :]).astype(
        jnp.float32
    )
    ids = mine(image_ids).reshape(half_micro, data_parts, pairs).transpose(1, 0, 2)
    batch = jnp.broadcast_to(jnp.arange(half_micro)[None, :, None], ids.shape)
    live = jnp.ones_like(ids)

    def spots(array, fill):
        array = array.reshape(data_parts, count)
        return jnp.pad(
            array, ((0, 0), (0, 8 - count)), constant_values=fill
        ).reshape(data_parts * 8)

    table = jnp.stack([spots(ids, 0), spots(batch, -1), spots(live, 0)]).astype(jnp.float32)
    id_row = jnp.pad(table.T, ((0, 0), (0, 125)))
    id_col = jnp.pad(table, ((0, 5), (0, 128 - data_parts * 8)))

    vmem = pl.BlockSpec(memory_space=pltpu.VMEM)

    def sem(*shape):
        return pltpu.SemaphoreType.DMA(shape)

    def buf(*shape, dtype=BF):
        return pltpu.VMEM(shape, dtype)

    grid = (2, 2, 2, shard)
    scratch = [
        buf(BLOCKS, 2, *grid, width),
        buf(*grid, psh.shape[1]),
        buf(NORMS, rows, width),
        buf(NORMS, rows, width, dtype=F32),
        buf(NORMS, rows, 1, dtype=F32),
        buf(2, 2, rows, local),
        buf(2, 2, rows, local),
        buf(2, 2, rows, local),
        buf(2, rows, local),
        buf(2, count * IMAGE_PAD, local),
        buf(2, count * IMAGE_PAD, local),
        buf(3, 2, rows, local),
        buf(2, 2, local // HEAD_DIM, rows, rows),
        buf(2, local // HEAD_DIM, rows, count * IMAGE_PAD),
        buf(2, 2, rows, width, dtype=F32),
        buf(2, 2, rows, width),
        buf(2, rows, width),
        buf(2 * NORMS, rows, width),
        buf(rows, width, dtype=F32),
        buf(rows, width, dtype=F32),
        buf(2, rows, width),
        buf(2, rows, 3 * local),
        buf(2, count * IMAGE_PAD, 2 * local),
        buf(SLOTS, 2, 2, 2, shard, width),
        buf(BLOCKS, 2, 2, shard, width),
        buf(BLOCKS, 2, shard, width),
        buf(BLOCKS, shard, width),
        buf(2, 8, width, dtype=F32),
        buf(model_parts, 48, width),
        buf(model_parts, quarter, width, dtype=F32),
        buf(model_parts, quarter, width, dtype=F32),
        buf(count * IMAGE_PAD, 2 * local, dtype=F32),
        buf(count * IMAGE_PAD, 2 * local),
        buf(count * IMAGE_PAD, 2 * local),
        buf(count * IMAGE_PAD, local),
        buf(data_parts, 16, width),
        buf(16, width),
        buf(data_parts, 8, psh.shape[1] // 2, dtype=F32),
        buf(data_parts, 8, psh.shape[1] // 2, dtype=F32),
        buf(data_parts, shard, psh.shape[1], dtype=F32),
        buf(shard + 8, psh.shape[1], dtype=F32),
        buf(shard + 8, psh.shape[1], dtype=F32),
        buf(32, width, dtype=F32),
        buf(4, 32, width, dtype=F32),
        buf(data_parts, 8, 128, dtype=F32),
        sem(BLOCKS + 1),
        sem(BLOCKS),
        sem(BLOCKS),
        *[sem(BLOCKS + 1, 2) for _ in range(6)],
        *[sem(BLOCKS, 2) for _ in range(6)],
        *[sem(BLOCKS) for _ in range(2)],
        sem(2),
        sem(2 * NORMS),
        sem(9),
        sem(9),
        sem(data_parts - 1),
        sem(data_parts - 1),
        sem(4),
        sem(4),
    ]
    inputs = (
        wsh, psh, bias, hid0, img, cot, tmask, cmask, id_row, id_col, norm_gains, offsets,
    )
    wout, mout, tgout, imout, pjout, lossout, vout = pl.pallas_call(
        layers,
        out_shape=(
            jax.ShapeDtypeStruct((BLOCKS, shard, width), F32),
            jax.ShapeDtypeStruct((groups, quarter, width), F32),
            jax.ShapeDtypeStruct((groups, quarter, width), F32),
            jax.ShapeDtypeStruct((groups, count * IMAGE_PAD, local), BF),
            jax.ShapeDtypeStruct((shard, psh.shape[1]), F32),
            jax.ShapeDtypeStruct((groups, 8, 128), F32),
            jax.ShapeDtypeStruct((32, width), F32),
        ),
        in_specs=[vmem] * len(inputs),
        out_specs=(vmem,) * 7,
        scratch_shapes=scratch,
        compiler_params=pltpu.CompilerParams(
            collective_id=0, has_side_effects=True, vmem_limit_bytes=63 * 2**20
        ),
    )(*inputs)

    def parts(block, number):
        return block.reshape(shard, number, local).transpose(1, 0, 2)

    def text_shape(array):
        return array.reshape(micro, pairs, share, width)

    split = 3 * local
    image_grad = (
        imout.reshape(micro, pairs, IMAGE_PAD, local)[:, :, :images].astype(F32)
    )
    loss = lossout[:, :count, 0].reshape(micro, pairs)
    return (
        text_shape(mout),
        loss,
        text_shape(tgout),
        image_grad,
        parts(wout[T_ATT, :, :split], 3),
        wout[T_ATT, :, split:].T,
        wout[T_UP],
        wout[T_DOWN].T,
        jnp.concatenate(
            [parts(wout[M_SELF, :, :split], 3), parts(wout[M_CROSS, :, :split], 3)], 0
        ),
        jnp.stack([wout[M_SELF, :, split:].T, wout[M_CROSS, :, split:].T]),
        wout[M_UP],
        wout[M_DOWN].T,
        pjout.reshape(shard, 2, -1).transpose(1, 0, 2),
        vout[0:5],
        vout[5:15],
        vout[24:30, :local],
        vout[16:18],
    )


def solution(mesh):
    placed = (
        P(None, "dp", None, None),
        P(None, "dp"),
        P(None, "dp", None, None),
        P(None, "dp", None),
        P(),
        P(None, "dp", "mp", None),
        P(None, "dp", "mp"),
        P("mp", "dp"),
        P("dp", "mp"),
        P("mp", "dp"),
        P(None, "dp", "mp"),
        P(None, "mp", "dp"),
        P("dp", "mp"),
        P("mp", "dp"),
        P(None, "dp", None),
        P(),
        P(),
        P(None, "mp"),
        P(None, "mp"),
    )
    small = mesh.shape["dp"] == 8 and mesh.shape["mp"] == 4
    return jax.shard_map(
        fast_shards if small else shards,
        mesh=mesh,
        in_specs=placed,
        out_specs=(
            P(None, "dp", "mp", None),
            P(None, "dp"),
            P(None, "dp", "mp", None),
            P(None, "dp", None, "mp"),
            P(None, "dp", "mp"),
            P("mp", "dp"),
            P("dp", "mp"),
            P("mp", "dp"),
            P(None, "dp", "mp"),
            P(None, "mp", "dp"),
            P("dp", "mp"),
            P("mp", "dp"),
            P(None, "dp", None),
            P(),
            P(),
            P(None, "mp"),
            P(None, "mp"),
        ),
        check_vma=False,
    )
```

```python
import math

import jax
import jax.numpy as jnp
from jax import lax
from jax.experimental import pallas as pl
from jax.experimental.pallas import tpu as pltpu
from jax.sharding import PartitionSpec as P

HEAD_DIM = 64


EPS = 1e-06
SCORE_SCALE = 0.05
EXACT_DOT_MODE = lax.Precision.HIGHEST
NEGATIVE = -1e30


def layer_norm(before, gain, shift):
    centre = before - jnp.mean(before, -1, keepdims=True)
    second = jnp.mean(centre * centre, -1, keepdims=True)
    return centre * lax.rsqrt(second + EPS) * gain + shift


def unit_rows(raw):
    return raw * lax.rsqrt(jnp.sum(raw * raw, -1, keepdims=True) + EPS)


def gelu_exact(pre):
    return jax.nn.gelu(pre, approximate=False)


def product(left, right):
    return jnp.dot(left, right, preferred_element_type=jnp.float32)


def row_contract(left, right):
    return lax.dot_general(
        left, right, (((0,), (0,)), ((), ())), preferred_element_type=jnp.float32
    )


def column_contract(left, right):
    return lax.dot_general(
        left, right, (((1,), (1,)), ((), ())), preferred_element_type=jnp.float32
    )


def rows_from(source, start, count):
    return lax.dynamic_slice_in_dim(source, start, count, 0)


def out_term(mixed, weight):

    def term(start, count):
        return product(rows_from(mixed, start, count), weight)

    return term


def back_term(grads, weight):

    def term(start, count):
        return column_contract(rows_from(grads, start, count), weight)

    return term


def joined_split(joined_grad, count):
    rows, columns = joined_grad.shape
    return jnp.transpose(joined_grad.reshape(rows, count, columns // count), (1, 0, 2))


def settle(hidden, term, bias, gain, shift):
    share_rows = hidden.shape[0] // lax.axis_size("mp")
    start = lax.axis_index("mp") * share_rows
    summed = lax.psum_scatter(
        term(jnp.int32(0), share_rows * lax.axis_size("mp")), "mp", scatter_dimension=0, tiled=True
    )
    before = rows_from(hidden, start, share_rows).astype(jnp.float32) + summed + bias
    return (before, layer_norm(before, gain, shift))


def spread(share):
    return lax.all_gather(share.astype(jnp.bfloat16), "mp", axis=0, tiled=True)


def unsettle(grad_share, before, gain, shift):
    _, pull = jax.vjp(layer_norm, before, gain, shift)
    grad_before, grad_gain, grad_shift = pull(grad_share)
    rounded = grad_before.astype(jnp.bfloat16)
    grad_bias = jnp.sum(rounded.astype(jnp.float32), 0)
    grad_full = lax.all_gather(rounded, "mp", axis=0, tiled=True)
    return (grad_before, grad_full, grad_gain, grad_shift, grad_bias)


def gather_back(grad_before, term):
    return grad_before + lax.psum_scatter(
        term(jnp.int32(0), grad_before.shape[0] * lax.axis_size("mp")),
        "mp",
        scatter_dimension=0,
        tiled=True,
    )


def attention_forward(queries, keys, values, valid, scale):
    scores = (
        jnp.einsum("qphd,pkhd->phqk", queries, keys, preferred_element_type=jnp.float32) * scale
    )
    scores = jnp.where(valid[:, None, None, :], scores, NEGATIVE)
    highest = jnp.max(scores, -1, keepdims=True)
    raised = jnp.exp(scores - highest)
    totals = jnp.sum(raised, -1, keepdims=True)
    probs = (raised / totals).astype(jnp.bfloat16)
    mixed = jnp.einsum("phqk,pkhd->qphd", probs, values, preferred_element_type=jnp.float32)
    return (mixed.astype(jnp.bfloat16), highest + jnp.log(totals))


def attention_backward(queries, keys, values, valid, log_total, grad_mixed, scale):
    scores = (
        jnp.einsum("qphd,pkhd->phqk", queries, keys, preferred_element_type=jnp.float32) * scale
    )
    scores = jnp.where(valid[:, None, None, :], scores, NEGATIVE)
    probs = jnp.exp(scores - log_total)
    grad_values = jnp.einsum(
        "phqk,qphd->pkhd",
        probs.astype(jnp.bfloat16),
        grad_mixed,
        preferred_element_type=jnp.float32,
    )
    grad_probs = jnp.einsum(
        "qphd,pkhd->phqk", grad_mixed, values, preferred_element_type=jnp.float32
    )
    grad_scores = probs * (grad_probs - jnp.sum(grad_probs * probs, -1, keepdims=True))
    rounded = grad_scores.astype(jnp.bfloat16)
    grad_queries = (
        jnp.einsum("phqk,pkhd->qphd", rounded, keys, preferred_element_type=jnp.float32) * scale
    )
    grad_keys = (
        jnp.einsum("phqk,qphd->pkhd", rounded, queries, preferred_element_type=jnp.float32) * scale
    )
    return (
        grad_queries.astype(jnp.bfloat16),
        grad_keys.astype(jnp.bfloat16),
        grad_values.astype(jnp.bfloat16),
    )


def self_forward(hidden, joined, bias_query, bias_value, valid, pairs, scale):
    local = joined.shape[1] // 3
    heads = local // HEAD_DIM
    made = product(hidden, joined)
    queries = (
        (made[:, :local] + bias_query).astype(jnp.bfloat16).reshape(-1, pairs, heads, HEAD_DIM)
    )
    keys = jnp.swapaxes(
        made[:, local : 2 * local].astype(jnp.bfloat16).reshape(-1, pairs, heads, HEAD_DIM), 0, 1
    )
    values = jnp.swapaxes(
        (made[:, 2 * local :] + bias_value)
        .astype(jnp.bfloat16)
        .reshape(-1, pairs, heads, HEAD_DIM),
        0,
        1,
    )
    mixed, log_total = attention_forward(queries, keys, values, valid, scale)
    return ((queries, keys, values, log_total), mixed.reshape(-1, local))


def self_backward(kept, hidden, mixed, grad_full, joined, weight_out, valid, scale):
    queries, keys, values, log_total = kept
    rows = hidden.shape[0]
    local = mixed.shape[1]
    grad_mixed = column_contract(grad_full, weight_out).astype(jnp.bfloat16).reshape(queries.shape)
    grad_queries, grad_keys, grad_values = attention_backward(
        queries, keys, values, valid, log_total, grad_mixed, scale
    )
    grads = jnp.concatenate(
        [
            grad_queries.reshape(rows, local),
            jnp.swapaxes(grad_keys, 0, 1).reshape(rows, local),
            jnp.swapaxes(grad_values, 0, 1).reshape(rows, local),
        ],
        1,
    )
    joined_grad = row_contract(hidden, grads)
    out_grad = row_contract(mixed, grad_full)
    bias_query = jnp.sum(grads[:, :local].astype(jnp.float32), 0)
    bias_value = jnp.sum(grads[:, 2 * local :].astype(jnp.float32), 0)
    return (back_term(grads, joined), joined_grad, out_grad, bias_query, bias_value)


def cross_forward(
    hidden, image_rows, weight_query, joined, bias_query, bias_value, valid, pairs, scale
):
    local = weight_query.shape[1]
    heads = local // HEAD_DIM
    queries = (
        (product(hidden, weight_query) + bias_query)
        .astype(jnp.bfloat16)
        .reshape(-1, pairs, heads, HEAD_DIM)
    )
    made = product(image_rows, joined)
    keys = made[:, :local].astype(jnp.bfloat16).reshape(pairs, -1, heads, HEAD_DIM)
    values = (made[:, local:] + bias_value).astype(jnp.bfloat16).reshape(pairs, -1, heads, HEAD_DIM)
    mixed, log_total = attention_forward(queries, keys, values, valid, scale)
    return ((queries, keys, values, log_total), mixed.reshape(-1, local))


def cross_backward(
    kept, hidden, image_rows, mixed, grad_full, weight_query, joined, weight_out, valid, scale
):
    queries, keys, values, log_total = kept
    rows = hidden.shape[0]
    local = mixed.shape[1]
    grad_mixed = column_contract(grad_full, weight_out).astype(jnp.bfloat16).reshape(queries.shape)
    grad_queries, grad_keys, grad_values = attention_backward(
        queries, keys, values, valid, log_total, grad_mixed, scale
    )
    query_grads = grad_queries.reshape(rows, local)
    image_grads = jnp.concatenate([grad_keys.reshape(-1, local), grad_values.reshape(-1, local)], 1)
    query_weight_grad = row_contract(hidden, query_grads)
    joined_grad = row_contract(image_rows, image_grads)
    out_grad = row_contract(mixed, grad_full)
    image_part = column_contract(image_grads, joined)
    bias_query = jnp.sum(query_grads.astype(jnp.float32), 0)
    bias_value = jnp.sum(image_grads[:, local:].astype(jnp.float32), 0)
    return (
        back_term(query_grads, weight_query),
        image_part,
        query_weight_grad,
        joined_grad,
        out_grad,
        bias_query,
        bias_value,
    )


def ffn_forward(hidden, weight_up, bias_up):
    pre = product(hidden, weight_up) + bias_up
    return (pre, gelu_exact(pre).astype(jnp.bfloat16))


def ffn_backward(hidden, pre, active, grad_full, weight_up, weight_down):
    grad_active = column_contract(grad_full, weight_down)
    _, pull = jax.vjp(gelu_exact, pre)
    grad_pre = pull(grad_active)[0].astype(jnp.bfloat16)
    down_grad = row_contract(active, grad_full)
    up_grad = row_contract(hidden, grad_pre)
    bias_grad = jnp.sum(grad_pre.astype(jnp.float32), 0)
    return (back_term(grad_pre, weight_up), up_grad, down_grad, bias_grad)


def contrast(text_cls, image_cls, text_proj, image_proj, own_ids, all_ids):
    caption_normed_embedding, text_pull = jax.vjp(unit_rows, product(text_cls, text_proj))
    picture_normed_embedding, image_pull = jax.vjp(unit_rows, product(image_cls, image_proj))
    gathered_text_features, gathered_image_features = (
        lax.all_gather(caption_normed_embedding, "dp", axis=0, tiled=True),
        lax.all_gather(picture_normed_embedding, "dp", axis=0, tiled=True),
    )
    same = (own_ids[:, None] == all_ids[None, :]).astype(jnp.float32)
    paired_target_index = same / jnp.sum(same, 1, keepdims=True)
    caption_row_logsoftmax = jax.nn.log_softmax(
        jnp.dot(caption_normed_embedding, gathered_image_features.T, precision=EXACT_DOT_MODE)
        / SCORE_SCALE,
        axis=1,
    )
    picture_row_logsoftmax = jax.nn.log_softmax(
        jnp.dot(picture_normed_embedding, gathered_text_features.T, precision=EXACT_DOT_MODE)
        / SCORE_SCALE,
        axis=1,
    )
    loss = -0.5 * (
        jnp.sum(paired_target_index * caption_row_logsoftmax, 1)
        + jnp.sum(paired_target_index * picture_row_logsoftmax, 1)
    )
    caption_score_excess = (
        0.5 * (jnp.exp(caption_row_logsoftmax) - paired_target_index) / SCORE_SCALE
    )
    picture_score_excess = (
        0.5 * (jnp.exp(picture_row_logsoftmax) - paired_target_index) / SCORE_SCALE
    )
    grad_text_own = jnp.dot(caption_score_excess, gathered_image_features, precision=EXACT_DOT_MODE)
    grad_image_own = jnp.dot(picture_score_excess, gathered_text_features, precision=EXACT_DOT_MODE)
    grad_all_image = jnp.dot(
        caption_score_excess.T, caption_normed_embedding, precision=EXACT_DOT_MODE
    )
    grad_all_text = jnp.dot(
        picture_score_excess.T, picture_normed_embedding, precision=EXACT_DOT_MODE
    )
    back_text, back_image = (
        lax.psum_scatter(grad_all_text, "dp", scatter_dimension=0, tiled=True),
        lax.psum_scatter(grad_all_image, "dp", scatter_dimension=0, tiled=True),
    )
    text_feature = grad_text_own + back_text
    image_feature = grad_image_own + back_image
    text_raw_grad = text_pull(text_feature)[0]
    image_raw_grad = image_pull(image_feature)[0]
    text_proj_grad = jnp.dot(
        text_cls.astype(jnp.float32).T, text_raw_grad, precision=EXACT_DOT_MODE
    )
    image_proj_grad = jnp.dot(
        image_cls.astype(jnp.float32).T, image_raw_grad, precision=EXACT_DOT_MODE
    )
    text_cls_grad = jnp.dot(
        text_raw_grad, text_proj.astype(jnp.float32).T, precision=EXACT_DOT_MODE
    )
    image_cls_grad = jnp.dot(
        image_raw_grad, image_proj.astype(jnp.float32).T, precision=EXACT_DOT_MODE
    )
    return (loss, text_cls_grad, image_cls_grad, text_proj_grad, image_proj_grad)


def shards(
    text_embeds,
    text_lengths,
    image_embeds,
    image_mask,
    image_ids,
    out_cot,
    text_qkv,
    text_out,
    text_up,
    text_down,
    merge_qkv,
    merge_out,
    merge_up,
    merge_down,
    projections,
    norm_gains,
    offsets,
    head_biases,
    up_biases,
):
    (
        text_qkv_all,
        text_out_all,
        text_up_all,
        text_down_all,
        merge_qkv_all,
        merge_out_all,
        merge_up_all,
        merge_down_all,
        projections_all,
    ) = (
        lax.all_gather(text_qkv, "dp", axis=1, tiled=True),
        lax.all_gather(text_out, "dp", axis=1, tiled=True),
        lax.all_gather(text_up, "dp", axis=0, tiled=True),
        lax.all_gather(text_down, "dp", axis=1, tiled=True),
        lax.all_gather(merge_qkv, "dp", axis=1, tiled=True),
        lax.all_gather(merge_out, "dp", axis=2, tiled=True),
        lax.all_gather(merge_up, "dp", axis=0, tiled=True),
        lax.all_gather(merge_down, "dp", axis=1, tiled=True),
        lax.all_gather(projections, "dp", axis=1, tiled=True),
    )
    text_joined = jnp.concatenate([text_qkv_all[0], text_qkv_all[1], text_qkv_all[2]], 1)
    self_joined = jnp.concatenate([merge_qkv_all[0], merge_qkv_all[1], merge_qkv_all[2]], 1)
    cross_joined = jnp.concatenate([merge_qkv_all[4], merge_qkv_all[5]], 1)
    micro, pairs, tokens, width = text_embeds.shape
    images = image_embeds.shape[2]
    local = text_qkv_all.shape[2]
    hidden_local = text_up_all.shape[1]
    model_parts = lax.axis_size("mp")
    model_index = lax.axis_index("mp")
    data_index = lax.axis_index("dp")
    scale = 1.0 / math.sqrt(HEAD_DIM)
    first_share = (model_index == 0).astype(jnp.float32)
    text_joined_grad = jnp.zeros((width, 3 * local), jnp.float32)
    text_out_grad = jnp.zeros((local, width), jnp.float32)
    text_up_grad = jnp.zeros((width, hidden_local), jnp.float32)
    text_down_grad = jnp.zeros((hidden_local, width), jnp.float32)
    self_joined_grad = jnp.zeros((width, 3 * local), jnp.float32)
    cross_query_grad = jnp.zeros((width, local), jnp.float32)
    cross_joined_grad = jnp.zeros((width, 2 * local), jnp.float32)
    self_out_grad = jnp.zeros((local, width), jnp.float32)
    cross_out_grad = jnp.zeros((local, width), jnp.float32)
    merge_up_grad = jnp.zeros((width, hidden_local), jnp.float32)
    merge_down_grad = jnp.zeros((hidden_local, width), jnp.float32)
    text_proj_total = jnp.zeros(projections_all.shape[1:], jnp.float32)
    image_proj_total = jnp.zeros(projections_all.shape[1:], jnp.float32)
    gain_list = [jnp.zeros((width,), jnp.float32) for place in range(5)]
    offset_list = [jnp.zeros((width,), jnp.float32) for place in range(10)]
    head_list = [jnp.zeros((local,), jnp.float32) for place in range(6)]
    up_list = [jnp.zeros((hidden_local,), jnp.float32) for place in range(2)]
    merged_list, loss_list, text_list, image_list = ([], [], [], [])
    for step in range(micro):
        hidden0 = jnp.swapaxes(text_embeds[step], 0, 1).reshape(tokens * pairs, width)
        image_rows = image_embeds[step].reshape(pairs * images, width)
        text_valid = (
            lax.broadcasted_iota(jnp.int32, (pairs, tokens), 1) < text_lengths[step][:, None]
        )
        image_valid = image_mask[step] > 0
        kept0, mixed0 = self_forward(
            hidden0, text_joined, head_biases[0], head_biases[1], text_valid, pairs, scale
        )
        before0, share1 = settle(
            hidden0, out_term(mixed0, text_out_all), offsets[0], norm_gains[0], offsets[5]
        )
        hidden1 = spread(share1)
        pre1, active1 = ffn_forward(hidden1, text_up_all, up_biases[0])
        before1, share2 = settle(
            hidden1, out_term(active1, text_down_all), offsets[1], norm_gains[1], offsets[6]
        )
        hidden2 = spread(share2)
        all_ids = image_ids[step]
        own_start = data_index * pairs
        own_ids = lax.dynamic_slice_in_dim(all_ids, own_start, pairs, 0)
        loss, text_cls_grad, image_cls_grad, text_proj_grad, image_proj_grad = contrast(
            hidden2[:pairs],
            image_embeds[step][:, 0],
            projections_all[0],
            projections_all[1],
            own_ids,
            all_ids,
        )
        loss_list.append(loss)
        text_proj_total = text_proj_total + text_proj_grad
        image_proj_total = image_proj_total + image_proj_grad
        kept2, mixed2 = self_forward(
            hidden2, self_joined, head_biases[2], head_biases[3], text_valid, pairs, scale
        )
        before2, share3 = settle(
            hidden2, out_term(mixed2, merge_out_all[0]), offsets[2], norm_gains[2], offsets[7]
        )
        hidden3 = spread(share3)
        kept3, mixed3 = cross_forward(
            hidden3,
            image_rows,
            merge_qkv_all[3],
            cross_joined,
            head_biases[4],
            head_biases[5],
            image_valid,
            pairs,
            scale,
        )
        before3, share4 = settle(
            hidden3, out_term(mixed3, merge_out_all[1]), offsets[3], norm_gains[3], offsets[8]
        )
        hidden4 = spread(share4)
        pre4, active4 = ffn_forward(hidden4, merge_up_all, up_biases[1])
        before4, out_share = settle(
            hidden4, out_term(active4, merge_down_all), offsets[4], norm_gains[4], offsets[9]
        )
        share_tokens = out_share.shape[0] // pairs
        merged_list.append(jnp.swapaxes(out_share.reshape(share_tokens, pairs, width), 0, 1))
        cot_rows = jnp.swapaxes(out_cot[step], 0, 1).reshape(-1, width).astype(jnp.float32)
        grad_before, grad_full, grad_gain, grad_shift, grad_bias = unsettle(
            cot_rows, before4, norm_gains[4], offsets[9]
        )
        gain_list[4] = gain_list[4] + grad_gain
        offset_list[9] = offset_list[9] + grad_shift
        offset_list[4] = offset_list[4] + grad_bias
        term, up_grad, down_grad, bias_up = ffn_backward(
            hidden4, pre4, active4, grad_full, merge_up_all, merge_down_all
        )
        merge_up_grad = merge_up_grad + up_grad
        merge_down_grad = merge_down_grad + down_grad
        up_list[1] = up_list[1] + bias_up
        grad_hidden4 = gather_back(grad_before, term)
        grad_before, grad_full, grad_gain, grad_shift, grad_bias = unsettle(
            grad_hidden4, before3, norm_gains[3], offsets[8]
        )
        gain_list[3] = gain_list[3] + grad_gain
        offset_list[8] = offset_list[8] + grad_shift
        offset_list[3] = offset_list[3] + grad_bias
        term, image_part, query_grad, joined_grad, out_grad, bias_query, bias_value = (
            cross_backward(
                kept3,
                hidden3,
                image_rows,
                mixed3,
                grad_full,
                merge_qkv_all[3],
                cross_joined,
                merge_out_all[1],
                image_valid,
                scale,
            )
        )
        cross_query_grad = cross_query_grad + query_grad
        cross_joined_grad = cross_joined_grad + joined_grad
        cross_out_grad = cross_out_grad + out_grad
        head_list[4] = head_list[4] + bias_query
        head_list[5] = head_list[5] + bias_value
        image_share = lax.psum_scatter(image_part, "mp", scatter_dimension=1, tiled=True).reshape(
            pairs, images, local
        )
        cls_part = lax.dynamic_slice_in_dim(image_cls_grad, model_index * local, local, 1)
        image_list.append(
            jnp.concatenate([image_share[:, :1] + cls_part[:, None], image_share[:, 1:]], 1)
        )
        grad_hidden3 = gather_back(grad_before, term)
        grad_before, grad_full, grad_gain, grad_shift, grad_bias = unsettle(
            grad_hidden3, before2, norm_gains[2], offsets[7]
        )
        gain_list[2] = gain_list[2] + grad_gain
        offset_list[7] = offset_list[7] + grad_shift
        offset_list[2] = offset_list[2] + grad_bias
        term, joined_grad, out_grad, bias_query, bias_value = self_backward(
            kept2, hidden2, mixed2, grad_full, self_joined, merge_out_all[0], text_valid, scale
        )
        self_joined_grad = self_joined_grad + joined_grad
        self_out_grad = self_out_grad + out_grad
        head_list[2] = head_list[2] + bias_query
        head_list[3] = head_list[3] + bias_value
        grad_hidden2 = gather_back(grad_before, term)
        extra = jnp.concatenate(
            [text_cls_grad, jnp.zeros((grad_hidden2.shape[0] - pairs, width), jnp.float32)], 0
        )
        grad_hidden2 = grad_hidden2 + extra * first_share
        grad_before, grad_full, grad_gain, grad_shift, grad_bias = unsettle(
            grad_hidden2, before1, norm_gains[1], offsets[6]
        )
        gain_list[1] = gain_list[1] + grad_gain
        offset_list[6] = offset_list[6] + grad_shift
        offset_list[1] = offset_list[1] + grad_bias
        term, up_grad, down_grad, bias_up = ffn_backward(
            hidden1, pre1, active1, grad_full, text_up_all, text_down_all
        )
        text_up_grad = text_up_grad + up_grad
        text_down_grad = text_down_grad + down_grad
        up_list[0] = up_list[0] + bias_up
        grad_hidden1 = gather_back(grad_before, term)
        grad_before, grad_full, grad_gain, grad_shift, grad_bias = unsettle(
            grad_hidden1, before0, norm_gains[0], offsets[5]
        )
        gain_list[0] = gain_list[0] + grad_gain
        offset_list[5] = offset_list[5] + grad_shift
        offset_list[0] = offset_list[0] + grad_bias
        term, joined_grad, out_grad, bias_query, bias_value = self_backward(
            kept0, hidden0, mixed0, grad_full, text_joined, text_out_all, text_valid, scale
        )
        text_joined_grad = text_joined_grad + joined_grad
        text_out_grad = text_out_grad + out_grad
        head_list[0] = head_list[0] + bias_query
        head_list[1] = head_list[1] + bias_value
        grad_hidden0 = gather_back(grad_before, term)
        text_list.append(jnp.swapaxes(grad_hidden0.reshape(share_tokens, pairs, width), 0, 1))
    head_full = lax.dynamic_update_slice_in_dim(
        jnp.zeros((6, width), jnp.float32), jnp.stack(head_list), model_index * local, 1
    )
    up_full = lax.dynamic_update_slice_in_dim(
        jnp.zeros((2, hidden_local * model_parts), jnp.float32),
        jnp.stack(up_list),
        model_index * hidden_local,
        1,
    )
    gains_sum, offsets_sum, heads_sum, ups_sum = lax.psum(
        (jnp.stack(gain_list), jnp.stack(offset_list), head_full, up_full), ("dp", "mp")
    )
    head_out = lax.dynamic_slice_in_dim(heads_sum, model_index * local, local, 1)
    up_out = lax.dynamic_slice_in_dim(ups_sum, model_index * hidden_local, hidden_local, 1)
    text_qkv_grad = joined_split(text_joined_grad, 3)
    projections_grad = jnp.stack([text_proj_total, image_proj_total])
    merging_qkv_grad = jnp.concatenate(
        [
            joined_split(self_joined_grad, 3),
            cross_query_grad[None],
            joined_split(cross_joined_grad, 2),
        ],
        0,
    )
    merging_out_grad = jnp.stack([self_out_grad, cross_out_grad])
    (
        text_qkv_done,
        text_out_done,
        text_up_done,
        text_down_done,
        projections_done,
        merge_qkv_done,
        merge_out_done,
        merge_up_done,
        merge_down_done,
    ) = (
        lax.psum_scatter(text_qkv_grad, "dp", scatter_dimension=1, tiled=True),
        lax.psum_scatter(text_out_grad, "dp", scatter_dimension=1, tiled=True),
        lax.psum_scatter(text_up_grad, "dp", scatter_dimension=0, tiled=True),
        lax.psum_scatter(text_down_grad, "dp", scatter_dimension=1, tiled=True),
        lax.psum_scatter(projections_grad, "dp", scatter_dimension=1, tiled=True),
        lax.psum_scatter(merging_qkv_grad, "dp", scatter_dimension=1, tiled=True),
        lax.psum_scatter(merging_out_grad, "dp", scatter_dimension=2, tiled=True),
        lax.psum_scatter(merge_up_grad, "dp", scatter_dimension=0, tiled=True),
        lax.psum_scatter(merge_down_grad, "dp", scatter_dimension=1, tiled=True),
    )
    return (
        jnp.stack(merged_list),
        jnp.stack(loss_list),
        jnp.stack(text_list),
        jnp.stack(image_list),
        text_qkv_done,
        text_out_done,
        text_up_done,
        text_down_done,
        merge_qkv_done,
        merge_out_done,
        merge_up_done,
        merge_down_done,
        projections_done,
        gains_sum,
        offsets_sum,
        head_out,
        up_out,
    )


MESH = pl.DeviceIdType.MESH
BF = jnp.bfloat16
F32 = jnp.float32
T_ATT, T_UP, T_DOWN, M_SELF, M_CROSS, M_UP, M_DOWN = range(7)
BLOCKS = 7
BACK_ORDER = (M_DOWN, M_UP, M_CROSS, M_SELF, T_DOWN, T_UP, T_ATT)
SLOTS = 4
IMAGE_PAD = 16
NORMS = 5


def mm(left, right):
    return lax.dot_general(left, right, (((1,), (0,)), ((), ())), preferred_element_type=F32)


def mm_nt(left, right):
    return lax.dot_general(left, right, (((1,), (1,)), ((), ())), preferred_element_type=F32)


def mm_tn(left, right):
    return lax.dot_general(left, right, (((0,), (0,)), ((), ())), preferred_element_type=F32)


def mm_exact(left, right, dims):
    return lax.dot_general(
        left, right, (dims, ((), ())), precision=EXACT_DOT_MODE, preferred_element_type=F32
    )


NN, NT, TN = ((1,), (0,)), ((1,), (1,)), ((0,), (0,))


def remote(src, dst, send, recv, where):
    return pltpu.make_async_remote_copy(
        src_ref=src, dst_ref=dst, send_sem=send, recv_sem=recv, device_id=where, device_id_type=MESH
    )


def gelu_parts(pre):
    cdf = 0.5 * (1.0 + lax.erf(pre * (1.0 / math.sqrt(2.0))))
    return cdf


def layers(
    lengths, *arrays
):
    sources, arrays = arrays[:LOADS], arrays[LOADS:]
    outputs, arrays = arrays[:7], arrays[7:]
    targets, rest = arrays[:LOADS], arrays[LOADS:]
    layers_body(lengths, sources, targets, *targets, *outputs, *rest)


LOADS = 18


def layers_body(
    lengths, sources, targets,
    text_qkv, text_out, text_up, head_bias, up_bias, text_in, text_down, image_mask, image_in,
    merge_qkv, merge_out, merge_up, merge_down, gains, offs, image_ids, projections, cot,
    wout, mout, tgout, imout, pjout, lossout, vout,
    G, PJ, H, XH, RSD, SQ, SK, SV, CQ, CK, CV, OA, PS, PC, PRE, ACT, XS, XR, ACC, DZ, DPRE, DQKV, DKV,
    RC, R2, R1, RZ, BG, CT, MS, TG, IMO, IMS, IMR, IML, tmask, cmask, CG, CLS, DU, DUW, DPJ, PXF, PXS, PXR, LSR, MSB, MRX, V, VR, LS,
    img,
    load_s,
    z_s, z_r, s1_s, s1_r, s2_s, s2_r, sc_s, sc_r,
    b2_s, b2_r, b1_s, b1_r, bc_s, bc_r, bz_s, bz_r,
    x_s, x_r, m_s, m_r, cg_s, cg_r, v_s, v_r,
):
    loads = [
        pltpu.make_async_copy(source, target, load_s.at[i])
        for i, (source, target) in enumerate(zip(sources, targets))
        if i != 8
    ]
    micro, pairs, tokens, width = text_in.shape
    half_micro = micro // 2
    count = half_micro * pairs
    rows = count * tokens
    share = tokens // 4
    images = image_mask.shape[2]
    image_rows = img.shape[0] // half_micro
    local = width // 4
    heads = local // HEAD_DIM
    quarter = rows // 4
    scale = 1.0 / math.sqrt(HEAD_DIM)
    dp = lax.axis_index("dp")
    z = lax.axis_index("mp")
    y = lax.div(dp, 4)
    x = lax.rem(lax.div(dp, 2), 2)
    c = lax.rem(dp, 2)
    group = lax.div(z, 2)
    rank = lax.rem(z, 2)
    z1 = z + 1 - 2 * rank
    z2 = z + 2 - 4 * group
    z3 = z1 + 2 - 4 * group
    to_x = (dp + 2 - 4 * x, z)
    to_y = (dp + 4 - 8 * y, z)
    to_c = (dp + 1 - 2 * c, z)
    to_z1, to_z2, to_z3 = (dp, z1), (dp, z2), (dp, z3)

    mine, theirs = half_micro * group, half_micro * (1 - group)
    part = sources[8].at[pl.ds(mine, half_micro)]
    loads.insert(8, pltpu.make_async_copy(part, image_in, load_s.at[8]))
    barrier = pltpu.get_barrier_semaphore()
    others = [(lax.rem(dp + step, 8), z) for step in range(1, 8)]
    for where in others + [to_z1, to_z2, to_z3]:
        pl.semaphore_signal(barrier, inc=1, device_id=where, device_id_type=MESH)
    for load in loads:
        load.start()
    def attention_block(qkv, out, first):
        turned = turn(out)
        return jnp.concatenate([qkv[first], qkv[first + 1], qkv[first + 2], turned], 1)

    def turn(matrix):
        size = matrix.shape[1]
        unit = jnp.where(
            lax.broadcasted_iota(jnp.int32, (size, size), 0)
            == lax.broadcasted_iota(jnp.int32, (size, size), 1),
            1.0,
            0.0,
        ).astype(BF)
        return mm_nt(unit, matrix).astype(BF)

    def pack(k):
        if k == T_ATT:
            block = attention_block(text_qkv, text_out[...], 0)
        elif k == T_UP:
            block = text_up[...]
        elif k == T_DOWN:
            block = text_down[...]
        elif k == M_SELF:
            block = attention_block(merge_qkv, merge_out[0], 0)
        elif k == M_CROSS:
            block = attention_block(merge_qkv, merge_out[1], 3)
        elif k == M_UP:
            block = merge_up[...]
        else:
            block = merge_down[...]
        G[k, 0, y, x, c] = block

    loads[0].wait()
    loads[1].wait()
    pack(T_ATT)
    pl.semaphore_wait(barrier, 10)

    def x_first(k, q):
        return (k + q) % 2 == 0

    def hop_z(k):
        return remote(
            G.at[k, 0, y, x, c], G.at[k, 1, y, x, c], z_s.at[k], z_r.at[k], to_z2
        )

    def hop_1(k, q):
        part = G.at[k, q, y, x, c]
        return remote(
            part, part, s1_s.at[k, q], s1_r.at[k, q], to_x if x_first(k, q) else to_y
        )

    def hop_2(k, q):
        part = G.at[k, q, y, :, c] if x_first(k, q) else G.at[k, q, :, x, c]
        return remote(
            part, part, s2_s.at[k, q], s2_r.at[k, q], to_y if x_first(k, q) else to_x
        )

    def hop_c(k, q):
        part = G.at[k, q, :, :, c]
        return remote(part, part, sc_s.at[k, q], sc_r.at[k, q], to_c)

    own_proj = PJ.at[y, x, c]
    p_1 = remote(own_proj, own_proj, s1_s.at[BLOCKS, 0], s1_r.at[BLOCKS, 0], to_x)
    p_2 = remote(PJ.at[y, :, c], PJ.at[y, :, c], s2_s.at[BLOCKS, 0], s2_r.at[BLOCKS, 0], to_y)
    p_c = remote(PJ.at[:, :, c], PJ.at[:, :, c], sc_s.at[BLOCKS, 0], sc_r.at[BLOCKS, 0], to_c)

    def tick(j):
        k = j
        if k < BLOCKS:
            if k > 0:
                pack(k)
            hop_z(k).start()
            hop_1(k, 0).start()
        k = j - 1
        if 0 <= k < BLOCKS:
            hop_z(k).wait_recv()
            hop_1(k, 1).start()
        k = j - 2
        if 0 <= k < BLOCKS:
            for q in range(2):
                hop_1(k, q).wait_recv()
                hop_2(k, q).start()
        k = j - 3
        if 0 <= k < BLOCKS:
            for q in range(2):
                hop_2(k, q).wait_recv()
                hop_c(k, q).start()
        k = j - 4
        if 0 <= k < BLOCKS:
            for q in range(2):
                hop_c(k, q).wait_recv()

    def sent_all():
        for k in range(BLOCKS):
            hop_z(k).wait_send()
            for q in range(2):
                hop_1(k, q).wait_send()
                hop_2(k, q).wait_send()
                hop_c(k, q).wait_send()

    def swap(e):
        return remote(XS.at[e % 2], XR.at[e], x_s.at[e % 2], x_r.at[e], to_z1)

    def swap_start(e):
        if e >= 2:
            swap(e - 2).wait_send()
        XS[e % 2] = ACC[...].astype(BF)
        swap(e).start()

    def swap_sum(e):
        swap(e).wait_recv()
        return XS[e % 2].astype(F32) + XR[e].astype(F32)

    for load in loads[2:5]:
        load.wait()
    BG[0, 0:6, 0:local] = head_bias[...]
    BG[0, 6:8, :] = up_bias[...]
    bias_copy = remote(BG.at[0], BG.at[1], m_s.at[0], m_r.at[0], to_z2)
    cot_copies = [
        remote(cot.at[pl.ds(mine, half_micro)], CT.at[z], m_s.at[1], m_r.at[1], to_z1),
        remote(cot.at[pl.ds(theirs, half_micro)], CT.at[z], m_s.at[2], m_r.at[2], to_z2),
        remote(cot.at[pl.ds(theirs, half_micro)], CT.at[z], m_s.at[3], m_r.at[3], to_z3),
    ]

    def pair_of(index):
        side = lax.rem(lax.div(index, share * pairs), half_micro)
        return side * pairs + lax.rem(index, pairs)

    def token_of(index):
        part = lax.div(index, share * count)
        return part * share + lax.div(lax.rem(index, share * pairs), pairs)

    def iota(shape, axis):
        return lax.broadcasted_iota(jnp.int32, shape, axis)

    def image_inputs():
        for n in range(half_micro):
            start, held = n * image_rows, images * pairs
            for low in range(0, image_rows, IMAGE_PAD):
                known = [
                    image_in[n, t]
                    for t in range(low // pairs, min((low + IMAGE_PAD) // pairs, images))
                ]
                missing = IMAGE_PAD - pairs * len(known)
                if missing:
                    known.append(jnp.zeros((missing, width), BF))
                block = jnp.concatenate([part.astype(F32) for part in known], 0)
                img[start + low : start + low + IMAGE_PAD, :] = block.astype(BF)

    def inputs():
        whole = [text_in[mine + n // pairs, n % pairs].astype(F32) for n in range(count)]
        whole = jnp.concatenate(whole, 0).astype(BF)
        to, place = iota((rows, rows), 0), iota((rows, rows), 1)
        order = jnp.where(place == pair_of(to) * tokens + token_of(to), 1.0, 0.0).astype(BF)
        H[0] = mm(order, whole).astype(BF)
        index = iota((1, rows), 1)
        limit = jnp.zeros((1, rows), jnp.int32)
        for n in range(count):
            limit = jnp.where(
                pair_of(index) == n, lengths[n % pairs, mine + n // pairs], limit
            )
        live = jnp.where(token_of(index) < limit, 1.0, 0.0)
        tmask[...] = jnp.where(pair_of(to) == pair_of(place), live, 0.0)
        live = []
        for n in range(half_micro):
            known = jnp.where(image_mask[mine + n] > 0, 1.0, 0.0)
            row = 0.0
            for p in range(pairs):
                size = (images, image_rows)
                to = iota(size, 1)
                fits = (lax.div(to, pairs) == iota(size, 0)) & (lax.rem(to, pairs) == p)
                part = jnp.broadcast_to(known[p : p + 1, :], (8, images)).astype(BF)
                row += mm(part, jnp.where(fits, 1.0, 0.0).astype(BF))
            live.append(row[0:1, :])
        live = jnp.concatenate(live, 1)
        size = (rows, half_micro * image_rows)
        to = iota(size, 1)
        of = lax.div(to, image_rows) * pairs + lax.rem(to, pairs)
        cmask[...] = jnp.where(pair_of(iota(size, 0)) == of, live, 0.0)

    tick(0)
    bias_copy.start()
    tick(1)
    for load in loads[5:]:
        load.wait()
    inputs()
    tick(2)
    image_inputs()
    PJ[y, x, c, :, 0 : PJ.shape[-1] // 2] = projections[0]
    PJ[y, x, c, :, PJ.shape[-1] // 2 :] = projections[1]
    tick(3)
    bias_copy.wait()
    for copy in cot_copies:
        copy.start()
    CT[z] = cot[pl.ds(mine, half_micro)]

    def weight(k, q, lo, hi):
        return G[k, q, :, :, :, :, lo:hi].reshape(width, hi - lo)

    def norm_forward(e, before):
        centre = before - jnp.mean(before, -1, keepdims=True)
        inverse = lax.rsqrt(jnp.mean(centre * centre, -1, keepdims=True) + EPS)
        xhat = centre * inverse
        XH[e] = xhat
        RSD[e] = inverse
        return xhat * gains[e : e + 1, :] + offs[NORMS + e : NORMS + e + 1, :]

    def settle_forward(e):
        before = H[e].astype(F32) + offs[e : e + 1, :] + swap_sum(e)
        out = norm_forward(e, before)
        if e + 1 < NORMS:
            H[e + 1] = out.astype(BF)
        return out

    def softmax(scores, mask):
        scores = jnp.where(mask > 0, scores * scale, NEGATIVE)
        raised = jnp.exp(scores - jnp.max(scores, -1, keepdims=True))
        return raised / jnp.sum(raised, -1, keepdims=True)

    def self_attention(k, e, layer):
        ACC[...] = jnp.zeros_like(ACC)

        def part(q, carry):
            made = mm(H[e], weight(k, q, 0, 3 * local))
            queries = (made[:, :local] + BG[q, 2 * layer : 2 * layer + 1, :local]).astype(BF)
            keys = made[:, local : 2 * local].astype(BF)
            values = (
                made[:, 2 * local :] + BG[q, 2 * layer + 1 : 2 * layer + 2, :local]
            ).astype(BF)
            SQ[layer, q], SK[layer, q], SV[layer, q] = queries, keys, values
            mixed = []
            for n in range(heads):
                cut = slice(n * HEAD_DIM, (n + 1) * HEAD_DIM)
                probs = softmax(mm_nt(queries[:, cut], keys[:, cut]), tmask[...]).astype(BF)
                PS[layer, q, n] = probs
                mixed.append(mm(probs, values[:, cut]).astype(BF))
            mixed = jnp.concatenate(mixed, 1)
            OA[layer, q] = mixed
            ACC[...] += mm_nt(mixed, weight(k, q, 3 * local, 4 * local))
            return carry

        lax.fori_loop(0, 2, part, 0)

    def image_keys():
        def part(q, carry):
            made = mm(img[...], weight(M_CROSS, q, local, 3 * local))
            CK[q] = made[:, :local].astype(BF)
            CV[q] = (made[:, local:] + BG[q, 5:6, :local]).astype(BF)
            return carry

        lax.fori_loop(0, 2, part, 0)

    def cross_attention():
        ACC[...] = jnp.zeros_like(ACC)

        def part(q, carry):
            queries = (mm(H[3], weight(M_CROSS, q, 0, local)) + BG[q, 4:5, :local]).astype(BF)
            CQ[q] = queries
            mixed = []
            for n in range(heads):
                cut = slice(n * HEAD_DIM, (n + 1) * HEAD_DIM)
                probs = softmax(mm_nt(queries[:, cut], CK[q, :, cut]), cmask[...]).astype(BF)
                PC[q, n] = probs
                mixed.append(mm(probs, CV[q, :, cut]).astype(BF))
            mixed = jnp.concatenate(mixed, 1)
            OA[2, q] = mixed
            ACC[...] += mm_nt(mixed, weight(M_CROSS, q, 3 * local, 4 * local))
            return carry

        lax.fori_loop(0, 2, part, 0)

    def feed_up(k, e, layer):
        def part(q, carry):
            pre = mm(H[e], weight(k, q, 0, width)) + BG[q, 6 + layer : 7 + layer, :]
            PRE[layer, q] = pre
            ACT[layer, q] = (pre * gelu_parts(pre)).astype(BF)
            return carry

        lax.fori_loop(0, 2, part, 0)

    def feed_down(k, layer):
        ACC[...] = jnp.zeros_like(ACC)

        def part(q, carry):
            ACC[...] += mm_nt(ACT[layer, q], weight(k, q, 0, width))
            return carry

        lax.fori_loop(0, 2, part, 0)

    tick(4)
    self_attention(T_ATT, 0, 0)
    swap_start(0)
    tick(5)
    settle_forward(0)
    feed_up(T_UP, 1, 0)
    tick(6)
    feed_down(T_DOWN, 0)
    swap_start(1)
    tick(7)
    settle_forward(1)

    def summary_rows():
        def pick(size, step):
            spot, place = iota((8, size), 0), iota((8, size), 1)
            fits = place == lax.div(spot, pairs) * step + lax.rem(spot, pairs)
            return jnp.where(fits & (spot < count), 1.0, 0.0).astype(BF)

        text_rows = mm(pick(rows, share * pairs), H[2])
        image_cls = mm(pick(img.shape[0], image_rows), img[...])
        CLS[...] = jnp.concatenate([text_rows, image_cls], 0).astype(BF)
        CG[dp] = CLS[...]

    summary_rows()
    summary = [
        remote(CLS, CG.at[dp], cg_s.at[i], cg_r.at[i], where) for i, where in enumerate(others)
    ]
    self_attention(M_SELF, 2, 1)
    swap_start(2)
    for copy in summary:
        copy.start()
    tick(8)
    image_keys()
    settle_forward(2)
    cross_attention()
    swap_start(3)
    tick(9)
    settle_forward(3)
    p_1.start()
    feed_up(M_UP, 4, 1)
    tick(10)
    feed_down(M_DOWN, 1)
    swap_start(4)
    p_1.wait()
    p_2.start()
    sent_all()
    V[...] = jnp.zeros_like(V)

    def back_c(k, q):
        slot = BACK_ORDER.index(k) % SLOTS
        return remote(
            G.at[k, q, :, :, 1 - c], RC.at[slot, q], bc_s.at[k, q], bc_r.at[k, q], to_c
        )

    def back_2(k, q):
        part = G.at[k, q, 1 - y, :, c] if x_first(k, q) else G.at[k, q, :, 1 - x, c]
        return remote(
            part, R2.at[k, q], b2_s.at[k, q], b2_r.at[k, q], to_y if x_first(k, q) else to_x
        )

    def back_1(k, q):
        part = G.at[k, q, y, 1 - x, c] if x_first(k, q) else G.at[k, q, 1 - y, x, c]
        return remote(
            part, R1.at[k, q], b1_s.at[k, q], b1_r.at[k, q], to_x if x_first(k, q) else to_y
        )

    def back_z(k):
        return remote(G.at[k, 1, y, x, c], RZ.at[k], bz_s.at[k], bz_r.at[k], to_z2)

    def both(a, b):
        return (a.astype(F32) + b.astype(F32)).astype(BF)

    def c_start(n):
        for q in range(2):
            back_c(BACK_ORDER[n], q).start()

    def a_step(n):
        k = BACK_ORDER[n]
        for q in range(2):
            back_c(k, q).wait()
            for a in range(2):
                for b in range(2):
                    G[k, q, a, b, c] = both(G[k, q, a, b, c], RC[n % SLOTS, q, a, b])
            back_2(k, q).start()

    def b_step(n):
        k = BACK_ORDER[n]
        for q in range(2):
            back_2(k, q).wait()
            for a in range(2):
                if x_first(k, q):
                    G[k, q, y, a, c] = both(G[k, q, y, a, c], R2[k, q, a])
                else:
                    G[k, q, a, x, c] = both(G[k, q, a, x, c], R2[k, q, a])
            back_1(k, q).start()

    def d_step(n):
        k = BACK_ORDER[n]
        back_1(k, 1).wait()
        G[k, 1, y, x, c] = both(G[k, 1, y, x, c], R1[k, 1])
        back_z(k).start()
        back_1(k, 0).wait()
        wout[k] = G[k, 0, y, x, c].astype(F32) + R1[k, 0].astype(F32)

    def e_step(n):
        k = BACK_ORDER[n]
        back_z(k).wait()
        wout[k] = wout[k] + RZ[k].astype(F32)

    def norm_backward(e, grad):
        xhat = XH[e]
        V[e : e + 1, :] = jnp.sum(grad * xhat, 0, keepdims=True)
        V[2 * NORMS + e : 2 * NORMS + e + 1, :] = jnp.sum(grad, 0, keepdims=True)
        scaled = grad * gains[e : e + 1, :]
        first = jnp.mean(scaled, -1, keepdims=True)
        second = jnp.mean(scaled * xhat, -1, keepdims=True)
        grad = RSD[e] * (scaled - first - xhat * second)
        DZ[...] = grad
        rounded = grad.astype(BF)
        V[NORMS + e : NORMS + e + 1, :] = jnp.sum(rounded.astype(F32), 0, keepdims=True)
        return rounded

    def keep_grad(k, q, lo, value):
        value = value.astype(BF)
        G[k, q, :, :, :, :, lo : lo + value.shape[1]] = value.reshape(
            2, 2, 2, width // 8, value.shape[1]
        )

    def feed_backward(up, down, e, layer, rounded):
        ACC[...] = jnp.zeros_like(ACC)
        turned = rounded.T

        def part(q, carry):
            grad = mm(rounded, weight(down, q, 0, width))
            keep_grad(down, q, 0, mm(turned, ACT[layer, q]))
            back_c(down, q).start()
            pre = PRE[layer, q]
            slope = gelu_parts(pre) + pre * (
                jnp.exp(-0.5 * pre * pre) * (1.0 / math.sqrt(2.0 * math.pi))
            )
            grad = (grad * slope).astype(BF)
            DPRE[q] = grad
            V[pl.ds(15 + 2 * q + layer, 1), :] = jnp.sum(grad.astype(F32), 0, keepdims=True)
            ACC[...] += mm_nt(grad, weight(up, q, 0, width))
            return carry

        lax.fori_loop(0, 2, part, 0)

    def feed_up_grad(up, e):
        turned = H[e].T

        def part(q, carry):
            keep_grad(up, q, 0, mm(turned, DPRE[q]))
            return carry

        lax.fori_loop(0, 2, part, 0)

    def head_backward(probs, queries, keys, values, grad):
        wide = probs.astype(F32)
        grad_values = mm_tn(probs, grad)
        grad_probs = mm_nt(grad, values)
        grad_scores = wide * (grad_probs - jnp.sum(grad_probs * wide, -1, keepdims=True))
        grad_scores = grad_scores.astype(BF)
        grad_queries = mm(grad_scores, keys) * scale
        grad_keys = mm_tn(grad_scores, queries) * scale
        return grad_queries.astype(BF), grad_keys.astype(BF), grad_values.astype(BF)

    def bias_sums(q, layer, grad_queries, grad_values):
        V[pl.ds(19 + 6 * q + 2 * layer, 1), 0:local] = jnp.sum(
            grad_queries.astype(F32), 0, keepdims=True
        )
        V[pl.ds(20 + 6 * q + 2 * layer, 1), 0:local] = jnp.sum(
            grad_values.astype(F32), 0, keepdims=True
        )

    def self_backward(k, layer, rounded):
        ACC[...] = jnp.zeros_like(ACC)

        def part(q, carry):
            grad_mixed = mm(rounded, weight(k, q, 3 * local, 4 * local)).astype(BF)
            parts = []
            for n in range(heads):
                cut = slice(n * HEAD_DIM, (n + 1) * HEAD_DIM)
                parts.append(
                    head_backward(
                        PS[layer, q, n],
                        SQ[layer, q, :, cut],
                        SK[layer, q, :, cut],
                        SV[layer, q, :, cut],
                        grad_mixed[:, cut],
                    )
                )
            made = [jnp.concatenate([part[i] for part in parts], 1) for i in range(3)]
            bias_sums(q, layer, made[0], made[2])
            grads = jnp.concatenate(made, 1)
            DQKV[q] = grads
            ACC[...] += mm_nt(grads, weight(k, q, 0, 3 * local))
            return carry

        lax.fori_loop(0, 2, part, 0)

    def self_grad(k, e, layer, rounded):
        turned = H[e].T
        turned_out = rounded.T

        def part(q, carry):
            keep_grad(
                k,
                q,
                0,
                jnp.concatenate(
                    [mm(turned, DQKV[q]), mm(turned_out, OA[layer, q])], 1
                ),
            )
            return carry

        lax.fori_loop(0, 2, part, 0)

    def cross_backward(rounded):
        ACC[...] = jnp.zeros_like(ACC)

        def part(q, carry):
            grad_mixed = mm(rounded, weight(M_CROSS, q, 3 * local, 4 * local)).astype(BF)
            parts = []
            for n in range(heads):
                cut = slice(n * HEAD_DIM, (n + 1) * HEAD_DIM)
                parts.append(
                    head_backward(
                        PC[q, n],
                        CQ[q, :, cut],
                        CK[q, :, cut],
                        CV[q, :, cut],
                        grad_mixed[:, cut],
                    )
                )
            made = [jnp.concatenate([part[i] for part in parts], 1) for i in range(3)]
            bias_sums(q, 2, made[0], made[2])
            DQKV[q, :, 0:local] = made[0]
            DKV[q] = jnp.concatenate(made[1:], 1)
            ACC[...] += mm_nt(made[0], weight(M_CROSS, q, 0, local))
            return carry

        lax.fori_loop(0, 2, part, 0)

    def image_columns(first, second):
        def rows_of(q, place):
            part = G[M_CROSS, q, lax.div(place, 2), lax.rem(place, 2), :, :, local : 3 * local]
            return part.reshape(local, 2 * local)

        total = None
        for q in range(2):
            turned = jnp.concatenate([rows_of(q, first), rows_of(q, second)], 0)
            term = mm_nt(DKV[q], turned)
            total = term if total is None else total + term
        return total

    def cross_grad(rounded):
        turned = H[3].T
        turned_out = rounded.T
        turned_image = img[...].T

        def part(q, carry):
            keep_grad(
                M_CROSS,
                q,
                0,
                jnp.concatenate(
                    [
                        mm(turned, DQKV[q, :, 0:local]),
                        mm(turned_image, DKV[q]),
                        mm(turned_out, OA[2, q]),
                    ],
                    1,
                ),
            )
            return carry

        lax.fori_loop(0, 2, part, 0)

    def contrast():
        spots = CG.shape[0] * 8
        proj = PJ[...].reshape(width, PJ.shape[-1])
        half = proj.shape[1] // 2
        text_rows = CG[:, 0:8, :].reshape(spots, width)
        image_cls = CG[:, 8:16, :].reshape(spots, width)
        raw_t = mm(text_rows, proj[:, :half])
        raw_w = mm(image_cls, proj[:, half:])
        inv_t = lax.rsqrt(jnp.sum(raw_t * raw_t, -1, keepdims=True) + EPS)
        inv_w = lax.rsqrt(jnp.sum(raw_w * raw_w, -1, keepdims=True) + EPS)
        t, w = raw_t * inv_t, raw_w * inv_w
        known = image_ids.shape[1]

        def spread_of(shape, spot_axis, batch):
            spot = lax.broadcasted_iota(jnp.int32, shape, spot_axis)
            pair = lax.broadcasted_iota(jnp.int32, shape, 1 - spot_axis)
            fits = (lax.div(spot, 8) == lax.div(pair, pairs)) & (
                lax.rem(spot, 8) == batch * pairs + lax.rem(pair, pairs)
            )
            return jnp.where(fits, 1.0, 0.0)

        row_key, col_key = 0.0, 0.0
        for n in range(half_micro):
            drawn = image_ids[pl.ds(mine + n, 1), :].astype(F32)
            drawn = jnp.broadcast_to(drawn, (8, known))
            row_key += mm_exact(spread_of((spots, known), 0, n), drawn, NT)[:, 0:1]
            col_key += mm_exact(drawn, spread_of((known, spots), 1, n), NN)[0:1, :]

        def batch_of(axis):
            shape = (spots, 1) if axis == 0 else (1, spots)
            place = lax.rem(lax.broadcasted_iota(jnp.int32, shape, axis), 8)
            return jnp.where(place < count, lax.div(place, pairs), -1)

        row_batch, col_batch = batch_of(0), batch_of(1)
        live = row_batch == col_batch
        same = jnp.where(live & (row_key == col_key), 1.0, 0.0)
        target = same / jnp.sum(same, 1, keepdims=True)

        def log_rows(scores):
            scores = jnp.where(live, scores / SCORE_SCALE, NEGATIVE)
            shifted = scores - jnp.max(scores, -1, keepdims=True)
            return shifted - jnp.log(jnp.sum(jnp.exp(shifted), -1, keepdims=True))

        log_t = log_rows(mm_exact(t, w, NT))
        log_w = log_rows(mm_exact(w, t, NT))
        loss = -0.5 * (
            jnp.sum(target * jnp.where(live, log_t, 0.0), 1, keepdims=True)
            + jnp.sum(target * jnp.where(live, log_w, 0.0), 1, keepdims=True)
        )
        over_t = (0.5 / SCORE_SCALE) * (jnp.exp(log_t) - target)
        over_w = (0.5 / SCORE_SCALE) * (jnp.exp(log_w) - target)
        grad_t = mm_exact(over_t, w, NN) + mm_exact(over_w, w, TN)
        grad_w = mm_exact(over_t, t, TN) + mm_exact(over_w, t, NN)
        grad_t = (grad_t - t * jnp.sum(t * grad_t, -1, keepdims=True)) * inv_t
        grad_w = (grad_w - w * jnp.sum(w * grad_w, -1, keepdims=True)) * inv_w
        valid = jnp.where(row_batch >= 0, 1.0, 0.0)
        grad_t, grad_w = grad_t * valid, grad_w * valid
        DU[...] = grad_t.reshape(8, 8, half)
        DUW[...] = grad_w.reshape(8, 8, half)
        LS[...] = jnp.broadcast_to(loss, (spots, 128)).reshape(8, 8, 128)
        size = (8, width // 8, half)
        DPJ[...] = mm_exact(text_rows.astype(F32), grad_t, TN).reshape(size)
        PXF[:, 0:half] = DPJ[dp]
        DPJ[...] = mm_exact(image_cls.astype(F32), grad_w, TN).reshape(size)
        PXF[:, half:] = DPJ[dp]
        PXS[...] = PXF[...].astype(BF)

    pair_copy = remote(PXS, PXR, m_s.at[5], m_r.at[5], to_z2)
    loss_copy = remote(LS.at[dp], LSR, m_s.at[9], m_r.at[9], to_z2)

    def image_extra(place):
        part = PJ[lax.div(place, 2), lax.rem(place, 2), :, :, PJ.shape[-1] // 2 :]
        return mm_exact(DUW[dp], part.reshape(local, PJ.shape[-1] // 2).astype(F32), NT)

    image_copy = remote(IMS, IMR, m_s.at[6], m_r.at[6], to_z1)
    image_last = remote(IML, imout.at[group], m_s.at[7], m_r.at[7], to_z2)

    def image_finish():
        extra = jnp.concatenate([image_extra(z), image_extra(z2)], 1)
        spot = iota((8, 2 * local), 0)
        image_copy.wait()
        IMO[...] += IMR[...].astype(F32)
        for n in range(count):
            start = n // pairs * image_rows
            span = slice(start, start + 8)
            IMO[span, :] = IMO[span, :] + jnp.where(
                spot == n % pairs, extra[n : n + 1, :], 0.0
            )

        def side_by_side(low):
            parts = [
                IMO[n * image_rows : (n + 1) * image_rows, low : low + local]
                for n in range(half_micro)
            ]
            return jnp.concatenate(parts, 1).astype(BF)

        IML[...] = side_by_side(local)
        image_last.start()
        imout[group] = side_by_side(0)

    for copy in cot_copies:
        copy.wait()
    DZ[...] = jnp.concatenate(
        [
            CT[i, n, t].astype(F32)
            for i in range(4)
            for n in range(half_micro)
            for t in range(share)
        ],
        0,
    )
    merged = settle_forward(4)
    rounded = norm_backward(4, DZ[...])
    feed_backward(M_UP, M_DOWN, 4, 1, rounded)
    MS[...] = merged.reshape(4, quarter, width)
    swap_start(5)
    feed_up_grad(M_UP, 4)
    c_start(1)
    a_step(0)
    mout[group] = MS[z]
    MSB[0] = MS[z2].astype(BF)
    merged_copy = remote(MSB.at[0], MRX.at[0], m_s.at[4], m_r.at[4], to_z2)
    text_copy = remote(MSB.at[1], MRX.at[1], m_s.at[8], m_r.at[8], to_z2)
    merged_copy.start()
    p_2.wait()
    p_c.start()
    rounded = norm_backward(3, DZ[...] + swap_sum(5))
    a_step(1)
    cross_backward(rounded)
    swap_start(6)
    b_step(0)
    IMS[...] = image_columns(z1, z3).astype(BF)
    IMO[...] = image_columns(z, z2)
    cross_grad(rounded)
    c_start(2)
    b_step(1)
    rounded = norm_backward(2, DZ[...] + swap_sum(6))
    a_step(2)
    image_copy.start()
    d_step(0)
    self_backward(M_SELF, 1, rounded)
    swap_start(7)
    self_grad(M_SELF, 2, 1, rounded)
    c_start(3)
    d_step(1)
    b_step(2)
    a_step(3)
    p_c.wait()
    for copy in summary:
        copy.wait()
    contrast()
    pair_copy.start()
    loss_copy.start()

    proj_text = PJ[:, :, :, :, 0 : PJ.shape[-1] // 2].reshape(width, PJ.shape[-1] // 2)
    extra = mm_exact(DU[dp], proj_text.astype(F32), NT)
    place = lax.broadcasted_iota(jnp.int32, (rows, width), 0)
    grad = DZ[...] + swap_sum(7)
    for n in range(count):
        grad = grad + jnp.where(
            place == n // pairs * share * pairs + n % pairs, extra[n : n + 1, :], 0.0
        )
    rounded = norm_backward(1, grad)
    feed_backward(T_UP, T_DOWN, 1, 0, rounded)
    swap_start(8)
    d_step(2)
    feed_up_grad(T_UP, 1)
    c_start(5)
    b_step(3)
    a_step(4)
    image_finish()
    rounded = norm_backward(0, DZ[...] + swap_sum(8))
    a_step(5)
    e_step(0)
    e_step(1)
    self_backward(T_ATT, 0, rounded)
    swap_start(9)

    stat_to = (to_c, to_x, to_y, to_z2)

    def stat_copy(i):
        return remote(V, VR.at[i], v_s.at[i], v_r.at[i], stat_to[i])

    stat_copy(0).start()
    d_step(3)
    b_step(4)
    self_grad(T_ATT, 0, 0, rounded)
    c_start(6)
    b_step(5)
    a_step(6)
    d_step(4)

    grad = DZ[...] + swap_sum(9)
    TG[...] = grad.reshape(4, quarter, width)
    MSB[1] = TG[z2].astype(BF)
    text_copy.start()
    tgout[group] = TG[z]
    def stat_step(i):
        stat_copy(i).wait()
        if i < 3:
            V[...] = V[...] + VR[i]
            stat_copy(i + 1).start()

    stat_step(0)
    d_step(5)
    stat_step(1)
    b_step(6)
    e_step(2)
    stat_step(2)
    e_step(3)
    e_step(4)
    d_step(6)
    stat_step(3)
    vout[0:15, :] = V[0:15, :] + VR[3, 0:15, :]
    vout[16:18, :] = V[15:17, :] + VR[3, 17:19, :]
    vout[24:30, :] = V[19:25, :] + VR[3, 25:31, :]
    e_step(5)
    pair_copy.wait()
    loss_copy.wait()
    pjout[...] = PXF[...] + PXR[...].astype(F32)
    lossout[group] = LS[dp]
    lossout[1 - group] = LSR[...]
    image_last.wait()
    text_copy.wait()
    tgout[1 - group] = MRX[1].astype(F32)
    merged_copy.wait()
    mout[1 - group] = MRX[0].astype(F32)
    swap(8).wait_send()
    swap(9).wait_send()
    e_step(6)


def unpack(
    wout, mout, tgout, imout, pjout, lossout, vout,
    merged, loss, text_grad, image_grad, text_qkv, text_out, text_up, text_down, merge_qkv,
    merge_out, merge_up, merge_down, projections, gains, offs, head_bias, up_bias,
):
    micro, share, pairs, width = merged.shape
    images = image_grad.shape[1]
    local = width // 4
    half_micro = micro // 2
    image_rows = imout.shape[1]

    for m in range(micro):
        side, start = m // half_micro, m % half_micro * share * pairs
        for t in range(share):
            span = slice(start + t * pairs, start + (t + 1) * pairs)
            merged[m, t] = mout[side, span, :]
            text_grad[m, t] = tgout[side, span, :]
        start = m % half_micro * local
        for low in range(0, images * pairs, IMAGE_PAD):
            block = imout[side, low : low + IMAGE_PAD, start : start + local].astype(F32)
            for t in range(low // pairs, min((low + IMAGE_PAD) // pairs, images)):
                image_grad[m, t] = block[t * pairs - low : (t + 1) * pairs - low]

    row = lax.broadcasted_iota(jnp.int32, (pairs, micro), 0)
    column = lax.broadcasted_iota(jnp.int32, (pairs, micro), 1)
    known = jnp.zeros((pairs, micro), F32)
    for m in range(micro):
        for p in range(pairs):
            n = m % half_micro * pairs + p
            known = jnp.where(
                (column == m) & (row == p), lossout[m // half_micro, n : n + 1, 0:1], known
            )
    loss[...] = known

    def block(k, place, out):
        out[...] = wout[k, :, place * local : (place + 1) * local]

    for i in range(3):
        block(T_ATT, i, text_qkv.at[i])
        block(M_SELF, i, merge_qkv.at[i])
        block(M_CROSS, i, merge_qkv.at[3 + i])
    text_out[...] = wout[T_ATT, :, 3 * local :].T
    merge_out[0] = wout[M_SELF, :, 3 * local :].T
    merge_out[1] = wout[M_CROSS, :, 3 * local :].T
    text_up[...] = wout[T_UP]
    merge_up[...] = wout[M_UP]
    text_down[...] = wout[T_DOWN]
    merge_down[...] = wout[M_DOWN]
    half = pjout.shape[1] // 2
    projections[0] = pjout[:, :half]
    projections[1] = pjout[:, half:]
    gains[...] = vout[0:5, :]
    offs[...] = vout[5:15, :]
    up_bias[...] = vout[16:18, :]
    head_bias[...] = vout[24:30, 0:local]


def fast_shards(
    text_embeds,
    text_lengths,
    image_embeds,
    image_mask,
    image_ids,
    out_cot,
    text_qkv,
    text_out,
    text_up,
    text_down,
    merge_qkv,
    merge_out,
    merge_up,
    merge_down,
    projections,
    norm_gains,
    offsets,
    head_biases,
    up_biases,
):
    micro, pairs, tokens, width = text_embeds.shape
    images = image_embeds.shape[2]
    data_parts = lax.axis_size("dp")
    model_parts = lax.axis_size("mp")
    local = width // model_parts
    shard = width // data_parts
    half_micro = micro // 2
    groups = 2
    count = half_micro * pairs
    share = tokens // model_parts
    rows = count * tokens
    quarter = rows // model_parts
    proj_width = 2 * projections.shape[2]
    image_rows = -(-images * pairs // IMAGE_PAD) * IMAGE_PAD
    vmem = pl.BlockSpec(memory_space=pltpu.VMEM)

    def sem(*shape):
        return pltpu.SemaphoreType.DMA(shape)

    def buf(*shape, dtype=BF):
        return pltpu.VMEM(shape, dtype)

    grid = (2, 2, 2, shard)
    inputs = (
        text_qkv, text_out, text_up, head_biases, up_biases, text_embeds, text_down.T, image_mask,
        image_embeds.transpose(0, 2, 1, 3), merge_qkv, merge_out, merge_up, merge_down.T,
        norm_gains, offsets, image_ids, projections, out_cot.transpose(0, 2, 1, 3),
    )
    held = [pltpu.VMEM(array.shape, array.dtype) for array in inputs]
    held[8] = pltpu.VMEM((half_micro, images, pairs, width), BF)
    scratch = [
        *held,
        buf(BLOCKS, 2, *grid, width),
        buf(*grid, proj_width),
        buf(NORMS, rows, width),
        buf(NORMS, rows, width, dtype=F32),
        buf(NORMS, rows, 1, dtype=F32),
        buf(2, 2, rows, local),
        buf(2, 2, rows, local),
        buf(2, 2, rows, local),
        buf(2, rows, local),
        buf(2, half_micro * image_rows, local),
        buf(2, half_micro * image_rows, local),
        buf(3, 2, rows, local),
        buf(2, 2, local // HEAD_DIM, rows, rows),
        buf(2, local // HEAD_DIM, rows, half_micro * image_rows),
        buf(2, 2, rows, width, dtype=F32),
        buf(2, 2, rows, width),
        buf(2, rows, width),
        buf(2 * NORMS, rows, width),
        buf(rows, width, dtype=F32),
        buf(rows, width, dtype=F32),
        buf(2, rows, width),
        buf(2, rows, 3 * local),
        buf(2, half_micro * image_rows, 2 * local),
        buf(SLOTS, 2, 2, 2, shard, width),
        buf(BLOCKS, 2, 2, shard, width),
        buf(BLOCKS, 2, shard, width),
        buf(BLOCKS, shard, width),
        buf(2, 8, width, dtype=F32),
        buf(model_parts, half_micro, share, pairs, width),
        buf(model_parts, quarter, width, dtype=F32),
        buf(model_parts, quarter, width, dtype=F32),
        buf(half_micro * image_rows, 2 * local, dtype=F32),
        buf(half_micro * image_rows, 2 * local),
        buf(half_micro * image_rows, 2 * local),
        buf(image_rows, half_micro * local),
        buf(rows, rows, dtype=F32),
        buf(rows, half_micro * image_rows, dtype=F32),
        buf(data_parts, 16, width),
        buf(16, width),
        buf(data_parts, 8, proj_width // 2, dtype=F32),
        buf(data_parts, 8, proj_width // 2, dtype=F32),
        buf(data_parts, shard, proj_width // 2, dtype=F32),
        buf(shard, proj_width, dtype=F32),
        buf(shard, proj_width),
        buf(shard, proj_width),
        buf(8, 128, dtype=F32),
        buf(2, quarter, width),
        buf(2, quarter, width),
        buf(32, width, dtype=F32),
        buf(4, 32, width, dtype=F32),
        buf(data_parts, 8, 128, dtype=F32),
        buf(half_micro * image_rows, width),
        sem(LOADS),
        sem(BLOCKS),
        sem(BLOCKS),
        *[sem(BLOCKS + 1, 2) for _ in range(6)],
        *[sem(BLOCKS, 2) for _ in range(6)],
        *[sem(BLOCKS) for _ in range(2)],
        sem(2),
        sem(2 * NORMS),
        sem(10),
        sem(10),
        sem(data_parts - 1),
        sem(data_parts - 1),
        sem(4),
        sem(4),
    ]
    packed = pl.pallas_call(
        layers,
        out_shape=(
            jax.ShapeDtypeStruct((BLOCKS, shard, width), F32),
            jax.ShapeDtypeStruct((groups, quarter, width), F32),
            jax.ShapeDtypeStruct((groups, quarter, width), F32),
            jax.ShapeDtypeStruct((groups, image_rows, half_micro * local), BF),
            jax.ShapeDtypeStruct((shard, proj_width), F32),
            jax.ShapeDtypeStruct((groups, 8, 128), F32),
            jax.ShapeDtypeStruct((32, width), F32),
        ),
        in_specs=[pl.BlockSpec(memory_space=pltpu.SMEM)] + [pl.BlockSpec(memory_space=pl.ANY)] * LOADS,
        out_specs=(vmem,) * 7,
        scratch_shapes=scratch,
        compiler_params=pltpu.CompilerParams(
            collective_id=0, has_side_effects=True, vmem_limit_bytes=63 * 2**20
        ),
    )(text_lengths.T, *inputs)

    def out(*shape):
        return jax.ShapeDtypeStruct(shape, F32)

    done = pl.pallas_call(
        unpack,
        out_shape=(
            out(micro, share, pairs, width),
            out(pairs, micro),
            out(micro, share, pairs, width),
            out(micro, images, pairs, local),
            *[
                out(*array.shape)
                for array in (
                    text_qkv, text_out, text_up, text_down.T, merge_qkv, merge_out, merge_up,
                    merge_down.T, projections, norm_gains, offsets, head_biases, up_biases,
                )
            ],
        ),
        in_specs=[vmem] * 7,
        out_specs=(vmem,) * 17,
        compiler_params=pltpu.CompilerParams(vmem_limit_bytes=63 * 2**20),
    )(*packed)
    done = list(done)
    for i in (0, 2, 3):
        done[i] = done[i].transpose(0, 2, 1, 3)
    for i in (1, 7, 11):
        done[i] = done[i].T
    return tuple(done)


def solution(mesh):
    placed = (
        P(None, "dp", None, None),
        P(None, "dp"),
        P(None, "dp", None, None),
        P(None, "dp", None),
        P(),
        P(None, "dp", "mp", None),
        P(None, "dp", "mp"),
        P("mp", "dp"),
        P("dp", "mp"),
        P("mp", "dp"),
        P(None, "dp", "mp"),
        P(None, "mp", "dp"),
        P("dp", "mp"),
        P("mp", "dp"),
        P(None, "dp", None),
        P(),
        P(),
        P(None, "mp"),
        P(None, "mp"),
    )
    small = mesh.shape["dp"] == 8 and mesh.shape["mp"] == 4
    return jax.shard_map(
        fast_shards if small else shards,
        mesh=mesh,
        in_specs=placed,
        out_specs=(
            P(None, "dp", "mp", None),
            P(None, "dp"),
            P(None, "dp", "mp", None),
            P(None, "dp", None, "mp"),
            P(None, "dp", "mp"),
            P("mp", "dp"),
            P("dp", "mp"),
            P("mp", "dp"),
            P(None, "dp", "mp"),
            P(None, "mp", "dp"),
            P("dp", "mp"),
            P("mp", "dp"),
            P(None, "dp", None),
            P(),
            P(),
            P(None, "mp"),
            P(None, "mp"),
        ),
        check_vma=False,
    )
```

```python
import math

import jax
import jax.numpy as jnp
from jax import lax
from jax.experimental import pallas as pl
from jax.experimental.pallas import tpu as pltpu
from jax.sharding import PartitionSpec as P

HEAD_DIM = 64


EPS = 1e-06
SCORE_SCALE = 0.05
EXACT_DOT_MODE = lax.Precision.HIGHEST
NEGATIVE = -1e30


def layer_norm(before, gain, shift):
    centre = before - jnp.mean(before, -1, keepdims=True)
    second = jnp.mean(centre * centre, -1, keepdims=True)
    return centre * lax.rsqrt(second + EPS) * gain + shift


def unit_rows(raw):
    return raw * lax.rsqrt(jnp.sum(raw * raw, -1, keepdims=True) + EPS)


def gelu_exact(pre):
    return jax.nn.gelu(pre, approximate=False)


def product(left, right):
    return jnp.dot(left, right, preferred_element_type=jnp.float32)


def row_contract(left, right):
    return lax.dot_general(
        left, right, (((0,), (0,)), ((), ())), preferred_element_type=jnp.float32
    )


def column_contract(left, right):
    return lax.dot_general(
        left, right, (((1,), (1,)), ((), ())), preferred_element_type=jnp.float32
    )


def rows_from(source, start, count):
    return lax.dynamic_slice_in_dim(source, start, count, 0)


def out_term(mixed, weight):

    def term(start, count):
        return product(rows_from(mixed, start, count), weight)

    return term


def back_term(grads, weight):

    def term(start, count):
        return column_contract(rows_from(grads, start, count), weight)

    return term


def joined_split(joined_grad, count):
    rows, columns = joined_grad.shape
    return jnp.transpose(joined_grad.reshape(rows, count, columns // count), (1, 0, 2))


def settle(hidden, term, bias, gain, shift):
    share_rows = hidden.shape[0] // lax.axis_size("mp")
    start = lax.axis_index("mp") * share_rows
    summed = lax.psum_scatter(
        term(jnp.int32(0), share_rows * lax.axis_size("mp")), "mp", scatter_dimension=0, tiled=True
    )
    before = rows_from(hidden, start, share_rows).astype(jnp.float32) + summed + bias
    return (before, layer_norm(before, gain, shift))


def spread(share):
    return lax.all_gather(share.astype(jnp.bfloat16), "mp", axis=0, tiled=True)


def unsettle(grad_share, before, gain, shift):
    _, pull = jax.vjp(layer_norm, before, gain, shift)
    grad_before, grad_gain, grad_shift = pull(grad_share)
    rounded = grad_before.astype(jnp.bfloat16)
    grad_bias = jnp.sum(rounded.astype(jnp.float32), 0)
    grad_full = lax.all_gather(rounded, "mp", axis=0, tiled=True)
    return (grad_before, grad_full, grad_gain, grad_shift, grad_bias)


def gather_back(grad_before, term):
    return grad_before + lax.psum_scatter(
        term(jnp.int32(0), grad_before.shape[0] * lax.axis_size("mp")),
        "mp",
        scatter_dimension=0,
        tiled=True,
    )


def attention_forward(queries, keys, values, valid, scale):
    scores = (
        jnp.einsum("qphd,pkhd->phqk", queries, keys, preferred_element_type=jnp.float32) * scale
    )
    scores = jnp.where(valid[:, None, None, :], scores, NEGATIVE)
    highest = jnp.max(scores, -1, keepdims=True)
    raised = jnp.exp(scores - highest)
    totals = jnp.sum(raised, -1, keepdims=True)
    probs = (raised / totals).astype(jnp.bfloat16)
    mixed = jnp.einsum("phqk,pkhd->qphd", probs, values, preferred_element_type=jnp.float32)
    return (mixed.astype(jnp.bfloat16), highest + jnp.log(totals))


def attention_backward(queries, keys, values, valid, log_total, grad_mixed, scale):
    scores = (
        jnp.einsum("qphd,pkhd->phqk", queries, keys, preferred_element_type=jnp.float32) * scale
    )
    scores = jnp.where(valid[:, None, None, :], scores, NEGATIVE)
    probs = jnp.exp(scores - log_total)
    grad_values = jnp.einsum(
        "phqk,qphd->pkhd",
        probs.astype(jnp.bfloat16),
        grad_mixed,
        preferred_element_type=jnp.float32,
    )
    grad_probs = jnp.einsum(
        "qphd,pkhd->phqk", grad_mixed, values, preferred_element_type=jnp.float32
    )
    grad_scores = probs * (grad_probs - jnp.sum(grad_probs * probs, -1, keepdims=True))
    rounded = grad_scores.astype(jnp.bfloat16)
    grad_queries = (
        jnp.einsum("phqk,pkhd->qphd", rounded, keys, preferred_element_type=jnp.float32) * scale
    )
    grad_keys = (
        jnp.einsum("phqk,qphd->pkhd", rounded, queries, preferred_element_type=jnp.float32) * scale
    )
    return (
        grad_queries.astype(jnp.bfloat16),
        grad_keys.astype(jnp.bfloat16),
        grad_values.astype(jnp.bfloat16),
    )


def self_forward(hidden, joined, bias_query, bias_value, valid, pairs, scale):
    local = joined.shape[1] // 3
    heads = local // HEAD_DIM
    made = product(hidden, joined)
    queries = (
        (made[:, :local] + bias_query).astype(jnp.bfloat16).reshape(-1, pairs, heads, HEAD_DIM)
    )
    keys = jnp.swapaxes(
        made[:, local : 2 * local].astype(jnp.bfloat16).reshape(-1, pairs, heads, HEAD_DIM), 0, 1
    )
    values = jnp.swapaxes(
        (made[:, 2 * local :] + bias_value)
        .astype(jnp.bfloat16)
        .reshape(-1, pairs, heads, HEAD_DIM),
        0,
        1,
    )
    mixed, log_total = attention_forward(queries, keys, values, valid, scale)
    return ((queries, keys, values, log_total), mixed.reshape(-1, local))


def self_backward(kept, hidden, mixed, grad_full, joined, weight_out, valid, scale):
    queries, keys, values, log_total = kept
    rows = hidden.shape[0]
    local = mixed.shape[1]
    grad_mixed = column_contract(grad_full, weight_out).astype(jnp.bfloat16).reshape(queries.shape)
    grad_queries, grad_keys, grad_values = attention_backward(
        queries, keys, values, valid, log_total, grad_mixed, scale
    )
    grads = jnp.concatenate(
        [
            grad_queries.reshape(rows, local),
            jnp.swapaxes(grad_keys, 0, 1).reshape(rows, local),
            jnp.swapaxes(grad_values, 0, 1).reshape(rows, local),
        ],
        1,
    )
    joined_grad = row_contract(hidden, grads)
    out_grad = row_contract(mixed, grad_full)
    bias_query = jnp.sum(grads[:, :local].astype(jnp.float32), 0)
    bias_value = jnp.sum(grads[:, 2 * local :].astype(jnp.float32), 0)
    return (back_term(grads, joined), joined_grad, out_grad, bias_query, bias_value)


def cross_forward(
    hidden, image_rows, weight_query, joined, bias_query, bias_value, valid, pairs, scale
):
    local = weight_query.shape[1]
    heads = local // HEAD_DIM
    queries = (
        (product(hidden, weight_query) + bias_query)
        .astype(jnp.bfloat16)
        .reshape(-1, pairs, heads, HEAD_DIM)
    )
    made = product(image_rows, joined)
    keys = made[:, :local].astype(jnp.bfloat16).reshape(pairs, -1, heads, HEAD_DIM)
    values = (made[:, local:] + bias_value).astype(jnp.bfloat16).reshape(pairs, -1, heads, HEAD_DIM)
    mixed, log_total = attention_forward(queries, keys, values, valid, scale)
    return ((queries, keys, values, log_total), mixed.reshape(-1, local))


def cross_backward(
    kept, hidden, image_rows, mixed, grad_full, weight_query, joined, weight_out, valid, scale
):
    queries, keys, values, log_total = kept
    rows = hidden.shape[0]
    local = mixed.shape[1]
    grad_mixed = column_contract(grad_full, weight_out).astype(jnp.bfloat16).reshape(queries.shape)
    grad_queries, grad_keys, grad_values = attention_backward(
        queries, keys, values, valid, log_total, grad_mixed, scale
    )
    query_grads = grad_queries.reshape(rows, local)
    image_grads = jnp.concatenate([grad_keys.reshape(-1, local), grad_values.reshape(-1, local)], 1)
    query_weight_grad = row_contract(hidden, query_grads)
    joined_grad = row_contract(image_rows, image_grads)
    out_grad = row_contract(mixed, grad_full)
    image_part = column_contract(image_grads, joined)
    bias_query = jnp.sum(query_grads.astype(jnp.float32), 0)
    bias_value = jnp.sum(image_grads[:, local:].astype(jnp.float32), 0)
    return (
        back_term(query_grads, weight_query),
        image_part,
        query_weight_grad,
        joined_grad,
        out_grad,
        bias_query,
        bias_value,
    )


def ffn_forward(hidden, weight_up, bias_up):
    pre = product(hidden, weight_up) + bias_up
    return (pre, gelu_exact(pre).astype(jnp.bfloat16))


def ffn_backward(hidden, pre, active, grad_full, weight_up, weight_down):
    grad_active = column_contract(grad_full, weight_down)
    _, pull = jax.vjp(gelu_exact, pre)
    grad_pre = pull(grad_active)[0].astype(jnp.bfloat16)
    down_grad = row_contract(active, grad_full)
    up_grad = row_contract(hidden, grad_pre)
    bias_grad = jnp.sum(grad_pre.astype(jnp.float32), 0)
    return (back_term(grad_pre, weight_up), up_grad, down_grad, bias_grad)


def contrast(text_cls, image_cls, text_proj, image_proj, own_ids, all_ids):
    caption_normed_embedding, text_pull = jax.vjp(unit_rows, product(text_cls, text_proj))
    picture_normed_embedding, image_pull = jax.vjp(unit_rows, product(image_cls, image_proj))
    gathered_text_features, gathered_image_features = (
        lax.all_gather(caption_normed_embedding, "dp", axis=0, tiled=True),
        lax.all_gather(picture_normed_embedding, "dp", axis=0, tiled=True),
    )
    same = (own_ids[:, None] == all_ids[None, :]).astype(jnp.float32)
    paired_target_index = same / jnp.sum(same, 1, keepdims=True)
    caption_row_logsoftmax = jax.nn.log_softmax(
        jnp.dot(caption_normed_embedding, gathered_image_features.T, precision=EXACT_DOT_MODE)
        / SCORE_SCALE,
        axis=1,
    )
    picture_row_logsoftmax = jax.nn.log_softmax(
        jnp.dot(picture_normed_embedding, gathered_text_features.T, precision=EXACT_DOT_MODE)
        / SCORE_SCALE,
        axis=1,
    )
    loss = -0.5 * (
        jnp.sum(paired_target_index * caption_row_logsoftmax, 1)
        + jnp.sum(paired_target_index * picture_row_logsoftmax, 1)
    )
    caption_score_excess = (
        0.5 * (jnp.exp(caption_row_logsoftmax) - paired_target_index) / SCORE_SCALE
    )
    picture_score_excess = (
        0.5 * (jnp.exp(picture_row_logsoftmax) - paired_target_index) / SCORE_SCALE
    )
    grad_text_own = jnp.dot(caption_score_excess, gathered_image_features, precision=EXACT_DOT_MODE)
    grad_image_own = jnp.dot(picture_score_excess, gathered_text_features, precision=EXACT_DOT_MODE)
    grad_all_image = jnp.dot(
        caption_score_excess.T, caption_normed_embedding, precision=EXACT_DOT_MODE
    )
    grad_all_text = jnp.dot(
        picture_score_excess.T, picture_normed_embedding, precision=EXACT_DOT_MODE
    )
    back_text, back_image = (
        lax.psum_scatter(grad_all_text, "dp", scatter_dimension=0, tiled=True),
        lax.psum_scatter(grad_all_image, "dp", scatter_dimension=0, tiled=True),
    )
    text_feature = grad_text_own + back_text
    image_feature = grad_image_own + back_image
    text_raw_grad = text_pull(text_feature)[0]
    image_raw_grad = image_pull(image_feature)[0]
    text_proj_grad = jnp.dot(
        text_cls.astype(jnp.float32).T, text_raw_grad, precision=EXACT_DOT_MODE
    )
    image_proj_grad = jnp.dot(
        image_cls.astype(jnp.float32).T, image_raw_grad, precision=EXACT_DOT_MODE
    )
    text_cls_grad = jnp.dot(
        text_raw_grad, text_proj.astype(jnp.float32).T, precision=EXACT_DOT_MODE
    )
    image_cls_grad = jnp.dot(
        image_raw_grad, image_proj.astype(jnp.float32).T, precision=EXACT_DOT_MODE
    )
    return (loss, text_cls_grad, image_cls_grad, text_proj_grad, image_proj_grad)


def shards(
    text_embeds,
    text_lengths,
    image_embeds,
    image_mask,
    image_ids,
    out_cot,
    text_qkv,
    text_out,
    text_up,
    text_down,
    merge_qkv,
    merge_out,
    merge_up,
    merge_down,
    projections,
    norm_gains,
    offsets,
    head_biases,
    up_biases,
):
    (
        text_qkv_all,
        text_out_all,
        text_up_all,
        text_down_all,
        merge_qkv_all,
        merge_out_all,
        merge_up_all,
        merge_down_all,
        projections_all,
    ) = (
        lax.all_gather(text_qkv, "dp", axis=1, tiled=True),
        lax.all_gather(text_out, "dp", axis=1, tiled=True),
        lax.all_gather(text_up, "dp", axis=0, tiled=True),
        lax.all_gather(text_down, "dp", axis=1, tiled=True),
        lax.all_gather(merge_qkv, "dp", axis=1, tiled=True),
        lax.all_gather(merge_out, "dp", axis=2, tiled=True),
        lax.all_gather(merge_up, "dp", axis=0, tiled=True),
        lax.all_gather(merge_down, "dp", axis=1, tiled=True),
        lax.all_gather(projections, "dp", axis=1, tiled=True),
    )
    text_joined = jnp.concatenate([text_qkv_all[0], text_qkv_all[1], text_qkv_all[2]], 1)
    self_joined = jnp.concatenate([merge_qkv_all[0], merge_qkv_all[1], merge_qkv_all[2]], 1)
    cross_joined = jnp.concatenate([merge_qkv_all[4], merge_qkv_all[5]], 1)
    micro, pairs, tokens, width = text_embeds.shape
    images = image_embeds.shape[2]
    local = text_qkv_all.shape[2]
    hidden_local = text_up_all.shape[1]
    model_parts = lax.axis_size("mp")
    model_index = lax.axis_index("mp")
    data_index = lax.axis_index("dp")
    scale = 1.0 / math.sqrt(HEAD_DIM)
    first_share = (model_index == 0).astype(jnp.float32)
    text_joined_grad = jnp.zeros((width, 3 * local), jnp.float32)
    text_out_grad = jnp.zeros((local, width), jnp.float32)
    text_up_grad = jnp.zeros((width, hidden_local), jnp.float32)
    text_down_grad = jnp.zeros((hidden_local, width), jnp.float32)
    self_joined_grad = jnp.zeros((width, 3 * local), jnp.float32)
    cross_query_grad = jnp.zeros((width, local), jnp.float32)
    cross_joined_grad = jnp.zeros((width, 2 * local), jnp.float32)
    self_out_grad = jnp.zeros((local, width), jnp.float32)
    cross_out_grad = jnp.zeros((local, width), jnp.float32)
    merge_up_grad = jnp.zeros((width, hidden_local), jnp.float32)
    merge_down_grad = jnp.zeros((hidden_local, width), jnp.float32)
    text_proj_total = jnp.zeros(projections_all.shape[1:], jnp.float32)
    image_proj_total = jnp.zeros(projections_all.shape[1:], jnp.float32)
    gain_list = [jnp.zeros((width,), jnp.float32) for place in range(5)]
    offset_list = [jnp.zeros((width,), jnp.float32) for place in range(10)]
    head_list = [jnp.zeros((local,), jnp.float32) for place in range(6)]
    up_list = [jnp.zeros((hidden_local,), jnp.float32) for place in range(2)]
    merged_list, loss_list, text_list, image_list = ([], [], [], [])
    for step in range(micro):
        hidden0 = jnp.swapaxes(text_embeds[step], 0, 1).reshape(tokens * pairs, width)
        image_rows = image_embeds[step].reshape(pairs * images, width)
        text_valid = (
            lax.broadcasted_iota(jnp.int32, (pairs, tokens), 1) < text_lengths[step][:, None]
        )
        image_valid = image_mask[step] > 0
        kept0, mixed0 = self_forward(
            hidden0, text_joined, head_biases[0], head_biases[1], text_valid, pairs, scale
        )
        before0, share1 = settle(
            hidden0, out_term(mixed0, text_out_all), offsets[0], norm_gains[0], offsets[5]
        )
        hidden1 = spread(share1)
        pre1, active1 = ffn_forward(hidden1, text_up_all, up_biases[0])
        before1, share2 = settle(
            hidden1, out_term(active1, text_down_all), offsets[1], norm_gains[1], offsets[6]
        )
        hidden2 = spread(share2)
        all_ids = image_ids[step]
        own_start = data_index * pairs
        own_ids = lax.dynamic_slice_in_dim(all_ids, own_start, pairs, 0)
        loss, text_cls_grad, image_cls_grad, text_proj_grad, image_proj_grad = contrast(
            hidden2[:pairs],
            image_embeds[step][:, 0],
            projections_all[0],
            projections_all[1],
            own_ids,
            all_ids,
        )
        loss_list.append(loss)
        text_proj_total = text_proj_total + text_proj_grad
        image_proj_total = image_proj_total + image_proj_grad
        kept2, mixed2 = self_forward(
            hidden2, self_joined, head_biases[2], head_biases[3], text_valid, pairs, scale
        )
        before2, share3 = settle(
            hidden2, out_term(mixed2, merge_out_all[0]), offsets[2], norm_gains[2], offsets[7]
        )
        hidden3 = spread(share3)
        kept3, mixed3 = cross_forward(
            hidden3,
            image_rows,
            merge_qkv_all[3],
            cross_joined,
            head_biases[4],
            head_biases[5],
            image_valid,
            pairs,
            scale,
        )
        before3, share4 = settle(
            hidden3, out_term(mixed3, merge_out_all[1]), offsets[3], norm_gains[3], offsets[8]
        )
        hidden4 = spread(share4)
        pre4, active4 = ffn_forward(hidden4, merge_up_all, up_biases[1])
        before4, out_share = settle(
            hidden4, out_term(active4, merge_down_all), offsets[4], norm_gains[4], offsets[9]
        )
        share_tokens = out_share.shape[0] // pairs
        merged_list.append(jnp.swapaxes(out_share.reshape(share_tokens, pairs, width), 0, 1))
        cot_rows = jnp.swapaxes(out_cot[step], 0, 1).reshape(-1, width).astype(jnp.float32)
        grad_before, grad_full, grad_gain, grad_shift, grad_bias = unsettle(
            cot_rows, before4, norm_gains[4], offsets[9]
        )
        gain_list[4] = gain_list[4] + grad_gain
        offset_list[9] = offset_list[9] + grad_shift
        offset_list[4] = offset_list[4] + grad_bias
        term, up_grad, down_grad, bias_up = ffn_backward(
            hidden4, pre4, active4, grad_full, merge_up_all, merge_down_all
        )
        merge_up_grad = merge_up_grad + up_grad
        merge_down_grad = merge_down_grad + down_grad
        up_list[1] = up_list[1] + bias_up
        grad_hidden4 = gather_back(grad_before, term)
        grad_before, grad_full, grad_gain, grad_shift, grad_bias = unsettle(
            grad_hidden4, before3, norm_gains[3], offsets[8]
        )
        gain_list[3] = gain_list[3] + grad_gain
        offset_list[8] = offset_list[8] + grad_shift
        offset_list[3] = offset_list[3] + grad_bias
        term, image_part, query_grad, joined_grad, out_grad, bias_query, bias_value = (
            cross_backward(
                kept3,
                hidden3,
                image_rows,
                mixed3,
                grad_full,
                merge_qkv_all[3],
                cross_joined,
                merge_out_all[1],
                image_valid,
                scale,
            )
        )
        cross_query_grad = cross_query_grad + query_grad
        cross_joined_grad = cross_joined_grad + joined_grad
        cross_out_grad = cross_out_grad + out_grad
        head_list[4] = head_list[4] + bias_query
        head_list[5] = head_list[5] + bias_value
        image_share = lax.psum_scatter(image_part, "mp", scatter_dimension=1, tiled=True).reshape(
            pairs, images, local
        )
        cls_part = lax.dynamic_slice_in_dim(image_cls_grad, model_index * local, local, 1)
        image_list.append(
            jnp.concatenate([image_share[:, :1] + cls_part[:, None], image_share[:, 1:]], 1)
        )
        grad_hidden3 = gather_back(grad_before, term)
        grad_before, grad_full, grad_gain, grad_shift, grad_bias = unsettle(
            grad_hidden3, before2, norm_gains[2], offsets[7]
        )
        gain_list[2] = gain_list[2] + grad_gain
        offset_list[7] = offset_list[7] + grad_shift
        offset_list[2] = offset_list[2] + grad_bias
        term, joined_grad, out_grad, bias_query, bias_value = self_backward(
            kept2, hidden2, mixed2, grad_full, self_joined, merge_out_all[0], text_valid, scale
        )
        self_joined_grad = self_joined_grad + joined_grad
        self_out_grad = self_out_grad + out_grad
        head_list[2] = head_list[2] + bias_query
        head_list[3] = head_list[3] + bias_value
        grad_hidden2 = gather_back(grad_before, term)
        extra = jnp.concatenate(
            [text_cls_grad, jnp.zeros((grad_hidden2.shape[0] - pairs, width), jnp.float32)], 0
        )
        grad_hidden2 = grad_hidden2 + extra * first_share
        grad_before, grad_full, grad_gain, grad_shift, grad_bias = unsettle(
            grad_hidden2, before1, norm_gains[1], offsets[6]
        )
        gain_list[1] = gain_list[1] + grad_gain
        offset_list[6] = offset_list[6] + grad_shift
        offset_list[1] = offset_list[1] + grad_bias
        term, up_grad, down_grad, bias_up = ffn_backward(
            hidden1, pre1, active1, grad_full, text_up_all, text_down_all
        )
        text_up_grad = text_up_grad + up_grad
        text_down_grad = text_down_grad + down_grad
        up_list[0] = up_list[0] + bias_up
        grad_hidden1 = gather_back(grad_before, term)
        grad_before, grad_full, grad_gain, grad_shift, grad_bias = unsettle(
            grad_hidden1, before0, norm_gains[0], offsets[5]
        )
        gain_list[0] = gain_list[0] + grad_gain
        offset_list[5] = offset_list[5] + grad_shift
        offset_list[0] = offset_list[0] + grad_bias
        term, joined_grad, out_grad, bias_query, bias_value = self_backward(
            kept0, hidden0, mixed0, grad_full, text_joined, text_out_all, text_valid, scale
        )
        text_joined_grad = text_joined_grad + joined_grad
        text_out_grad = text_out_grad + out_grad
        head_list[0] = head_list[0] + bias_query
        head_list[1] = head_list[1] + bias_value
        grad_hidden0 = gather_back(grad_before, term)
        text_list.append(jnp.swapaxes(grad_hidden0.reshape(share_tokens, pairs, width), 0, 1))
    head_full = lax.dynamic_update_slice_in_dim(
        jnp.zeros((6, width), jnp.float32), jnp.stack(head_list), model_index * local, 1
    )
    up_full = lax.dynamic_update_slice_in_dim(
        jnp.zeros((2, hidden_local * model_parts), jnp.float32),
        jnp.stack(up_list),
        model_index * hidden_local,
        1,
    )
    gains_sum, offsets_sum, heads_sum, ups_sum = lax.psum(
        (jnp.stack(gain_list), jnp.stack(offset_list), head_full, up_full), ("dp", "mp")
    )
    head_out = lax.dynamic_slice_in_dim(heads_sum, model_index * local, local, 1)
    up_out = lax.dynamic_slice_in_dim(ups_sum, model_index * hidden_local, hidden_local, 1)
    text_qkv_grad = joined_split(text_joined_grad, 3)
    projections_grad = jnp.stack([text_proj_total, image_proj_total])
    merging_qkv_grad = jnp.concatenate(
        [
            joined_split(self_joined_grad, 3),
            cross_query_grad[None],
            joined_split(cross_joined_grad, 2),
        ],
        0,
    )
    merging_out_grad = jnp.stack([self_out_grad, cross_out_grad])
    (
        text_qkv_done,
        text_out_done,
        text_up_done,
        text_down_done,
        projections_done,
        merge_qkv_done,
        merge_out_done,
        merge_up_done,
        merge_down_done,
    ) = (
        lax.psum_scatter(text_qkv_grad, "dp", scatter_dimension=1, tiled=True),
        lax.psum_scatter(text_out_grad, "dp", scatter_dimension=1, tiled=True),
        lax.psum_scatter(text_up_grad, "dp", scatter_dimension=0, tiled=True),
        lax.psum_scatter(text_down_grad, "dp", scatter_dimension=1, tiled=True),
        lax.psum_scatter(projections_grad, "dp", scatter_dimension=1, tiled=True),
        lax.psum_scatter(merging_qkv_grad, "dp", scatter_dimension=1, tiled=True),
        lax.psum_scatter(merging_out_grad, "dp", scatter_dimension=2, tiled=True),
        lax.psum_scatter(merge_up_grad, "dp", scatter_dimension=0, tiled=True),
        lax.psum_scatter(merge_down_grad, "dp", scatter_dimension=1, tiled=True),
    )
    return (
        jnp.stack(merged_list),
        jnp.stack(loss_list),
        jnp.stack(text_list),
        jnp.stack(image_list),
        text_qkv_done,
        text_out_done,
        text_up_done,
        text_down_done,
        merge_qkv_done,
        merge_out_done,
        merge_up_done,
        merge_down_done,
        projections_done,
        gains_sum,
        offsets_sum,
        head_out,
        up_out,
    )


MESH = pl.DeviceIdType.MESH
BF = jnp.bfloat16
F32 = jnp.float32
T_ATT, T_UP, T_DOWN, M_SELF, M_CROSS, M_UP, M_DOWN = range(7)
BLOCKS = 7
BACK_ORDER = (M_DOWN, M_UP, M_CROSS, M_SELF, T_DOWN, T_UP, T_ATT)
SLOTS = 5
IMAGE_PAD = 16
NORMS = 5


def mm(left, right):
    return lax.dot_general(left, right, (((1,), (0,)), ((), ())), preferred_element_type=F32)


def mm_nt(left, right):
    return lax.dot_general(left, right, (((1,), (1,)), ((), ())), preferred_element_type=F32)


def mm_tn(left, right):
    return lax.dot_general(left, right, (((0,), (0,)), ((), ())), preferred_element_type=F32)


def mm_exact(left, right, dims):
    return lax.dot_general(
        left, right, (dims, ((), ())), precision=EXACT_DOT_MODE, preferred_element_type=F32
    )


NN, NT, TN = ((1,), (0,)), ((1,), (1,)), ((0,), (0,))


def remote(src, dst, send, recv, where):
    return pltpu.make_async_remote_copy(
        src_ref=src, dst_ref=dst, send_sem=send, recv_sem=recv, device_id=where, device_id_type=MESH
    )


def gelu_parts(pre):
    cdf = 0.5 * (1.0 + lax.erf(pre * (1.0 / math.sqrt(2.0))))
    return cdf


def layers(
    lengths, *arrays
):
    sources, arrays = arrays[:LOADS], arrays[LOADS:]
    outputs, arrays = arrays[:7], arrays[7:]
    targets, rest = arrays[:LOADS], arrays[LOADS:]
    layers_body(lengths, sources, targets, *targets, *outputs, *rest)


LOADS = 18


def layers_body(
    lengths, sources, targets,
    text_qkv, text_out, text_up, head_bias, up_bias, text_in, text_down, image_mask, image_in,
    merge_qkv, merge_out, merge_up, merge_down, gains, offs, image_ids, projections, cot,
    wout, mout, tgout, imout, pjout, lossout, vout,
    G, PJ, H, XH, RSD, SQ, SK, SV, CQ, CK, CV, OA, PS, PC, PRE, ACT, XS, XR, ACC, DZ, DPRE, DQKV, DKV,
    RC, R2, R1, RZ, BG, CT, MS, TG, IMO, IMS, IMR, IML, tmask, cmask, CG, CLS, DU, DUW, DPJ, TXS, TXR, PXF, PXS, PXR, LSR, MSB, MRX, V, VR, LS,
    img,
    load_s,
    z_s, z_r, s1_s, s1_r, s2_s, s2_r, sc_s, sc_r,
    b2_s, b2_r, b1_s, b1_r, bc_s, bc_r, bz_s, bz_r,
    x_s, x_r, m_s, m_r, cg_s, cg_r, v_s, v_r,
):
    loads = [
        pltpu.make_async_copy(source, target, load_s.at[i])
        for i, (source, target) in enumerate(zip(sources, targets))
        if i != 8
    ]
    micro, pairs, tokens, width = text_in.shape
    half_micro = micro // 2
    count = half_micro * pairs
    rows = count * tokens
    share = tokens // 4
    images = image_mask.shape[2]
    image_rows = img.shape[0] // half_micro
    local = width // 4
    heads = local // HEAD_DIM
    quarter = rows // 4
    scale = 1.0 / math.sqrt(HEAD_DIM)
    dp = lax.axis_index("dp")
    z = lax.axis_index("mp")
    y = lax.div(dp, 4)
    x = lax.rem(lax.div(dp, 2), 2)
    c = lax.rem(dp, 2)
    group = lax.div(z, 2)
    rank = lax.rem(z, 2)
    z1 = z + 1 - 2 * rank
    z2 = z + 2 - 4 * group
    z3 = z1 + 2 - 4 * group
    to_x = (dp + 2 - 4 * x, z)
    to_y = (dp + 4 - 8 * y, z)
    to_c = (dp + 1 - 2 * c, z)
    to_z1, to_z2, to_z3 = (dp, z1), (dp, z2), (dp, z3)

    mine, theirs = half_micro * group, half_micro * (1 - group)
    part = sources[8].at[pl.ds(mine, half_micro)]
    loads.insert(8, pltpu.make_async_copy(part, image_in, load_s.at[8]))
    barrier = pltpu.get_barrier_semaphore()
    others = [(lax.rem(dp + step, 8), z) for step in range(1, 8)]
    for where in others + [to_z1, to_z2, to_z3]:
        pl.semaphore_signal(barrier, inc=1, device_id=where, device_id_type=MESH)
    for load in loads:
        load.start()
    def attention_block(qkv, out, first):
        turned = turn(out)
        return jnp.concatenate([qkv[first], qkv[first + 1], qkv[first + 2], turned], 1)

    def turn(matrix):
        size = matrix.shape[1]
        unit = jnp.where(
            lax.broadcasted_iota(jnp.int32, (size, size), 0)
            == lax.broadcasted_iota(jnp.int32, (size, size), 1),
            1.0,
            0.0,
        ).astype(BF)
        return mm_nt(unit, matrix).astype(BF)

    def pack(k):
        if k == T_ATT:
            block = attention_block(text_qkv, text_out[...], 0)
        elif k == T_UP:
            block = text_up[...]
        elif k == T_DOWN:
            block = text_down[...]
        elif k == M_SELF:
            block = attention_block(merge_qkv, merge_out[0], 0)
        elif k == M_CROSS:
            block = attention_block(merge_qkv, merge_out[1], 3)
        elif k == M_UP:
            block = merge_up[...]
        else:
            block = merge_down[...]
        G[k, 0, y, x, c] = block

    loads[0].wait()
    loads[1].wait()
    pack(T_ATT)
    pl.semaphore_wait(barrier, 10)

    def x_first(k, q):
        return (k + q) % 2 == 0

    def hop_z(k):
        return remote(
            G.at[k, 0, y, x, c], G.at[k, 1, y, x, c], z_s.at[k], z_r.at[k], to_z2
        )

    def hop_1(k, q):
        part = G.at[k, q, y, x, c]
        return remote(
            part, part, s1_s.at[k, q, 0], s1_r.at[k, q, 0], to_x if x_first(k, q) else to_y
        )

    def hop_2(k, q):
        part = G.at[k, q, y, :, c] if x_first(k, q) else G.at[k, q, :, x, c]
        return remote(
            part, part, s2_s.at[k, q, 0], s2_r.at[k, q, 0], to_y if x_first(k, q) else to_x
        )

    def hop_c(k, q):
        part = G.at[k, q, :, :, c]
        return remote(part, part, sc_s.at[k, q], sc_r.at[k, q], to_c)

    cuts = [pl.ds(0, width // 16), pl.ds(width // 16, width // 16)]

    own_proj = PJ.at[y, x, c]
    p_1 = remote(own_proj, own_proj, s1_s.at[BLOCKS, 0, 0], s1_r.at[BLOCKS, 0, 0], to_x)
    p_2 = remote(PJ.at[y, :, c], PJ.at[y, :, c], s2_s.at[BLOCKS, 0, 0], s2_r.at[BLOCKS, 0, 0], to_y)
    p_c = remote(PJ.at[:, :, c], PJ.at[:, :, c], sc_s.at[BLOCKS, 0], sc_r.at[BLOCKS, 0], to_c)

    def tick(j):
        k = j
        if k < BLOCKS:
            if k > 0:
                pack(k)
            hop_z(k).start()
            hop_1(k, 0).start()
        k = j - 1
        if 0 <= k < BLOCKS:
            hop_z(k).wait_recv()
            hop_1(k, 1).start()
        k = j - 2
        if 0 <= k < BLOCKS:
            for q in range(2):
                hop_1(k, q).wait_recv()
                hop_2(k, q).start()
        k = j - 3
        if 0 <= k < BLOCKS:
            for q in range(2):
                hop_2(k, q).wait_recv()
                hop_c(k, q).start()
        k = j - 4
        if 0 <= k < BLOCKS:
            for q in range(2):
                hop_c(k, q).wait_recv()

    def sent_all():
        for k in range(BLOCKS):
            hop_z(k).wait_send()
            for q in range(2):
                hop_1(k, q).wait_send()
                hop_2(k, q).wait_send()
                hop_c(k, q).wait_send()

    def swap(e):
        return remote(XS.at[e % 2], XR.at[e], x_s.at[e % 2], x_r.at[e], to_z1)

    def swap_start(e):
        if e >= 2:
            swap(e - 2).wait_send()
        XS[e % 2] = ACC[...].astype(BF)
        swap(e).start()

    def swap_sum(e):
        swap(e).wait_recv()
        return XS[e % 2].astype(F32) + XR[e].astype(F32)

    for load in loads[2:5]:
        load.wait()
    BG[0, 0:6, 0:local] = head_bias[...]
    BG[0, 6:8, :] = up_bias[...]
    bias_copy = remote(BG.at[0], BG.at[1], m_s.at[0], m_r.at[0], to_z2)
    cot_copies = [
        remote(cot.at[pl.ds(mine, half_micro)], CT.at[z], m_s.at[1], m_r.at[1], to_z1),
        remote(cot.at[pl.ds(theirs, half_micro)], CT.at[z], m_s.at[2], m_r.at[2], to_z2),
        remote(cot.at[pl.ds(theirs, half_micro)], CT.at[z], m_s.at[3], m_r.at[3], to_z3),
    ]

    def pair_of(index):
        side = lax.rem(lax.div(index, share * pairs), half_micro)
        return side * pairs + lax.rem(index, pairs)

    def token_of(index):
        part = lax.div(index, share * count)
        return part * share + lax.div(lax.rem(index, share * pairs), pairs)

    def iota(shape, axis):
        return lax.broadcasted_iota(jnp.int32, shape, axis)

    def image_inputs():
        for n in range(half_micro):
            start, held = n * image_rows, images * pairs
            for low in range(0, image_rows, IMAGE_PAD):
                known = [
                    image_in[n, t]
                    for t in range(low // pairs, min((low + IMAGE_PAD) // pairs, images))
                ]
                missing = IMAGE_PAD - pairs * len(known)
                if missing:
                    known.append(jnp.zeros((missing, width), BF))
                block = jnp.concatenate([part.astype(F32) for part in known], 0)
                img[start + low : start + low + IMAGE_PAD, :] = block.astype(BF)

    def inputs():
        whole = [text_in[mine + n // pairs, n % pairs].astype(F32) for n in range(count)]
        whole = jnp.concatenate(whole, 0).astype(BF)
        to, place = iota((rows, rows), 0), iota((rows, rows), 1)
        order = jnp.where(place == pair_of(to) * tokens + token_of(to), 1.0, 0.0).astype(BF)
        H[0] = mm(order, whole).astype(BF)
        index = iota((1, rows), 1)
        limit = jnp.zeros((1, rows), jnp.int32)
        for n in range(count):
            limit = jnp.where(
                pair_of(index) == n, lengths[n % pairs, mine + n // pairs], limit
            )
        live = jnp.where(token_of(index) < limit, 1.0, 0.0)
        tmask[...] = jnp.where(pair_of(to) == pair_of(place), live, 0.0)
        live = []
        for n in range(half_micro):
            known = jnp.where(image_mask[mine + n] > 0, 1.0, 0.0)
            row = 0.0
            for p in range(pairs):
                size = (images, image_rows)
                to = iota(size, 1)
                fits = (lax.div(to, pairs) == iota(size, 0)) & (lax.rem(to, pairs) == p)
                part = jnp.broadcast_to(known[p : p + 1, :], (8, images)).astype(BF)
                row += mm(part, jnp.where(fits, 1.0, 0.0).astype(BF))
            live.append(row[0:1, :])
        live = jnp.concatenate(live, 1)
        size = (rows, half_micro * image_rows)
        to = iota(size, 1)
        of = lax.div(to, image_rows) * pairs + lax.rem(to, pairs)
        cmask[...] = jnp.where(pair_of(iota(size, 0)) == of, live, 0.0)

    tick(0)
    bias_copy.start()
    tick(1)
    for load in loads[5:]:
        load.wait()
    inputs()
    tick(2)
    image_inputs()
    PJ[y, x, c, :, 0 : PJ.shape[-1] // 2] = projections[0]
    PJ[y, x, c, :, PJ.shape[-1] // 2 :] = projections[1]
    tick(3)
    bias_copy.wait()
    for copy in cot_copies:
        copy.start()
    CT[z] = cot[pl.ds(mine, half_micro)]

    def weight(k, q, lo, hi):
        return G[k, q, :, :, :, :, lo:hi].reshape(width, hi - lo)

    def norm_forward(e, before):
        centre = before - jnp.mean(before, -1, keepdims=True)
        inverse = lax.rsqrt(jnp.mean(centre * centre, -1, keepdims=True) + EPS)
        xhat = centre * inverse
        XH[e] = xhat
        RSD[e] = inverse
        return xhat * gains[e : e + 1, :] + offs[NORMS + e : NORMS + e + 1, :]

    def settle_forward(e):
        before = H[e].astype(F32) + offs[e : e + 1, :] + swap_sum(e)
        out = norm_forward(e, before)
        if e + 1 < NORMS:
            H[e + 1] = out.astype(BF)
        return out

    def softmax(scores, mask):
        scores = jnp.where(mask > 0, scores * scale, NEGATIVE)
        raised = jnp.exp(scores - jnp.max(scores, -1, keepdims=True))
        return raised / jnp.sum(raised, -1, keepdims=True)

    def self_attention(k, e, layer):
        ACC[...] = jnp.zeros_like(ACC)

        def part(q, carry):
            made = mm(H[e], weight(k, q, 0, 3 * local))
            queries = (made[:, :local] + BG[q, 2 * layer : 2 * layer + 1, :local]).astype(BF)
            keys = made[:, local : 2 * local].astype(BF)
            values = (
                made[:, 2 * local :] + BG[q, 2 * layer + 1 : 2 * layer + 2, :local]
            ).astype(BF)
            SQ[layer, q], SK[layer, q], SV[layer, q] = queries, keys, values
            mixed = []
            for n in range(heads):
                cut = slice(n * HEAD_DIM, (n + 1) * HEAD_DIM)
                probs = softmax(mm_nt(queries[:, cut], keys[:, cut]), tmask[...]).astype(BF)
                PS[layer, q, n] = probs
                mixed.append(mm(probs, values[:, cut]).astype(BF))
            mixed = jnp.concatenate(mixed, 1)
            OA[layer, q] = mixed
            ACC[...] += mm_nt(mixed, weight(k, q, 3 * local, 4 * local))
            return carry

        lax.fori_loop(0, 2, part, 0)

    def image_keys():
        def part(q, carry):
            made = mm(img[...], weight(M_CROSS, q, local, 3 * local))
            CK[q] = made[:, :local].astype(BF)
            CV[q] = (made[:, local:] + BG[q, 5:6, :local]).astype(BF)
            return carry

        lax.fori_loop(0, 2, part, 0)

    def cross_attention():
        ACC[...] = jnp.zeros_like(ACC)

        def part(q, carry):
            queries = (mm(H[3], weight(M_CROSS, q, 0, local)) + BG[q, 4:5, :local]).astype(BF)
            CQ[q] = queries
            mixed = []
            for n in range(heads):
                cut = slice(n * HEAD_DIM, (n + 1) * HEAD_DIM)
                probs = softmax(mm_nt(queries[:, cut], CK[q, :, cut]), cmask[...]).astype(BF)
                PC[q, n] = probs
                mixed.append(mm(probs, CV[q, :, cut]).astype(BF))
            mixed = jnp.concatenate(mixed, 1)
            OA[2, q] = mixed
            ACC[...] += mm_nt(mixed, weight(M_CROSS, q, 3 * local, 4 * local))
            return carry

        lax.fori_loop(0, 2, part, 0)

    def feed_up(k, e, layer):
        def part(q, carry):
            pre = mm(H[e], weight(k, q, 0, width)) + BG[q, 6 + layer : 7 + layer, :]
            PRE[layer, q] = pre
            ACT[layer, q] = (pre * gelu_parts(pre)).astype(BF)
            return carry

        lax.fori_loop(0, 2, part, 0)

    def feed_down(k, layer):
        ACC[...] = jnp.zeros_like(ACC)

        def part(q, carry):
            ACC[...] += mm_nt(ACT[layer, q], weight(k, q, 0, width))
            return carry

        lax.fori_loop(0, 2, part, 0)

    tick(4)
    self_attention(T_ATT, 0, 0)
    swap_start(0)
    tick(5)
    settle_forward(0)
    feed_up(T_UP, 1, 0)
    tick(6)
    feed_down(T_DOWN, 0)
    swap_start(1)
    tick(7)
    settle_forward(1)

    def summary_rows():
        def pick(size, step):
            spot, place = iota((8, size), 0), iota((8, size), 1)
            fits = place == lax.div(spot, pairs) * step + lax.rem(spot, pairs)
            return jnp.where(fits & (spot < count), 1.0, 0.0).astype(BF)

        text_rows = mm(pick(rows, share * pairs), H[2])
        image_cls = mm(pick(img.shape[0], image_rows), img[...])
        CLS[...] = jnp.concatenate([text_rows, image_cls], 0).astype(BF)
        CG[dp] = CLS[...]

    summary_rows()
    summary = [
        remote(CLS, CG.at[dp], cg_s.at[i], cg_r.at[i], where) for i, where in enumerate(others)
    ]
    self_attention(M_SELF, 2, 1)
    swap_start(2)
    for copy in summary:
        copy.start()
    tick(8)
    image_keys()
    settle_forward(2)
    cross_attention()
    swap_start(3)
    tick(9)
    settle_forward(3)
    p_1.start()
    feed_up(M_UP, 4, 1)
    tick(10)
    feed_down(M_DOWN, 1)
    swap_start(4)
    p_1.wait()
    p_2.start()
    sent_all()
    V[...] = jnp.zeros_like(V)

    def slot(k):
        return BACK_ORDER.index(k) % SLOTS

    def back_c(k, q):
        return remote(
            G.at[k, q, :, :, 1 - c], RC.at[slot(k), q], bc_s.at[k, q], bc_r.at[k, q], to_c
        )

    def back_2(k, q):
        parts = [G.at[k, q, 1 - y, :, c, cuts[0]], G.at[k, q, :, 1 - x, c, cuts[1]]]
        return [
            remote(part, R2.at[k, q, h], b2_s.at[k, q, h], b2_r.at[k, q, h], (to_y, to_x)[h])
            for h, part in enumerate(parts)
        ]

    def back_1(k, q):
        parts = [G.at[k, q, y, 1 - x, c, cuts[0]], G.at[k, q, 1 - y, x, c, cuts[1]]]
        return [
            remote(part, R1.at[k, q, h], b1_s.at[k, q, h], b1_r.at[k, q, h], (to_x, to_y)[h])
            for h, part in enumerate(parts)
        ]

    def back_z(k):
        return remote(G.at[k, 1, y, x, c], RZ.at[k], bz_s.at[k], bz_r.at[k], to_z2)

    def both(a, b):
        return (a.astype(F32) + b.astype(F32)).astype(BF)

    def a_step(n, q):
        k = BACK_ORDER[n]
        back_c(k, q).wait()
        for a in range(2):
            for b in range(2):
                G[k, q, a, b, c] = both(G[k, q, a, b, c], RC[slot(k), q, a, b])
        for copy in back_2(k, q):
            copy.start()

    def b_step(n, q):
        k = BACK_ORDER[n]
        for copy in back_2(k, q):
            copy.wait()
        for a in range(2):
            G[k, q, y, a, c, cuts[0]] = both(G[k, q, y, a, c, cuts[0]], R2[k, q, 0, a])
            G[k, q, a, x, c, cuts[1]] = both(G[k, q, a, x, c, cuts[1]], R2[k, q, 1, a])
        for copy in back_1(k, q):
            copy.start()

    def d_step(n, q):
        k = BACK_ORDER[n]
        for copy in back_1(k, q):
            copy.wait()
        for h in range(2):
            if q == 1:
                G[k, q, y, x, c, cuts[h]] = both(G[k, q, y, x, c, cuts[h]], R1[k, q, h])
            else:
                wout[k, cuts[h]] = G[k, q, y, x, c, cuts[h]].astype(F32) + R1[k, q, h].astype(F32)
        if q == 1:
            back_z(k).start()

    def e_step(n):
        k = BACK_ORDER[n]
        back_z(k).wait()
        wout[k] = wout[k] + RZ[k].astype(F32)

    def norm_backward(e, grad):
        xhat = XH[e]
        V[0, e : e + 1, :] = jnp.sum(grad * xhat, 0, keepdims=True)
        V[0, 2 * NORMS + e : 2 * NORMS + e + 1, :] = jnp.sum(grad, 0, keepdims=True)
        scaled = grad * gains[e : e + 1, :]
        first = jnp.mean(scaled, -1, keepdims=True)
        second = jnp.mean(scaled * xhat, -1, keepdims=True)
        grad = RSD[e] * (scaled - first - xhat * second)
        DZ[...] = grad
        rounded = grad.astype(BF)
        V[0, NORMS + e : NORMS + e + 1, :] = jnp.sum(rounded.astype(F32), 0, keepdims=True)
        return rounded

    def keep_grad(k, q, lo, value):
        value = value.astype(BF)
        G[k, q, :, :, :, :, lo : lo + value.shape[1]] = value.reshape(
            2, 2, 2, width // 8, value.shape[1]
        )

    def feed_backward(up, down, e, layer, rounded):
        ACC[...] = jnp.zeros_like(ACC)
        turned = rounded.T

        def part(i, carry):
            q = 1 - i
            grad = mm(rounded, weight(down, q, 0, width))
            keep_grad(down, q, 0, mm(turned, ACT[layer, q]))
            back_c(down, q).start()
            pre = PRE[layer, q]
            slope = gelu_parts(pre) + pre * (
                jnp.exp(-0.5 * pre * pre) * (1.0 / math.sqrt(2.0 * math.pi))
            )
            grad = (grad * slope).astype(BF)
            DPRE[q] = grad
            V[1, pl.ds(2 * q + layer, 1), :] = jnp.sum(grad.astype(F32), 0, keepdims=True)
            ACC[...] += mm_nt(grad, weight(up, q, 0, width))
            return carry

        lax.fori_loop(0, 2, part, 0)

    def feed_up_grad(up, e):
        turned = H[e].T

        def part(i, carry):
            q = 1 - i
            keep_grad(up, q, 0, mm(turned, DPRE[q]))
            back_c(up, q).start()
            return carry

        lax.fori_loop(0, 2, part, 0)

    def head_backward(probs, queries, keys, values, grad):
        wide = probs.astype(F32)
        grad_values = mm_tn(probs, grad)
        grad_probs = mm_nt(grad, values)
        grad_scores = wide * (grad_probs - jnp.sum(grad_probs * wide, -1, keepdims=True))
        grad_scores = grad_scores.astype(BF)
        grad_queries = mm(grad_scores, keys) * scale
        grad_keys = mm_tn(grad_scores, queries) * scale
        return grad_queries.astype(BF), grad_keys.astype(BF), grad_values.astype(BF)

    def bias_sums(q, layer, grad_queries, grad_values):
        V[1, pl.ds(4 + 6 * q + 2 * layer, 1), 0:local] = jnp.sum(
            grad_queries.astype(F32), 0, keepdims=True
        )
        V[1, pl.ds(5 + 6 * q + 2 * layer, 1), 0:local] = jnp.sum(
            grad_values.astype(F32), 0, keepdims=True
        )

    def self_backward(k, layer, rounded):
        ACC[...] = jnp.zeros_like(ACC)

        def part(i, carry):
            q = 1 - i
            grad_mixed = mm(rounded, weight(k, q, 3 * local, 4 * local)).astype(BF)
            parts = []
            for n in range(heads):
                cut = slice(n * HEAD_DIM, (n + 1) * HEAD_DIM)
                parts.append(
                    head_backward(
                        PS[layer, q, n],
                        SQ[layer, q, :, cut],
                        SK[layer, q, :, cut],
                        SV[layer, q, :, cut],
                        grad_mixed[:, cut],
                    )
                )
            made = [jnp.concatenate([part[i] for part in parts], 1) for i in range(3)]
            bias_sums(q, layer, made[0], made[2])
            grads = jnp.concatenate(made, 1)
            DQKV[q] = grads
            ACC[...] += mm_nt(grads, weight(k, q, 0, 3 * local))
            return carry

        lax.fori_loop(0, 2, part, 0)

    def self_grad(k, e, layer, rounded):
        turned = H[e].T
        turned_out = rounded.T

        def part(i, carry):
            q = 1 - i
            keep_grad(
                k,
                q,
                0,
                jnp.concatenate(
                    [mm(turned, DQKV[q]), mm(turned_out, OA[layer, q])], 1
                ),
            )
            back_c(k, q).start()
            return carry

        lax.fori_loop(0, 2, part, 0)

    def cross_backward(rounded):
        ACC[...] = jnp.zeros_like(ACC)

        def part(i, carry):
            q = 1 - i
            grad_mixed = mm(rounded, weight(M_CROSS, q, 3 * local, 4 * local)).astype(BF)
            parts = []
            for n in range(heads):
                cut = slice(n * HEAD_DIM, (n + 1) * HEAD_DIM)
                parts.append(
                    head_backward(
                        PC[q, n],
                        CQ[q, :, cut],
                        CK[q, :, cut],
                        CV[q, :, cut],
                        grad_mixed[:, cut],
                    )
                )
            made = [jnp.concatenate([part[i] for part in parts], 1) for i in range(3)]
            bias_sums(q, 2, made[0], made[2])
            DQKV[q, :, 0:local] = made[0]
            DKV[q] = jnp.concatenate(made[1:], 1)
            ACC[...] += mm_nt(made[0], weight(M_CROSS, q, 0, local))
            return carry

        lax.fori_loop(0, 2, part, 0)

    def image_columns(first, second):
        def rows_of(q, place):
            part = G[M_CROSS, q, lax.div(place, 2), lax.rem(place, 2), :, :, local : 3 * local]
            return part.reshape(local, 2 * local)

        total = None
        for q in range(2):
            turned = jnp.concatenate([rows_of(q, first), rows_of(q, second)], 0)
            term = mm_nt(DKV[q], turned)
            total = term if total is None else total + term
        return total

    def cross_grad(rounded):
        turned = H[3].T
        turned_out = rounded.T
        turned_image = img[...].T

        def part(i, carry):
            q = 1 - i
            keep_grad(
                M_CROSS,
                q,
                0,
                jnp.concatenate(
                    [
                        mm(turned, DQKV[q, :, 0:local]),
                        mm(turned_image, DKV[q]),
                        mm(turned_out, OA[2, q]),
                    ],
                    1,
                ),
            )
            back_c(M_CROSS, q).start()
            return carry

        lax.fori_loop(0, 2, part, 0)

    def contrast():
        spots = CG.shape[0] * 8
        proj = PJ[...].reshape(width, PJ.shape[-1])
        half = proj.shape[1] // 2
        text_rows = CG[:, 0:8, :].reshape(spots, width)
        image_cls = CG[:, 8:16, :].reshape(spots, width)
        raw_t = mm(text_rows, proj[:, :half])
        raw_w = mm(image_cls, proj[:, half:])
        inv_t = lax.rsqrt(jnp.sum(raw_t * raw_t, -1, keepdims=True) + EPS)
        inv_w = lax.rsqrt(jnp.sum(raw_w * raw_w, -1, keepdims=True) + EPS)
        t, w = raw_t * inv_t, raw_w * inv_w
        known = image_ids.shape[1]

        def spread_of(shape, spot_axis, batch):
            spot = lax.broadcasted_iota(jnp.int32, shape, spot_axis)
            pair = lax.broadcasted_iota(jnp.int32, shape, 1 - spot_axis)
            fits = (lax.div(spot, 8) == lax.div(pair, pairs)) & (
                lax.rem(spot, 8) == batch * pairs + lax.rem(pair, pairs)
            )
            return jnp.where(fits, 1.0, 0.0)

        row_key, col_key = 0.0, 0.0
        for n in range(half_micro):
            drawn = image_ids[pl.ds(mine + n, 1), :].astype(F32)
            drawn = jnp.broadcast_to(drawn, (8, known))
            row_key += mm_exact(spread_of((spots, known), 0, n), drawn, NT)[:, 0:1]
            col_key += mm_exact(drawn, spread_of((known, spots), 1, n), NN)[0:1, :]

        def batch_of(axis):
            shape = (spots, 1) if axis == 0 else (1, spots)
            place = lax.rem(lax.broadcasted_iota(jnp.int32, shape, axis), 8)
            return jnp.where(place < count, lax.div(place, pairs), -1)

        row_batch, col_batch = batch_of(0), batch_of(1)
        live = row_batch == col_batch
        same = jnp.where(live & (row_key == col_key), 1.0, 0.0)
        target = same / jnp.sum(same, 1, keepdims=True)

        def log_rows(scores):
            scores = jnp.where(live, scores / SCORE_SCALE, NEGATIVE)
            shifted = scores - jnp.max(scores, -1, keepdims=True)
            return shifted - jnp.log(jnp.sum(jnp.exp(shifted), -1, keepdims=True))

        log_t = log_rows(mm_exact(t, w, NT))
        log_w = log_rows(mm_exact(w, t, NT))
        loss = -0.5 * (
            jnp.sum(target * jnp.where(live, log_t, 0.0), 1, keepdims=True)
            + jnp.sum(target * jnp.where(live, log_w, 0.0), 1, keepdims=True)
        )
        over_t = (0.5 / SCORE_SCALE) * (jnp.exp(log_t) - target)
        over_w = (0.5 / SCORE_SCALE) * (jnp.exp(log_w) - target)
        grad_t = mm_exact(over_t, w, NN) + mm_exact(over_w, w, TN)
        grad_w = mm_exact(over_t, t, TN) + mm_exact(over_w, t, NN)
        grad_t = (grad_t - t * jnp.sum(t * grad_t, -1, keepdims=True)) * inv_t
        grad_w = (grad_w - w * jnp.sum(w * grad_w, -1, keepdims=True)) * inv_w
        valid = jnp.where(row_batch >= 0, 1.0, 0.0)
        grad_t, grad_w = grad_t * valid, grad_w * valid
        DU[...] = grad_t.reshape(8, 8, half)
        DUW[...] = grad_w.reshape(8, 8, half)
        LS[...] = jnp.broadcast_to(loss, (spots, 128)).reshape(8, 8, 128)
        size = (8, width // 8, half)
        DPJ[...] = mm_exact(text_rows.astype(F32), grad_t, TN).reshape(size)
        PXF[:, 0:half] = DPJ[dp]
        DPJ[...] = mm_exact(image_cls.astype(F32), grad_w, TN).reshape(size)
        PXF[:, half:] = DPJ[dp]
        PXS[...] = PXF[...].astype(BF)

    pair_copy = remote(PXS, PXR, m_s.at[5], m_r.at[5], to_z2)
    loss_copy = remote(LS.at[dp], LSR, m_s.at[9], m_r.at[9], to_z2)

    def image_extra(place):
        part = PJ[lax.div(place, 2), lax.rem(place, 2), :, :, PJ.shape[-1] // 2 :]
        return mm_exact(DUW[dp], part.reshape(local, PJ.shape[-1] // 2).astype(F32), NT)

    image_copy = remote(IMS, IMR, m_s.at[6], m_r.at[6], to_z1)
    image_last = remote(IML, imout.at[group], m_s.at[7], m_r.at[7], to_z2)

    def image_finish():
        extra = jnp.concatenate([image_extra(z), image_extra(z2)], 1)
        spot = iota((8, 2 * local), 0)
        image_copy.wait()
        IMO[...] += IMR[...].astype(F32)
        for n in range(count):
            start = n // pairs * image_rows
            span = slice(start, start + 8)
            IMO[span, :] = IMO[span, :] + jnp.where(
                spot == n % pairs, extra[n : n + 1, :], 0.0
            )

        def side_by_side(low):
            parts = [
                IMO[n * image_rows : (n + 1) * image_rows, low : low + local]
                for n in range(half_micro)
            ]
            return jnp.concatenate(parts, 1).astype(BF)

        IML[...] = side_by_side(local)
        image_last.start()
        imout[group] = side_by_side(0)

    for copy in cot_copies:
        copy.wait()
    DZ[...] = jnp.concatenate(
        [
            CT[i, n, t].astype(F32)
            for i in range(4)
            for n in range(half_micro)
            for t in range(share)
        ],
        0,
    )
    merged = settle_forward(4)
    rounded = norm_backward(4, DZ[...])
    feed_backward(M_UP, M_DOWN, 4, 1, rounded)
    swap_start(5)
    p_2.wait()
    p_c.start()
    feed_up_grad(M_UP, 4)
    MS[...] = merged.reshape(4, quarter, width)
    mout[group] = MS[z]
    MSB[0] = MS[z2].astype(BF)
    merged_copy = remote(MSB.at[0], MRX.at[0], m_s.at[4], m_r.at[4], to_z2)
    text_copy = remote(MSB.at[1], MRX.at[1], m_s.at[8], m_r.at[8], to_z2)
    merged_copy.start()
    a_step(0, 1)
    a_step(1, 1)
    a_step(0, 0)
    p_c.wait()
    for copy in summary:
        copy.wait()
    contrast()
    pair_copy.start()
    loss_copy.start()
    b_step(0, 1)
    rounded = norm_backward(3, DZ[...] + swap_sum(5))
    cross_backward(rounded)
    swap_start(6)
    a_step(1, 0)
    b_step(1, 1)
    IMS[...] = image_columns(z1, z3).astype(BF)
    IMO[...] = image_columns(z, z2)
    d_step(0, 1)
    b_step(0, 0)
    cross_grad(rounded)
    a_step(2, 1)
    b_step(1, 0)
    d_step(1, 1)
    rounded = norm_backward(2, DZ[...] + swap_sum(6))
    self_backward(M_SELF, 1, rounded)
    swap_start(7)
    self_grad(M_SELF, 2, 1, rounded)
    b_step(2, 1)
    a_step(3, 1)
    image_copy.start()
    d_step(2, 1)

    proj_text = PJ[:, :, :, :, 0 : PJ.shape[-1] // 2].reshape(width, PJ.shape[-1] // 2)
    extra = mm_exact(DU[dp], proj_text.astype(F32), NT)
    place = lax.broadcasted_iota(jnp.int32, (rows, width), 0)
    grad = DZ[...] + swap_sum(7)
    for n in range(count):
        grad = grad + jnp.where(
            place == n // pairs * share * pairs + n % pairs, extra[n : n + 1, :], 0.0
        )
    rounded = norm_backward(1, grad)
    b_step(3, 1)
    feed_backward(T_UP, T_DOWN, 1, 0, rounded)
    swap_start(8)
    a_step(3, 0)
    a_step(4, 1)
    d_step(3, 1)
    feed_up_grad(T_UP, 1)
    a_step(4, 0)
    d_step(0, 0)
    image_finish()
    b_step(4, 1)
    e_step(0)
    b_step(4, 0)
    a_step(5, 1)
    d_step(1, 0)
    a_step(2, 0)
    d_step(4, 1)
    rounded = norm_backward(0, DZ[...] + swap_sum(8))
    self_backward(T_ATT, 0, rounded)

    MS[...] = ACC[...].reshape(4, quarter, width)
    TXS[0] = MS[z1].astype(BF)
    TXS[1] = MS[z3].astype(BF)
    text_swap = remote(TXS, TXR, x_s.at[2], x_r.at[9], to_z1)
    text_swap.start()
    TG[...] = (DZ[...] + ACC[...]).reshape(4, quarter, width)

    stat_from = (V.at[1 - c], V.at[c], V.at[c], V.at[c], V.at[c])
    stat_to = (to_c, to_x, to_y, to_z2, to_c)

    def stat_copy(i):
        return remote(stat_from[i], VR.at[i], v_s.at[i], v_r.at[i], stat_to[i])

    def stat_step(i):
        stat_copy(i).wait()
        known = VR[i]
        if i == 3:
            turned = jnp.concatenate(
                [known[2:4], known[0:2], known[10:16], known[4:10]], 0
            )
            known = jnp.where(c == 0, known, turned)
        if i < 4:
            V[c] = V[c] + known
            stat_copy(i + 1).start()
        else:
            vout[c] = V[c]
            vout[1 - c] = known

    stat_copy(0).start()
    d_step(4, 0)
    self_grad(T_ATT, 0, 0, rounded)
    b_step(5, 1)
    stat_step(0)
    e_step(1)
    a_step(6, 1)
    d_step(5, 1)
    stat_step(1)
    b_step(2, 0)
    e_step(4)
    b_step(6, 1)
    b_step(3, 0)
    a_step(5, 0)
    stat_step(2)
    a_step(6, 0)
    d_step(6, 1)
    text_swap.wait()
    tgout[group] = TG[z] + TXR[0].astype(F32)
    MSB[1] = (TG[z2] + TXR[1].astype(F32)).astype(BF)
    text_copy.start()
    d_step(2, 0)
    b_step(5, 0)
    b_step(6, 0)
    d_step(3, 0)
    e_step(3)
    e_step(2)
    stat_step(3)
    pair_copy.wait()
    loss_copy.wait()
    pjout[...] = PXF[...] + PXR[...].astype(F32)
    lossout[group] = LS[dp]
    lossout[1 - group] = LSR[...]
    merged_copy.wait()
    mout[1 - group] = MRX[0].astype(F32)
    image_last.wait()
    stat_step(4)
    d_step(6, 0)
    d_step(5, 0)
    e_step(5)
    e_step(6)
    text_copy.wait()
    tgout[1 - group] = MRX[1].astype(F32)
    swap(7).wait_send()
    swap(8).wait_send()


def unpack(
    wout, mout, tgout, imout, pjout, lossout, vout,
    merged, loss, text_grad, image_grad, text_qkv, text_out, text_up, text_down, merge_qkv,
    merge_out, merge_up, merge_down, projections, gains, offs, head_bias, up_bias,
):
    micro, share, pairs, width = merged.shape
    images = image_grad.shape[1]
    local = width // 4
    half_micro = micro // 2
    image_rows = imout.shape[1]

    for m in range(micro):
        side, start = m // half_micro, m % half_micro * share * pairs
        for t in range(share):
            span = slice(start + t * pairs, start + (t + 1) * pairs)
            merged[m, t] = mout[side, span, :]
            text_grad[m, t] = tgout[side, span, :]
        start = m % half_micro * local
        for low in range(0, images * pairs, IMAGE_PAD):
            block = imout[side, low : low + IMAGE_PAD, start : start + local].astype(F32)
            for t in range(low // pairs, min((low + IMAGE_PAD) // pairs, images)):
                image_grad[m, t] = block[t * pairs - low : (t + 1) * pairs - low]

    row = lax.broadcasted_iota(jnp.int32, (pairs, micro), 0)
    column = lax.broadcasted_iota(jnp.int32, (pairs, micro), 1)
    known = jnp.zeros((pairs, micro), F32)
    for m in range(micro):
        for p in range(pairs):
            n = m % half_micro * pairs + p
            known = jnp.where(
                (column == m) & (row == p), lossout[m // half_micro, n : n + 1, 0:1], known
            )
    loss[...] = known

    def block(k, place, out):
        out[...] = wout[k, :, place * local : (place + 1) * local]

    for i in range(3):
        block(T_ATT, i, text_qkv.at[i])
        block(M_SELF, i, merge_qkv.at[i])
        block(M_CROSS, i, merge_qkv.at[3 + i])
    text_out[...] = wout[T_ATT, :, 3 * local :].T
    merge_out[0] = wout[M_SELF, :, 3 * local :].T
    merge_out[1] = wout[M_CROSS, :, 3 * local :].T
    text_up[...] = wout[T_UP]
    merge_up[...] = wout[M_UP]
    text_down[...] = wout[T_DOWN]
    merge_down[...] = wout[M_DOWN]
    half = pjout.shape[1] // 2
    projections[0] = pjout[:, :half]
    projections[1] = pjout[:, half:]
    gains[...] = vout[0, 0:5, :]
    offs[...] = vout[0, 5:15, :]
    up_bias[...] = vout[1, 0:2, :]
    head_bias[...] = vout[1, 4:10, 0:local]


def fast_shards(
    text_embeds,
    text_lengths,
    image_embeds,
    image_mask,
    image_ids,
    out_cot,
    text_qkv,
    text_out,
    text_up,
    text_down,
    merge_qkv,
    merge_out,
    merge_up,
    merge_down,
    projections,
    norm_gains,
    offsets,
    head_biases,
    up_biases,
):
    micro, pairs, tokens, width = text_embeds.shape
    images = image_embeds.shape[2]
    data_parts = lax.axis_size("dp")
    model_parts = lax.axis_size("mp")
    local = width // model_parts
    shard = width // data_parts
    half_micro = micro // 2
    groups = 2
    count = half_micro * pairs
    share = tokens // model_parts
    rows = count * tokens
    quarter = rows // model_parts
    proj_width = 2 * projections.shape[2]
    image_rows = -(-images * pairs // IMAGE_PAD) * IMAGE_PAD
    vmem = pl.BlockSpec(memory_space=pltpu.VMEM)

    def sem(*shape):
        return pltpu.SemaphoreType.DMA(shape)

    def buf(*shape, dtype=BF):
        return pltpu.VMEM(shape, dtype)

    grid = (2, 2, 2, shard)
    inputs = (
        text_qkv, text_out, text_up, head_biases, up_biases, text_embeds, text_down.T, image_mask,
        image_embeds.transpose(0, 2, 1, 3), merge_qkv, merge_out, merge_up, merge_down.T,
        norm_gains, offsets, image_ids, projections, out_cot.transpose(0, 2, 1, 3),
    )
    held = [pltpu.VMEM(array.shape, array.dtype) for array in inputs]
    held[8] = pltpu.VMEM((half_micro, images, pairs, width), BF)
    scratch = [
        *held,
        buf(BLOCKS, 2, *grid, width),
        buf(*grid, proj_width),
        buf(NORMS, rows, width),
        buf(NORMS, rows, width, dtype=F32),
        buf(NORMS, rows, 1, dtype=F32),
        buf(2, 2, rows, local),
        buf(2, 2, rows, local),
        buf(2, 2, rows, local),
        buf(2, rows, local),
        buf(2, half_micro * image_rows, local),
        buf(2, half_micro * image_rows, local),
        buf(3, 2, rows, local),
        buf(2, 2, local // HEAD_DIM, rows, rows),
        buf(2, local // HEAD_DIM, rows, half_micro * image_rows),
        buf(2, 2, rows, width, dtype=F32),
        buf(2, 2, rows, width),
        buf(2, rows, width),
        buf(2 * NORMS, rows, width),
        buf(rows, width, dtype=F32),
        buf(rows, width, dtype=F32),
        buf(2, rows, width),
        buf(2, rows, 3 * local),
        buf(2, half_micro * image_rows, 2 * local),
        buf(SLOTS, 2, 2, 2, shard, width),
        buf(BLOCKS, 2, 2, 2, shard // 2, width),
        buf(BLOCKS, 2, 2, shard // 2, width),
        buf(BLOCKS, shard, width),
        buf(2, 8, width, dtype=F32),
        buf(model_parts, half_micro, share, pairs, width),
        buf(model_parts, quarter, width, dtype=F32),
        buf(model_parts, quarter, width, dtype=F32),
        buf(half_micro * image_rows, 2 * local, dtype=F32),
        buf(half_micro * image_rows, 2 * local),
        buf(half_micro * image_rows, 2 * local),
        buf(image_rows, half_micro * local),
        buf(rows, rows, dtype=F32),
        buf(rows, half_micro * image_rows, dtype=F32),
        buf(data_parts, 16, width),
        buf(16, width),
        buf(data_parts, 8, proj_width // 2, dtype=F32),
        buf(data_parts, 8, proj_width // 2, dtype=F32),
        buf(data_parts, shard, proj_width // 2, dtype=F32),
        buf(2, quarter, width),
        buf(2, quarter, width),
        buf(shard, proj_width, dtype=F32),
        buf(shard, proj_width),
        buf(shard, proj_width),
        buf(8, 128, dtype=F32),
        buf(2, quarter, width),
        buf(2, quarter, width),
        buf(2, 16, width, dtype=F32),
        buf(5, 16, width, dtype=F32),
        buf(data_parts, 8, 128, dtype=F32),
        buf(half_micro * image_rows, width),
        sem(LOADS),
        sem(BLOCKS),
        sem(BLOCKS),
        *[sem(BLOCKS + 1, 2, 2) for _ in range(4)],
        *[sem(BLOCKS + 1, 2) for _ in range(2)],
        *[sem(BLOCKS, 2, 2) for _ in range(4)],
        *[sem(BLOCKS, 2) for _ in range(2)],
        *[sem(BLOCKS) for _ in range(2)],
        sem(3),
        sem(2 * NORMS),
        sem(10),
        sem(10),
        sem(data_parts - 1),
        sem(data_parts - 1),
        sem(5),
        sem(5),
    ]
    packed = pl.pallas_call(
        layers,
        out_shape=(
            jax.ShapeDtypeStruct((BLOCKS, shard, width), F32),
            jax.ShapeDtypeStruct((groups, quarter, width), F32),
            jax.ShapeDtypeStruct((groups, quarter, width), F32),
            jax.ShapeDtypeStruct((groups, image_rows, half_micro * local), BF),
            jax.ShapeDtypeStruct((shard, proj_width), F32),
            jax.ShapeDtypeStruct((groups, 8, 128), F32),
            jax.ShapeDtypeStruct((2, 16, width), F32),
        ),
        in_specs=[pl.BlockSpec(memory_space=pltpu.SMEM)] + [pl.BlockSpec(memory_space=pl.ANY)] * LOADS,
        out_specs=(vmem,) * 7,
        scratch_shapes=scratch,
        compiler_params=pltpu.CompilerParams(
            collective_id=0, has_side_effects=True, vmem_limit_bytes=63 * 2**20
        ),
    )(text_lengths.T, *inputs)

    def out(*shape):
        return jax.ShapeDtypeStruct(shape, F32)

    done = pl.pallas_call(
        unpack,
        out_shape=(
            out(micro, share, pairs, width),
            out(pairs, micro),
            out(micro, share, pairs, width),
            out(micro, images, pairs, local),
            *[
                out(*array.shape)
                for array in (
                    text_qkv, text_out, text_up, text_down.T, merge_qkv, merge_out, merge_up,
                    merge_down.T, projections, norm_gains, offsets, head_biases, up_biases,
                )
            ],
        ),
        in_specs=[vmem] * 7,
        out_specs=(vmem,) * 17,
        compiler_params=pltpu.CompilerParams(vmem_limit_bytes=63 * 2**20),
    )(*packed)
    done = list(done)
    for i in (0, 2, 3):
        done[i] = done[i].transpose(0, 2, 1, 3)
    for i in (1, 7, 11):
        done[i] = done[i].T
    return tuple(done)


def solution(mesh):
    placed = (
        P(None, "dp", None, None),
        P(None, "dp"),
        P(None, "dp", None, None),
        P(None, "dp", None),
        P(),
        P(None, "dp", "mp", None),
        P(None, "dp", "mp"),
        P("mp", "dp"),
        P("dp", "mp"),
        P("mp", "dp"),
        P(None, "dp", "mp"),
        P(None, "mp", "dp"),
        P("dp", "mp"),
        P("mp", "dp"),
        P(None, "dp", None),
        P(),
        P(),
        P(None, "mp"),
        P(None, "mp"),
    )
    small = mesh.shape["dp"] == 8 and mesh.shape["mp"] == 4
    return jax.shard_map(
        fast_shards if small else shards,
        mesh=mesh,
        in_specs=placed,
        out_specs=(
            P(None, "dp", "mp", None),
            P(None, "dp"),
            P(None, "dp", "mp", None),
            P(None, "dp", None, "mp"),
            P(None, "dp", "mp"),
            P("mp", "dp"),
            P("dp", "mp"),
            P("mp", "dp"),
            P(None, "dp", "mp"),
            P(None, "mp", "dp"),
            P("dp", "mp"),
            P("mp", "dp"),
            P(None, "dp", None),
            P(),
            P(),
            P(None, "mp"),
            P(None, "mp"),
        ),
        check_vma=False,
    )
```
